32 devices in a mesh: dp: 8 (over z, x), rep: 4 (over y, core).
Axes of the slice: x: 2, y: 2, z: 4, core: 2. Of those that a mesh axis runs over, the one named last changes fastest.
Arguments:
- hidden_in: bfloat16 [64, 256, 1152], P(('dp', 'rep')), may hold values from -6 to 6
- condition: bfloat16 [64, 1152], P(('dp', 'rep')), may hold values from -6 to 6
- patch_mask: int32 [64, 256], P(('dp', 'rep')), may hold values from 0 to 1, as said below
- image_counts: int32 [32], P(('dp', 'rep')), may hold values from 1 to 2, as said below
- modulation_weight: bfloat16 [1152, 6912], P('dp'), may hold values from -0.1875 to 0.1875
- modulation_bias: bfloat16 [6912], P('dp'), may hold values from -3 to 3
- attend_weight: bfloat16 [1152, 3456], P('dp'), may hold values from -0.1875 to 0.1875
- attend_bias: bfloat16 [2, 1152], P(None, 'dp'), may hold values from -3 to 3
- output_weight: bfloat16 [1152, 1152], P('dp'), may hold values from -0.75 to 0.75
- output_bias: bfloat16 [1152], P('dp'), may hold values from -3 to 3
- expand_weight: bfloat16 [1152, 4608], P('dp'), may hold values from -0.1875 to 0.1875
- expand_bias: bfloat16 [4608], P('dp'), may hold values from -3 to 3
- shrink_weight: bfloat16 [4608, 1152], P('dp'), may hold values from -0.09375 to 0.09375
- shrink_bias: bfloat16 [1152], P('dp'), may hold values from -3 to 3
- cotangent: bfloat16 [64, 256, 1152], P(('dp', 'rep')), may hold values from -6 to 6
Outputs:
- layer_out: bfloat16 [64, 256, 1152], P(('dp', 'rep'))
- gradient_hidden: float32 [64, 256, 1152], P(('dp', 'rep'))
- gradient_condition: float32 [64, 1152], P(('dp', 'rep'))
- gradient_modulation_weight: float32 [1152, 6912], P('dp')
- gradient_modulation_bias: float32 [6912], P('dp')
- gradient_attend_weight: float32 [1152, 3456], P('dp')
- gradient_attend_bias: float32 [2, 1152], P(None, 'dp')
- gradient_output_weight: float32 [1152, 1152], P('dp')
- gradient_output_bias: float32 [1152], P('dp')
- gradient_expand_weight: float32 [1152, 4608], P('dp')
- gradient_expand_bias: float32 [4608], P('dp')
- gradient_shrink_weight: float32 [4608, 1152], P('dp')
- gradient_shrink_bias: float32 [1152], P('dp')
The draws below stay inside these ranges and needn't reach their ends.
Inputs may be any that keep to these rules, and one draw needn't show every extreme that they name: `patch_mask`: in each image the valid patches form a prefix of 128 patches or more; some image has exactly 128. `image_counts`: each device holds 1 to 2 images in its first slots; some device holds 2 and some device holds 1.
All inputs are finite; a program needn't handle non-finite values.
Results may differ from the reference program's by a relative error of at most 0.015.
The reference program's roundings to bfloat16 on the way count: a program that leaves them out, or rounds other values in their place, can miss the bound.
Values may be sent and summed in bfloat16 or wider, within the bound.
No kernel may reach another device: no remote copies, remote signals or barrier semaphores. Data moves between devices by JAX's collectives and lax.ppermute only.
A program may use at most 384 MiB of HBM per device.

```python
import math
import jax
import jax.numpy as jnp
from jax import lax

D = 1152
HEADS = 16
HEAD_DIM = 72
FF = 4608
PATCHES = 256
SLOTS = 2
RANKS = 32
IMAGES = 64


def draw_patch_mask(key, part):
    key = jax.random.fold_in(key, 11)
    length_key, pick_key = jax.random.split(key)
    lengths = jax.random.randint(length_key, (IMAGES,), PATCHES // 2, PATCHES + 1)
    chosen = jax.random.randint(pick_key, (), 0, IMAGES)
    lengths = lengths.at[chosen].set(PATCHES // 2)
    return (jnp.arange(PATCHES)[None, :] < lengths[:, None]).astype(jnp.int32)


def draw_image_counts(key, part):
    key = jax.random.fold_in(key, 23)
    count_key, full_key, single_key = jax.random.split(key, 3)
    counts = jax.random.randint(count_key, (RANKS,), 1, SLOTS + 1)
    full_rank = jax.random.randint(full_key, (), 0, RANKS)
    single_rank = (full_rank + 1 + jax.random.randint(single_key, (), 0, RANKS - 1)) % RANKS
    counts = counts.at[full_rank].set(SLOTS)
    counts = counts.at[single_rank].set(1)
    return counts.astype(jnp.int32)


def spiked(entries, stream_key, source, target, parts, factor):
    def block_of(dim):
        return (jnp.arange(entries.shape[dim]) // (entries.shape[dim] // parts)).reshape((-1,) + (1,) * (entries.ndim - 1 - dim))

    first = jax.random.permutation(stream_key, parts)[block_of(target)]
    far = (block_of(target) + parts // 2) % parts
    return jnp.where((block_of(source) == first) | (block_of(source) == far), factor * entries, entries)


def levels(key, dims, shards, least, top_value):
    def one(axis_at, blocks):
        draws = jax.random.uniform(jax.random.fold_in(jax.random.fold_in(key, 6), axis_at), (blocks,), jnp.float32, least / len(shards), top_value / len(shards))
        return jnp.repeat(jnp.exp(draws), dims[axis_at] // blocks).reshape((-1,) + (1,) * (len(dims) - axis_at - 1))

    gain = one(*shards[0])
    for cut in shards[1:]:
        gain = gain * one(*cut)
    return gain


def bell_draw(stream_key, extent, deviation, most, cuts=(), kind=jnp.bfloat16):
    entries = deviation * jax.random.normal(stream_key, extent, jnp.float32)
    if cuts:
        entries = entries * levels(stream_key, extent, cuts, -0.22, 0.18)
    return jnp.clip(entries, -most, most).astype(kind)


def gaussian_with(own_key, dims, width, reach, shards, heavy, kind=jnp.bfloat16):
    result = width * jax.random.normal(own_key, dims, jnp.float32)
    if shards:
        result = result * levels(own_key, dims, shards, -0.22, 0.18)
    return jnp.clip(spiked(result, jax.random.fold_in(own_key, 3), *heavy), -reach, reach).astype(kind)


def setup_inputs(seed: int = 0) -> dict:
    splits = jax.random.split(jax.random.key(seed), 16)
    return {
        "hidden_in": bell_draw(splits[0], (IMAGES, PATCHES, D), 1.0, 6.0, ((0, 32),)),
        "condition": bell_draw(splits[1], (IMAGES, D), 1.0, 6.0, ((0, 32),)),
        "patch_mask": draw_patch_mask(jax.random.fold_in(splits[15], 71), 0),
        "image_counts": draw_image_counts(jax.random.fold_in(splits[15], 71), 0),
        "modulation_weight": bell_draw(splits[4], (D, 6 * D), D ** -0.5, 0.1875, ((0, 8),)),
        "modulation_bias": bell_draw(splits[5], (6 * D,), 0.5, 3.0, ((0, 8),)),
        "attend_weight": bell_draw(splits[6], (D, 3 * D), D ** -0.5, 0.1875, ((0, 8),)),
        "attend_bias": bell_draw(splits[7], (2, D), 0.5, 3.0, ((1, 8),)),
        "output_weight": bell_draw(splits[8], (D, D), (D // 16) ** -0.5, 0.75, ((0, 8),)),
        "output_bias": bell_draw(splits[9], (D,), 0.5, 3.0, ((0, 8),)),
        "expand_weight": bell_draw(splits[10], (D, FF), D ** -0.5, 0.1875, ((0, 8),)),
        "expand_bias": bell_draw(splits[11], (FF,), 0.5, 3.0, ((0, 8),)),
        "shrink_weight": bell_draw(splits[12], (FF, D), FF ** -0.5, 0.09375, ((0, 8),)),
        "shrink_bias": bell_draw(splits[13], (D,), 0.5, 3.0, ((0, 8),)),
        "cotangent": gaussian_with(splits[14], (IMAGES, PATCHES, D), 1.0, 6.0, ((0, 32),), (0, 2, 32, 2.75)),
    }


highest = lax.Precision.HIGHEST
epsilon = 1e-06

@jax.custom_vjp
def low(v):
    return lax.optimization_barrier(v.astype(jnp.bfloat16)).astype(jnp.float32)

@jax.custom_vjp
def low_back(v):
    return v

def low_keep(v):
    return (low(v), None)

def low_pass(kept, grad):
    return (grad,)

def back_keep(v):
    return (v, None)

def back_low(kept, grad):
    return (low(grad),)
low.defvjp(low_keep, low_pass)
low_back.defvjp(back_keep, back_low)

def matmul(left_side, right_side):
    return jnp.dot(left_side, right_side, precision=highest, preferred_element_type=jnp.float32)

def layer_norm(values):
    centered = values - lax.optimization_barrier(jnp.mean(values, -1, keepdims=True))
    variance = lax.optimization_barrier(jnp.mean(centered * centered, -1, keepdims=True))
    return centered * lax.rsqrt(variance + epsilon)

def block_forward(params, hidden, condition_f, mask_block, live_block):
    mod_weight, mod_bias, att_weight, att_bias, out_weight, out_bias, exp_weight, exp_bias, shr_weight, shr_bias = params
    image_count = hidden.shape[0]
    cond_act = low(jax.nn.silu(condition_f))
    modulation = low_back(matmul(cond_act, mod_weight) + mod_bias).reshape(image_count, 6, 1, D)
    shift_one = modulation[:, 0]
    scale_one = modulation[:, 1]
    gate_one = modulation[:, 2]
    shift_two = modulation[:, 3]
    scale_two = modulation[:, 4]
    gate_two = modulation[:, 5]
    normed_one = low(layer_norm(hidden) * (1.0 + scale_one) + shift_one)
    bias_full = jnp.concatenate([att_bias[0], jnp.zeros((D,), jnp.float32), att_bias[1]])
    triple = low(low_back(matmul(normed_one.reshape(-1, D), att_weight) + bias_full))
    triple = triple.reshape(image_count, PATCHES, 3, HEADS, HEAD_DIM)
    queries = triple[:, :, 0]
    keys_all = triple[:, :, 1]
    values_all = triple[:, :, 2]
    scores = low_back(jnp.einsum('sqhd,skhd->shqk', queries, keys_all, precision=highest) * HEAD_DIM ** (-0.5))
    scores = jnp.where(mask_block[:, None, None, :] > 0, scores, -1e+30)
    shifted = scores - lax.optimization_barrier(jnp.max(scores, -1, keepdims=True))
    exponent = jnp.exp(shifted)
    probs = low(exponent / lax.optimization_barrier(jnp.sum(exponent, -1, keepdims=True)))
    attended = jnp.einsum('shqk,skhd->sqhd', probs, values_all, precision=highest)
    attended = low(low_back(attended)).reshape(-1, D)
    branch = low_back(matmul(attended, out_weight) + out_bias).reshape(image_count, PATCHES, D)
    middle = hidden + gate_one * branch
    normed_two = low(layer_norm(middle) * (1.0 + scale_two) + shift_two)
    inner = low_back(matmul(normed_two.reshape(-1, D), exp_weight) + exp_bias)
    active = low(jax.nn.gelu(inner, approximate=True))
    mlp_out = low_back(matmul(active, shr_weight) + shr_bias).reshape(image_count, PATCHES, D)
    return live_block[:, None, None] * (middle + gate_two * mlp_out)

def reference(hidden_in, condition, patch_mask, image_counts, modulation_weight, modulation_bias, attend_weight, attend_bias, output_weight, output_bias, expand_weight, expand_bias, shrink_weight, shrink_bias, cotangent):
    position = jnp.arange(IMAGES, dtype=jnp.int32)
    live_images = (position % SLOTS < image_counts[position // SLOTS]).astype(jnp.float32)
    weights = (modulation_weight.astype(jnp.float32), modulation_bias.astype(jnp.float32), attend_weight.astype(jnp.float32), attend_bias.astype(jnp.float32), output_weight.astype(jnp.float32), output_bias.astype(jnp.float32), expand_weight.astype(jnp.float32), expand_bias.astype(jnp.float32), shrink_weight.astype(jnp.float32), shrink_bias.astype(jnp.float32))
    group_size = math.gcd(IMAGES, max(1, 4096 // PATCHES))
    group_count = IMAGES // group_size
    mask_groups = patch_mask.reshape(group_count, group_size, PATCHES)
    live_groups = live_images.reshape(group_count, group_size)

    def forward(hidden, condition_f, params):

        def one_group(block_items):
            return jax.checkpoint(block_forward)(params, block_items[0], block_items[1], block_items[2], block_items[3])
        stacked = (hidden.reshape(group_count, group_size, PATCHES, D), condition_f.reshape(group_count, group_size, D), mask_groups, live_groups)
        return lax.map(one_group, stacked).reshape(IMAGES, PATCHES, D)
    layer_out, pullback = jax.vjp(forward, hidden_in.astype(jnp.float32), condition.astype(jnp.float32), weights)
    gradient_hidden, gradient_condition, weight_slopes = pullback(cotangent.astype(jnp.float32))
    slope_mod_weight, slope_mod_bias, slope_att_weight, slope_att_bias, slope_out_weight, slope_out_bias, slope_exp_weight, slope_exp_bias, slope_shr_weight, slope_shr_bias = weight_slopes
    return (layer_out.astype(jnp.bfloat16), gradient_hidden, gradient_condition, slope_mod_weight, slope_mod_bias, slope_att_weight, slope_att_bias, slope_out_weight, slope_out_bias, slope_exp_weight, slope_exp_bias, slope_shr_weight, slope_shr_bias)
```

```python
from functools import partial

import jax
import jax.numpy as jnp
from jax import lax
from jax.sharding import PartitionSpec as P

HEADS = 16


epsilon = 1e-06
masked_score = -1e30


def layer_norm(values):
    centered = values - jnp.mean(values, -1, keepdims=True)
    variance = jnp.mean(centered * centered, -1, keepdims=True)
    return centered * lax.rsqrt(variance + epsilon)


def modulate(values, shift_part, scale_part):
    return layer_norm(values) * (1.0 + scale_part) + shift_part


def inner_rows(left_side, right_side):
    return lax.dot_general(
        left_side, right_side, (((0,), (0,)), ((), ())), preferred_element_type=jnp.float32
    )


def times(left_side, right_side):
    return jnp.dot(left_side, right_side, preferred_element_type=jnp.float32)


def times_transposed(left_side, right_side):
    return lax.dot_general(
        left_side, right_side, (((1,), (1,)), ((), ())), preferred_element_type=jnp.float32
    )


class PermuteLinks:
    def __init__(self, dp):
        self.dp = dp
        self.depth = dp // 2
        here = lax.axis_index("dp")
        copy = lax.axis_index("rep")
        self.z = here // 2
        self.x = here % 2
        self.own = (copy % 2) * 2 + copy // 2
        self.order = [self.own ^ step for step in range(4)]

    def up(self, value):
        return lax.ppermute(value, "dp", [(i, (i + 2) % self.dp) for i in range(self.dp)])

    def swap_x(self, value):
        return lax.ppermute(value, "dp", [(i, i ^ 1) for i in range(self.dp)])

    def swap_y(self, value):
        return lax.ppermute(value, "rep", [(i, i ^ 2) for i in range(4)])

    def swap_core(self, value):
        return lax.ppermute(value, "rep", [(i, i ^ 1) for i in range(4)])

    def at_depth(self, step):
        return (self.z - step) % self.depth

    def pick(self, stacked, index):
        return lax.dynamic_index_in_dim(stacked, index, 0, keepdims=False)

    def collect(self, block):
        rows, columns = block.shape
        whole = jnp.zeros((self.dp, rows, columns), block.dtype)
        for step in range(self.depth):
            if step:
                block = self.up(block)
            place = 2 * self.at_depth(step)
            whole = lax.dynamic_update_slice(whole, block[None], (place + self.x, 0, 0))
            whole = lax.dynamic_update_slice(
                whole, self.swap_x(block)[None], (place + 1 - self.x, 0, 0)
            )
        return whole.reshape(self.dp * rows, columns)

    def gather(self, units, split_y):
        own = self.collect(self.pick(units, self.order[0]))
        if split_y:
            other = self.swap_y(own)
        else:
            other = self.collect(self.pick(units, self.order[1]))
        return [own, other, self.swap_core(own), self.swap_core(other)]

    def add(self, one, two):
        return (one.astype(jnp.float32) + two.astype(jnp.float32)).astype(jnp.bfloat16)

    def sum_shards(self, whole):
        rows = whole.shape[0] // self.dp
        cut = whole.reshape(self.depth, 2, rows, whole.shape[1])
        kept = lax.dynamic_index_in_dim(cut, self.x, 1, keepdims=False)
        sent = lax.dynamic_index_in_dim(cut, 1 - self.x, 1, keepdims=False)
        kept = self.add(kept, self.swap_x(sent))
        moving = self.pick(kept, self.at_depth(1))
        for step in range(2, self.depth + 1):
            moving = self.add(self.up(moving), self.pick(kept, self.at_depth(step)))
        return moving

    def reduce(self, wholes, split_y):
        own = self.add(wholes[0], self.swap_core(wholes[2]))
        other = self.add(wholes[1], self.swap_core(wholes[3]))
        if split_y:
            own = self.sum_shards(self.add(own, self.swap_y(other)))
            other = self.swap_y(own)
        else:
            own = self.sum_shards(own)
            other = self.sum_shards(other)
            own, other = self.add(own, self.swap_y(other)), self.add(other, self.swap_y(own))
        return [own, other, self.swap_core(own), self.swap_core(other)]


class PlainLinks:
    def __init__(self):
        self.order = [0, 1, 2, 3]

    def pick(self, stacked, index):
        return stacked[index]

    def gather(self, units, split_y):
        whole = lax.all_gather(units, "dp", axis=1, tiled=True)
        return [whole[0], whole[1], whole[2], whole[3]]

    def reduce(self, wholes, split_y):
        mine = lax.psum_scatter(jnp.stack(wholes), "dp", scatter_dimension=1, tiled=True)
        mine = lax.psum(mine, "rep")
        return [mine[0], mine[1], mine[2], mine[3]]


def in_order(links, units):
    whole = jnp.zeros((4,) + units[0].shape, units[0].dtype)
    for index, unit in zip(links.order, units):
        whole = lax.dynamic_update_slice(whole, unit[None], (index, 0, 0))
    return whole


def per_device(
    axis_sizes,
    hidden_in,
    condition,
    patch_mask,
    image_counts,
    modulation_weight,
    modulation_bias,
    attend_weight,
    attend_bias,
    output_weight,
    output_bias,
    expand_weight,
    expand_bias,
    shrink_weight,
    shrink_bias,
    cotangent,
):
    dp, rep = axis_sizes
    everyone = ("dp", "rep")
    here = lax.axis_index("dp")
    copy = lax.axis_index("rep")
    links = PermuteLinks(dp) if (dp == 8 and rep == 4) else PlainLinks()
    slot_count, patch_count, model_width = hidden_in.shape
    shard = modulation_weight.shape[0]
    inner_width = expand_weight.shape[1]
    head_count = HEADS
    head_dim = model_width // head_count
    row_count = slot_count * patch_count
    score_scale = head_dim ** (-0.5)
    key_valid = (patch_mask > 0)[:, None, None, :]
    live_images = (jnp.arange(slot_count) < image_counts[0]).astype(jnp.float32)

    attend_units = links.gather(
        jnp.concatenate(
            [attend_weight.reshape(shard, 3, model_width).transpose(1, 0, 2), output_weight[None]]
        ),
        False,
    )
    expand_units = links.gather(
        expand_weight.reshape(shard, dp, 4, shard).transpose(2, 0, 1, 3).reshape(4, shard, -1),
        True,
    )
    shrink_units = links.gather(
        shrink_weight.reshape(4, shard, model_width), True
    )
    query_full, key_full, value_full, output_full = in_order(links, attend_units)

    bias_sizes = (
        modulation_bias.shape[0],
        2 * shard,
        shard,
        expand_bias.shape[0],
        shard,
    )
    small = jnp.concatenate(
        [
            condition.reshape(-1),
            modulation_bias,
            attend_bias.reshape(-1),
            output_bias,
            expand_bias,
            shrink_bias,
        ]
    )
    small_all = lax.all_gather(small[None], everyone, axis=0, tiled=True).reshape(dp, rep, -1)
    cond_size = slot_count * model_width
    condition_all = small_all[:, :, :cond_size].reshape(dp, rep, slot_count, model_width)
    biases = small_all[:, 0, cond_size:].astype(jnp.float32)
    cuts = []
    start = 0
    for size in bias_sizes:
        cuts.append(biases[:, start : start + size])
        start += size
    modulation_bias_full = cuts[0].reshape(-1)
    attend_bias_full = cuts[1].reshape(dp, 2, shard).transpose(1, 0, 2).reshape(2, model_width)
    output_bias_full = cuts[2].reshape(-1)
    expand_bias_units = cuts[3].reshape(dp, 4, shard).transpose(1, 0, 2).reshape(4, -1)
    shrink_bias_full = cuts[4].reshape(-1)

    cond_rows = lax.dynamic_slice_in_dim(condition_all, here * shard, shard, 3)
    act_rows = jax.nn.silu(cond_rows.astype(jnp.float32)).astype(jnp.bfloat16)
    act_copy = lax.dynamic_index_in_dim(act_rows, copy, 1, keepdims=False)
    mod_terms = times(act_copy.reshape(dp * slot_count, shard), modulation_weight)
    modulation = (
        lax.psum_scatter(mod_terms, "dp", scatter_dimension=0, tiled=True) + modulation_bias_full
    )
    condition_f = condition.astype(jnp.float32)
    silu_back = jax.vjp(jax.nn.silu, condition_f)[1]

    hidden = hidden_in.astype(jnp.float32)
    pieces = modulation.reshape(slot_count, 6, 1, model_width)
    shift_one = pieces[:, 0]
    scale_one = pieces[:, 1]
    gate_one = pieces[:, 2]
    shift_two = pieces[:, 3]
    scale_two = pieces[:, 4]
    gate_two = pieces[:, 5]
    normed_value, back_one = jax.vjp(modulate, hidden, shift_one, scale_one)
    normed_one = normed_value.astype(jnp.bfloat16).reshape(row_count, model_width)

    def heads_of(flat):
        return flat.astype(jnp.bfloat16).reshape(slot_count, patch_count, head_count, head_dim)

    queries = heads_of(times(normed_one, query_full) + attend_bias_full[0])
    keys_all = heads_of(times(normed_one, key_full))
    values_all = heads_of(times(normed_one, value_full) + attend_bias_full[1])

    def attention_scores(query_low, key_low):
        raw = (
            jnp.einsum("sqhd,skhd->shqk", query_low, key_low, preferred_element_type=jnp.float32)
            * score_scale
        )
        return jnp.where(key_valid, raw, masked_score)

    scores = attention_scores(queries, keys_all)
    row_peak = jnp.max(scores, -1, keepdims=True)
    exponent = jnp.exp(scores - row_peak)
    row_total = jnp.sum(exponent, -1, keepdims=True)
    probs_low = (exponent / row_total).astype(jnp.bfloat16)
    log_total = row_peak + jnp.log(row_total)
    attended = jnp.einsum(
        "shqk,skhd->sqhd", probs_low, values_all, preferred_element_type=jnp.float32
    )
    attended_low = attended.reshape(row_count, model_width).astype(jnp.bfloat16)
    branch = times(attended_low, output_full) + output_bias_full
    branch = branch.reshape(slot_count, patch_count, model_width)
    middle = hidden + gate_one * branch
    normed_two_value, back_two = jax.vjp(modulate, middle, shift_two, scale_two)
    normed_two = normed_two_value.astype(jnp.bfloat16).reshape(row_count, model_width)

    slope = cotangent.astype(jnp.float32) * live_images[:, None, None]
    shrink_slope = (slope * gate_two).astype(jnp.bfloat16).reshape(row_count, model_width)
    mlp_out = shrink_bias_full
    normed_two_slope = 0.0
    expand_terms = []
    shrink_terms = []
    inner_sums = []
    for index, expand_unit, shrink_unit in zip(links.order, expand_units, shrink_units):
        inner = times(normed_two, expand_unit) + links.pick(expand_bias_units, index)
        active, gelu_back = jax.vjp(partial(jax.nn.gelu, approximate=True), inner)
        active_low = active.astype(jnp.bfloat16)
        mlp_out = mlp_out + times(active_low, shrink_unit)
        shrink_terms.append(inner_rows(active_low, shrink_slope).astype(jnp.bfloat16))
        active_slope = times_transposed(shrink_slope, shrink_unit)
        inner_low = gelu_back(active_slope)[0].astype(jnp.bfloat16)
        normed_two_slope = normed_two_slope + times_transposed(inner_low, expand_unit)
        expand_terms.append(inner_rows(normed_two, inner_low).astype(jnp.bfloat16))
        inner_sums.append(jnp.sum(inner_low, 0, dtype=jnp.float32))
    mlp_out = mlp_out.reshape(slot_count, patch_count, model_width)
    layer_out = (live_images[:, None, None] * (middle + gate_two * mlp_out)).astype(jnp.bfloat16)
    gate_two_slope = jnp.sum(slope * mlp_out, axis=1)
    shrink_sums = links.reduce(shrink_terms, True)
    expand_sums = links.reduce(expand_terms, False)
    normed_two_slope = normed_two_slope.reshape(slot_count, patch_count, model_width)
    middle_extra, shift_two_slope, scale_two_slope = back_two(normed_two_slope)
    middle_slope = slope + middle_extra
    gate_one_slope = jnp.sum(middle_slope * branch, axis=1)
    branch_low = (middle_slope * gate_one).astype(jnp.bfloat16).reshape(row_count, model_width)
    attended_slope = heads_of(times_transposed(branch_low, output_full))
    probs_again = jnp.exp(attention_scores(queries, keys_all) - log_total)
    again_low = probs_again.astype(jnp.bfloat16)
    prob_slope = jnp.einsum(
        "sqhd,skhd->shqk", attended_slope, values_all, preferred_element_type=jnp.float32
    )
    value_slope = jnp.einsum(
        "shqk,sqhd->skhd", again_low, attended_slope, preferred_element_type=jnp.float32
    )
    score_slope = (
        probs_again * (prob_slope - jnp.sum(probs_again * prob_slope, -1, keepdims=True))
    ).astype(jnp.bfloat16)
    query_slope = (
        jnp.einsum("shqk,skhd->sqhd", score_slope, keys_all, preferred_element_type=jnp.float32)
        * score_scale
    )
    key_slope = (
        jnp.einsum("shqk,sqhd->skhd", score_slope, queries, preferred_element_type=jnp.float32)
        * score_scale
    )

    def flat_of(by_head):
        return by_head.astype(jnp.bfloat16).reshape(row_count, model_width)

    query_low_slope = flat_of(query_slope)
    key_low_slope = flat_of(key_slope)
    value_low_slope = flat_of(value_slope)
    normed_one_slope = (
        times_transposed(query_low_slope, query_full)
        + times_transposed(key_low_slope, key_full)
        + times_transposed(value_low_slope, value_full)
    ).reshape(slot_count, patch_count, model_width)
    hidden_extra, shift_one_slope, scale_one_slope = back_one(normed_one_slope)
    gradient_hidden = middle_slope + hidden_extra

    rights = jnp.stack([query_low_slope, key_low_slope, value_low_slope, branch_low])
    lefts = jnp.stack([normed_one, normed_one, normed_one, attended_low])
    attend_terms = [
        inner_rows(links.pick(lefts, index), links.pick(rights, index)).astype(jnp.bfloat16)
        for index in links.order
    ]
    attend_sums = links.reduce(attend_terms, True)

    modulation_slope = (
        jnp.concatenate(
            [
                shift_one_slope,
                scale_one_slope,
                gate_one_slope[:, None],
                shift_two_slope,
                scale_two_slope,
                gate_two_slope[:, None],
            ],
            axis=1,
        )
        .reshape(slot_count, 6 * model_width)
        .astype(jnp.bfloat16)
    )
    mod_slope_all = lax.all_gather(modulation_slope, everyone, axis=0, tiled=True)
    slope_mod_weight = inner_rows(
        act_rows.reshape(dp * rep * slot_count, shard), mod_slope_all
    )
    mod_bias_size = modulation_bias.shape[0]
    slope_mod_bias = jnp.sum(
        lax.dynamic_slice_in_dim(mod_slope_all, here * mod_bias_size, mod_bias_size, 1),
        0,
        dtype=jnp.float32,
    )
    mod_slope_copy = lax.dynamic_index_in_dim(
        mod_slope_all.reshape(dp, rep, slot_count, -1), copy, 1, keepdims=False
    ).reshape(dp * slot_count, -1)
    cond_columns = times_transposed(mod_slope_copy, modulation_weight)
    cond_slope_all = lax.all_gather(cond_columns[None], "dp", axis=0, tiled=True)
    cond_slope = (
        lax.dynamic_slice_in_dim(cond_slope_all, here * slot_count, slot_count, 1)
        .transpose(1, 0, 2)
        .reshape(slot_count, model_width)
    )
    gradient_condition = silu_back(cond_slope)[0]

    sums = lax.psum(
        jnp.concatenate(
            [
                jnp.sum(query_low_slope, 0, dtype=jnp.float32),
                jnp.sum(value_low_slope, 0, dtype=jnp.float32),
                jnp.sum(branch_low, 0, dtype=jnp.float32),
                jnp.sum(shrink_slope, 0, dtype=jnp.float32),
                in_order(links, [part[None] for part in inner_sums])
                .reshape(4, dp, shard)
                .transpose(1, 0, 2)
                .reshape(-1),
            ]
        ),
        everyone,
    )
    rows = lax.dynamic_index_in_dim(
        sums[: 4 * model_width].reshape(4, dp, shard), here, 1, keepdims=False
    )
    slope_att_bias = rows[0:2]
    slope_out_bias = rows[2]
    slope_shr_bias = rows[3]
    slope_exp_bias = lax.dynamic_slice_in_dim(
        sums[4 * model_width :], here * expand_bias.shape[0], expand_bias.shape[0], 0
    )

    attend_all = in_order(links, attend_sums).astype(jnp.float32)
    slope_att_weight = attend_all[:3].transpose(1, 0, 2).reshape(shard, 3 * model_width)
    slope_out_weight = attend_all[3]
    slope_exp_weight = (
        in_order(links, expand_sums)
        .reshape(4, shard, dp, shard)
        .transpose(1, 2, 0, 3)
        .reshape(shard, inner_width)
        .astype(jnp.float32)
    )
    slope_shr_weight = (
        in_order(links, shrink_sums).reshape(4 * shard, model_width).astype(jnp.float32)
    )
    return (
        layer_out,
        gradient_hidden,
        gradient_condition,
        slope_mod_weight,
        slope_mod_bias,
        slope_att_weight,
        slope_att_bias,
        slope_out_weight,
        slope_out_bias,
        slope_exp_weight,
        slope_exp_bias,
        slope_shr_weight,
        slope_shr_bias,
    )


def solution(mesh):
    return jax.shard_map(
        partial(per_device, (mesh.shape["dp"], mesh.shape["rep"])),
        mesh=mesh,
        in_specs=(
            P(("dp", "rep"), None, None),
            P(("dp", "rep"), None),
            P(("dp", "rep"), None),
            P(("dp", "rep")),
            P("dp", None),
            P("dp"),
            P("dp", None),
            P(None, "dp"),
            P("dp", None),
            P("dp"),
            P("dp", None),
            P("dp"),
            P("dp", None),
            P("dp"),
            P(("dp", "rep"), None, None),
        ),
        out_specs=(
            P(("dp", "rep"), None, None),
            P(("dp", "rep"), None, None),
            P(("dp", "rep"), None),
            P("dp", None),
            P("dp"),
            P("dp", None),
            P(None, "dp"),
            P("dp", None),
            P("dp"),
            P("dp", None),
            P("dp"),
            P("dp", None),
            P("dp"),
        ),
        check_vma=False,
    )
```

```python
import math
from functools import partial

import jax
import jax.numpy as jnp
from jax import lax
from jax.experimental import pallas as pl
from jax.experimental.pallas import tpu as pltpu
from jax.sharding import PartitionSpec as P

HEADS = 16


epsilon = 1e-06
masked_score = -1e30


def layer_norm(values):
    centered = values - jnp.mean(values, -1, keepdims=True)
    variance = jnp.mean(centered * centered, -1, keepdims=True)
    return centered * lax.rsqrt(variance + epsilon)


def modulate(values, shift_part, scale_part):
    return layer_norm(values) * (1.0 + scale_part) + shift_part


def gelu(values):
    return jax.nn.gelu(values, approximate=True)


def low(values):
    return values.astype(jnp.bfloat16)


def inner_rows(left_side, right_side):
    return lax.dot_general(
        left_side, right_side, (((0,), (0,)), ((), ())), preferred_element_type=jnp.float32
    )


def times(left_side, right_side):
    return jnp.dot(left_side, right_side, preferred_element_type=jnp.float32)


def times_transposed(left_side, right_side):
    return lax.dot_general(
        left_side, right_side, (((1,), (1,)), ((), ())), preferred_element_type=jnp.float32
    )


def column_sums(values):
    return jnp.sum(values, 0, dtype=jnp.float32)


def head_window(head, head_dim, model_width):
    first = head * head_dim
    last = first + head_dim
    start = first // 128 * 128
    stop = min(-(-last // 128) * 128, model_width)
    lane = lax.broadcasted_iota(jnp.int32, (1, stop - start), 1) + start
    return slice(start, stop), (lane >= first) & (lane < last)


def only(inside, values):
    return jnp.where(inside, values, jnp.zeros_like(values))


def head_order(heads):
    half = heads // 2
    return [head + shift for head in range(half) for shift in (0, half)]


def head_scores(query, key_window, valid, score_scale):
    scores = times_transposed(query, key_window) * score_scale
    return jnp.where(valid, scores, masked_score)


def attend_kernel(heads, query_ref, key_ref, value_ref, mask_ref, out_ref, log_ref, total_ref):
    patch_count, model_width = query_ref.shape
    head_dim = model_width // heads
    valid = mask_ref[0] > 0
    total_ref[...] = jnp.zeros_like(total_ref)
    for head in head_order(heads):
        cut, inside = head_window(head, head_dim, model_width)
        query = only(inside, query_ref[:, cut])
        scores = head_scores(query, key_ref[:, cut], valid, head_dim ** (-0.5))
        peak = jnp.max(scores, -1, keepdims=True)
        exponent = jnp.exp(scores - peak)
        row_total = jnp.sum(exponent, -1, keepdims=True)
        log_ref[:, head : head + 1] = peak + jnp.log(row_total)
        probs = low(exponent * (1.0 / row_total))
        total_ref[:, cut] += times(probs, only(inside, value_ref[:, cut]))
    out_ref[...] = low(total_ref[...])


def attend(queries, keys_all, values_all, patch_mask):
    slot_count, patch_count = patch_mask.shape
    model_width = queries.shape[1]
    block = pl.BlockSpec((patch_count, model_width), lambda slot: (slot, 0))
    return pl.pallas_call(
        partial(attend_kernel, HEADS),
        grid=(slot_count,),
        out_shape=[
            jax.ShapeDtypeStruct(queries.shape, jnp.bfloat16),
            jax.ShapeDtypeStruct((queries.shape[0], HEADS), jnp.float32),
        ],
        in_specs=[block] * 3 + [pl.BlockSpec((1, 1, patch_count), lambda slot: (slot, 0, 0))],
        out_specs=[block, pl.BlockSpec((patch_count, HEADS), lambda slot: (slot, 0))],
        scratch_shapes=[pltpu.VMEM((patch_count, model_width), jnp.float32)],
        compiler_params=pltpu.CompilerParams(vmem_limit_bytes=32 << 20),
    )(queries, keys_all, values_all, patch_mask[:, None, :])


def attend_back_kernel(
    heads,
    query_ref,
    key_ref,
    value_ref,
    slope_ref,
    mask_ref,
    log_ref,
    query_out,
    key_out,
    value_out,
    query_total,
    key_total,
    value_total,
):
    patch_count, model_width = query_ref.shape
    head_dim = model_width // heads
    score_scale = head_dim ** (-0.5)
    valid = mask_ref[0] > 0
    for total in (query_total, key_total, value_total):
        total[...] = jnp.zeros_like(total)
    for head in head_order(heads):
        cut, inside = head_window(head, head_dim, model_width)
        query = only(inside, query_ref[:, cut])
        key = only(inside, key_ref[:, cut])
        slope = only(inside, slope_ref[:, cut])
        probs = jnp.exp(head_scores(query, key, valid, score_scale) - log_ref[:, head : head + 1])
        prob_slope = times_transposed(slope, value_ref[:, cut])
        row = jnp.sum(probs * prob_slope, -1, keepdims=True)
        score_slope = low(probs * (prob_slope - row))
        query_total[:, cut] += times(score_slope, key)
        key_total[:, cut] += inner_rows(score_slope, query)
        value_total[:, cut] += inner_rows(low(probs), slope)
    query_out[...] = low(query_total[...] * score_scale)
    key_out[...] = low(key_total[...] * score_scale)
    value_out[...] = low(value_total[...])


def attend_back(queries, keys_all, values_all, slopes, patch_mask, logs):
    slot_count, patch_count = patch_mask.shape
    model_width = queries.shape[1]
    block = pl.BlockSpec((patch_count, model_width), lambda slot: (slot, 0))
    return pl.pallas_call(
        partial(attend_back_kernel, HEADS),
        grid=(slot_count,),
        out_shape=[jax.ShapeDtypeStruct(queries.shape, jnp.bfloat16)] * 3,
        in_specs=[block] * 4
        + [
            pl.BlockSpec((1, 1, patch_count), lambda slot: (slot, 0, 0)),
            pl.BlockSpec((patch_count, HEADS), lambda slot: (slot, 0)),
        ],
        out_specs=[block] * 3,
        scratch_shapes=[pltpu.VMEM((patch_count, model_width), jnp.float32)] * 3,
        compiler_params=pltpu.CompilerParams(vmem_limit_bytes=32 << 20),
    )(queries, keys_all, values_all, slopes, patch_mask[:, None, :], logs)


def norm_parts(values):
    centered = values - jnp.mean(values, -1, keepdims=True)
    inverse = lax.rsqrt(jnp.mean(centered * centered, -1, keepdims=True) + epsilon)
    return centered * inverse, inverse


def norm_back(normed, inverse, slope):
    mean = jnp.mean(slope, -1, keepdims=True)
    return (slope - mean - normed * jnp.mean(slope * normed, -1, keepdims=True)) * inverse


def patch_sums(values):
    return jnp.sum(values, 0, keepdims=True)


def middle_kernel(attended_ref, weight_ref, bias_ref, hidden_ref, mod_ref, branch_ref, middle_ref, normed_ref):
    gate_one, shift_two, scale_two = [mod_ref[0, i : i + 1] for i in (2, 3, 4)]
    branch = times(attended_ref[...], weight_ref[0]) + bias_ref[...]
    branch_ref[...] = branch
    middle = hidden_ref[...].astype(jnp.float32) + gate_one * branch
    middle_ref[...] = middle
    normed_ref[...] = low(norm_parts(middle)[0] * (1.0 + scale_two) + shift_two)


def finish_kernel(
    live_ref,
    middle_ref,
    branch_ref,
    out_ref,
    back_ref,
    cotangent_ref,
    bias_ref,
    mod_ref,
    layer_ref,
    middle_slope_ref,
    branch_low_ref,
    slopes_ref,
):
    gate_one, shift_two, scale_two, gate_two = [mod_ref[0, i : i + 1] for i in (2, 3, 4, 5)]
    live = live_ref[pl.program_id(0)]
    middle = middle_ref[...]
    mlp_out = out_ref[...] + bias_ref[...]
    layer_ref[...] = low(live * (middle + gate_two * mlp_out))
    slope = cotangent_ref[...].astype(jnp.float32) * live
    slopes_ref[0, 3:4] = patch_sums(slope * mlp_out)
    normed, inverse = norm_parts(middle)
    back = back_ref[...]
    slopes_ref[0, 1:2] = patch_sums(back)
    slopes_ref[0, 2:3] = patch_sums(back * normed)
    middle_slope = slope + norm_back(normed, inverse, back * (1.0 + scale_two))
    middle_slope_ref[...] = middle_slope
    slopes_ref[0, 0:1] = patch_sums(middle_slope * branch_ref[...])
    branch_low_ref[...] = low(middle_slope * gate_one)


def start_back_kernel(
    query_ref, key_ref, value_ref, weight_ref, middle_slope_ref, hidden_ref, mod_ref, out_ref, slopes_ref
):
    scale_one = mod_ref[0, 1:2]
    back = times_transposed(query_ref[...], weight_ref[0])
    back += times_transposed(key_ref[...], weight_ref[1])
    back += times_transposed(value_ref[...], weight_ref[2])
    normed, inverse = norm_parts(hidden_ref[...].astype(jnp.float32))
    slopes_ref[0, 0:1] = patch_sums(back)
    slopes_ref[0, 1:2] = patch_sums(back * normed)
    out_ref[...] = middle_slope_ref[...] + norm_back(normed, inverse, back * (1.0 + scale_one))


def assemble_kernel(place_ref, *refs):
    blocks, whole_ref = refs[:-1], refs[-1]
    for index, block in enumerate(blocks):
        whole_ref[place_ref[index]] = block[0]


def assemble(blocks, places, count):
    shape = (count,) + blocks[0][0].shape[1:]

    def row_spec(row):
        return pl.BlockSpec((1,) + shape[1:], lambda step: (row, 0, 0))

    return pl.pallas_call(
        assemble_kernel,
        grid=(1,),
        in_specs=[pl.BlockSpec(memory_space=pltpu.SMEM)] + [row_spec(row) for _, row in blocks],
        out_specs=pl.BlockSpec(shape, lambda step: (0, 0, 0)),
        out_shape=jax.ShapeDtypeStruct(shape, blocks[0][0].dtype),
        compiler_params=pltpu.CompilerParams(vmem_limit_bytes=32 << 20),
        cost_estimate=pl.CostEstimate(
            flops=0, bytes_accessed=4 * count * shape[1] * shape[2], transcendentals=0
        ),
    )(jnp.stack(places).astype(jnp.int32), *[array for array, _ in blocks])


def rows_of(parts):
    if len(parts) == 1:
        return parts[0]
    row = lax.broadcasted_iota(jnp.int32, (2, 1, 1), 0)
    return jnp.where(row == 0, parts[0], parts[1])


def take(places, wholes, parts=()):
    count = len(places)
    total = 0.0
    for whole in wholes:
        cut = [lax.dynamic_slice_in_dim(whole, place, 1, 0) for place in places]
        total = total + rows_of(cut).astype(jnp.float32)
    for part, row in parts:
        total = total + part[row : row + count].astype(jnp.float32)
    return low(total)


def pair_rows(one, one_row, two, two_row):
    return rows_of([one[one_row : one_row + 1], two[two_row : two_row + 1]])


def reorder_kernel(place_ref, *refs):
    units, whole_ref = refs[:-1], refs[-1]
    for index, unit in enumerate(units):
        whole_ref[place_ref[index]] = unit[...]


def reorder(units, order, parts):
    rows, width = units[0].shape
    block = rows // parts
    return pl.pallas_call(
        reorder_kernel,
        grid=(parts,),
        in_specs=[pl.BlockSpec(memory_space=pltpu.SMEM)]
        + [pl.BlockSpec((block, width), lambda step: (step, 0))] * 4,
        out_specs=pl.BlockSpec((4, block, width), lambda step: (0, step, 0)),
        out_shape=jax.ShapeDtypeStruct((4, rows, width), units[0].dtype),
        compiler_params=pltpu.CompilerParams(vmem_limit_bytes=32 << 20),
        cost_estimate=pl.CostEstimate(
            flops=0, bytes_accessed=16 * rows * width, transcendentals=0
        ),
    )(jnp.stack(order).astype(jnp.int32), *units)


def regroup_kernel(parts, in_ref, out_ref):
    width = in_ref.shape[1] // (4 * parts)
    for unit in range(4):
        out_ref[unit] = jnp.concatenate(
            [
                in_ref[:, (4 * part + unit) * width : (4 * part + unit + 1) * width]
                for part in range(parts)
            ],
            axis=1,
        )


def regroup(columns, parts):
    rows, width = columns.shape
    return pl.pallas_call(
        partial(regroup_kernel, parts),
        out_shape=jax.ShapeDtypeStruct((4, rows, width // 4), columns.dtype),
        compiler_params=pltpu.CompilerParams(vmem_limit_bytes=32 << 20),
    )(columns)


def spread_kernel(parts, order_ref, *refs):
    units, out_ref, held = refs[:4], refs[4], refs[5]
    for index in range(4):
        held[order_ref[index]] = units[index][...]
    width = units[0].shape[1] // parts
    out_ref[...] = jnp.concatenate(
        [
            held[unit, :, part * width : (part + 1) * width].astype(jnp.float32)
            for part in range(parts)
            for unit in range(4)
        ],
        axis=1,
    )


def spread(units, order, parts):
    rows, width = units[0].shape
    vmem = pl.BlockSpec(memory_space=pltpu.VMEM)
    return pl.pallas_call(
        partial(spread_kernel, parts),
        in_specs=[pl.BlockSpec(memory_space=pltpu.SMEM)] + [vmem] * 4,
        out_specs=vmem,
        out_shape=jax.ShapeDtypeStruct((rows, 4 * width), jnp.float32),
        scratch_shapes=[pltpu.VMEM((4, rows, width), units[0].dtype)],
        compiler_params=pltpu.CompilerParams(vmem_limit_bytes=32 << 20),
    )(jnp.stack(order).astype(jnp.int32), *units)


class Layer:
    def __init__(self, hidden_in, condition, patch_mask, image_counts, cotangent):
        self.slots, self.patches, self.width = hidden_in.shape
        self.rows = self.slots * self.patches
        self.patch_mask = patch_mask
        self.condition = condition
        self.live = (jnp.arange(self.slots) < image_counts[0]).astype(jnp.float32)
        self.hidden_in = hidden_in
        self.hidden = hidden_in.reshape(self.rows, self.width)
        self.cotangent = cotangent
        self.whole = (self.rows, self.width)

    def flat(self, values):
        return values.reshape(self.rows, self.width)

    def pieces(self, modulation):
        cut = modulation.reshape(self.slots, 6, 1, self.width)
        return [cut[:, i] for i in range(6)]

    def start(self, modulation):
        shift_one, scale_one = self.pieces(modulation)[:2]
        normed = modulate(self.hidden_in.astype(jnp.float32), shift_one, scale_one)
        return self.flat(low(normed))

    def shrink_slope(self, modulation):
        slope = self.cotangent.astype(jnp.float32) * self.live[:, None, None]
        return self.flat(low(slope * self.pieces(modulation)[5]))

    def attention(self, normed_one, weights, attend_bias):
        queries = low(times(normed_one, weights[0]) + attend_bias[0])
        keys_all = low(times(normed_one, weights[1]))
        values_all = low(times(normed_one, weights[2]) + attend_bias[1])
        attended, logs = attend(queries, keys_all, values_all, self.patch_mask)
        return queries, keys_all, values_all, attended, logs

    def per_image(self, kernel, outs, ins):
        rows = pl.BlockSpec((self.patches, self.width), lambda slot: (slot, 0))

        def spec(kind, shape):
            if kind == "rows":
                return rows
            if kind == "scalar":
                return pl.BlockSpec(memory_space=pltpu.SMEM)
            if kind == "all":
                return pl.BlockSpec(shape, lambda slot: (0,) * len(shape))
            if isinstance(kind, tuple):
                return pl.BlockSpec((kind[0],) + shape[1:], lambda slot: (kind[1], 0, 0))
            return pl.BlockSpec((1,) + shape[1:], lambda slot: (slot, 0, 0))

        shapes = [
            self.whole if kind == "rows" else (self.slots, kind, self.width) for kind, _ in outs
        ]
        return pl.pallas_call(
            kernel,
            grid=(self.slots,),
            in_specs=[spec(kind, array.shape) for kind, array in ins],
            out_specs=[spec(kind, shape) for (kind, _), shape in zip(outs, shapes)],
            out_shape=[jax.ShapeDtypeStruct(shape, kind[1]) for kind, shape in zip(outs, shapes)],
            compiler_params=pltpu.CompilerParams(vmem_limit_bytes=56 << 20),
        )(*[array for _, array in ins])

    def six(self, modulation):
        return "mod", modulation.reshape(self.slots, 6, self.width)

    def middle(self, attended, weights, output_bias, modulation):
        return self.per_image(
            middle_kernel,
            [("rows", jnp.float32), ("rows", jnp.float32), ("rows", jnp.bfloat16)],
            [
                ("rows", attended),
                ((1, 3), weights),
                ("all", output_bias),
                ("rows", self.hidden),
                self.six(modulation),
            ],
        )

    def expand(self, normed_two, unit, biases, index):
        bias = lax.dynamic_index_in_dim(biases, index, 0, keepdims=False)
        inner = times(normed_two, unit) + bias
        return inner, low(gelu(inner))

    def shrink(self, inner, active, shrink_slope, expand_unit, unit, *totals):
        active_slope = times_transposed(shrink_slope, unit)
        inner_slope = low(jax.vjp(gelu, inner)[1](active_slope)[0])
        out = times(active, unit)
        back = times_transposed(inner_slope, expand_unit)
        if totals:
            out, back = out + totals[0], back + totals[1]
        return inner_slope, column_sums(inner_slope)[None], out, back

    def finish(self, middle, branch, out, back, shrink_bias, modulation):
        layer_out, *others = self.per_image(
            finish_kernel,
            [
                ("rows", jnp.bfloat16),
                ("rows", jnp.float32),
                ("rows", jnp.bfloat16),
                (4, jnp.float32),
            ],
            [
                ("scalar", self.live),
                ("rows", middle),
                ("rows", branch),
                ("rows", out),
                ("rows", back),
                ("rows", self.flat(self.cotangent)),
                ("all", shrink_bias),
                self.six(modulation),
            ],
        )
        return layer_out.reshape(self.hidden_in.shape), *others

    def attention_back(self, slopes, queries, keys_all, values_all, logs):
        return attend_back(queries, keys_all, values_all, slopes, self.patch_mask, logs)

    def start_back(self, slopes, weights, middle_slope, modulation, later_slopes):
        gradient, first_slopes = self.per_image(
            start_back_kernel,
            [("rows", jnp.float32), (2, jnp.float32)],
            [("rows", slope) for slope in slopes]
            + [
                ((3, 0), weights),
                ("rows", middle_slope),
                ("rows", self.hidden),
                self.six(modulation),
            ],
        )
        modulation_slope = low(jnp.concatenate([first_slopes, later_slopes], 1))
        return gradient.reshape(self.hidden_in.shape), modulation_slope.reshape(self.slots, -1)

    def condition_back(self, slope):
        return jax.vjp(jax.nn.silu, self.condition.astype(jnp.float32))[1](slope)[0]


def act_rows(conditions, here, shard):
    rows = lax.dynamic_slice_in_dim(conditions, here * shard, shard, 1)
    return low(jax.nn.silu(rows.astype(jnp.float32)))


def unpack_kernel(parts, packed_ref, mod_ref, attend_ref, output_ref, expand_ref, shrink_ref):
    shard = output_ref.shape[1] // parts
    start = packed_ref.shape[1] - 14 * shard

    def joined(first, size):
        cut = [
            packed_ref[part : part + 1, start + first : start + first + size].astype(jnp.float32)
            for part in range(parts)
        ]
        return jnp.concatenate(cut, axis=1)

    mod_ref[...] = joined(0, 6 * shard)
    for row in range(2):
        attend_ref[row : row + 1] = joined((6 + row) * shard, shard)
    output_ref[...] = joined(8 * shard, shard)
    for unit in range(4):
        expand_ref[unit : unit + 1] = joined((9 + unit) * shard, shard)
    shrink_ref[...] = joined(13 * shard, shard)


def unpack(packed, shard):
    parts = packed.shape[0]
    width = parts * shard
    return pl.pallas_call(
        partial(unpack_kernel, parts),
        out_shape=[
            jax.ShapeDtypeStruct((rows, columns), jnp.float32)
            for rows, columns in ((1, 6 * width), (2, width), (1, width), (4, width), (1, width))
        ],
    )(packed)


def pack(condition, *biases):
    row = jnp.concatenate([condition.reshape(-1)] + [bias.reshape(-1) for bias in biases])
    return row[None]


def modulation_tail(modulation_slopes, conditions, here, shard, bias_size):
    weight = inner_rows(act_rows(conditions, here, shard), modulation_slopes)
    bias = lax.dynamic_slice_in_dim(modulation_slopes, here * bias_size, bias_size, 1)
    return weight, column_sums(bias)


def bias_tail(sums, here, shard):
    mine = lax.dynamic_slice_in_dim(sums, here * shard, shard, 1)
    return mine[0:2], mine[2], mine[4:8].reshape(-1), mine[3]


def condition_columns(gathered, image, slots):
    mine = lax.dynamic_slice_in_dim(gathered, image, slots, 1)
    return mine.transpose(1, 0, 2).reshape(slots, -1)


def plain_device(
    dp,
    rep,
    hidden_in,
    condition,
    patch_mask,
    image_counts,
    modulation_weight,
    modulation_bias,
    attend_weight,
    attend_bias,
    output_weight,
    output_bias,
    expand_weight,
    expand_bias,
    shrink_weight,
    shrink_bias,
    cotangent,
):
    here = lax.axis_index("dp")
    layer = Layer(hidden_in, condition, patch_mask, image_counts, cotangent)
    shard, width, slots = modulation_weight.shape[0], layer.width, layer.slots

    def whole(block):
        return lax.all_gather(block, "dp", axis=0, tiled=True)

    def summed(term):
        return lax.psum(
            lax.psum_scatter(term, "dp", scatter_dimension=0, tiled=True), "rep"
        ).astype(jnp.float32)

    packed = pack(
        condition, modulation_bias, attend_bias, output_bias, expand_bias, shrink_bias
    )
    packed = lax.all_gather(packed, "dp", axis=0, tiled=True)
    conditions = packed[:, : condition.size].reshape(-1, width)
    biases = unpack(packed, shard)
    expand_biases = biases[3].reshape(4, dp, shard).transpose(1, 0, 2).reshape(4, width)
    terms = times(act_rows(conditions, here, shard), modulation_weight)
    modulation = lax.psum_scatter(terms, "dp", scatter_dimension=0, tiled=True) + biases[0]
    weights = whole(jnp.concatenate([attend_weight, output_weight], 1))
    weights = weights.reshape(width, 4, width).transpose(1, 0, 2)
    expand_full, shrink_full = whole(expand_weight), whole(shrink_weight)
    normed_one = layer.start(modulation)
    shrink_slope = layer.shrink_slope(modulation)
    queries, keys_all, values_all, attended, logs = layer.attention(normed_one, weights, biases[1])
    branch, middle, normed_two = layer.middle(attended, weights, biases[2], modulation)
    totals = ()
    expand_terms, shrink_terms, inner_sums = [], [], []
    for unit in range(4):
        cut = slice(unit * width, (unit + 1) * width)
        inner, active = layer.expand(normed_two, expand_full[:, cut], expand_biases, unit)
        inner_slope, inner_sum, *totals = layer.shrink(
            inner, active, shrink_slope, expand_full[:, cut], shrink_full[cut], *totals
        )
        expand_terms.append(low(inner_rows(normed_two, inner_slope)))
        shrink_terms.append(low(inner_rows(active, shrink_slope)))
        inner_sums.append(inner_sum)
    layer_out, middle_slope, branch_low, later = layer.finish(
        middle, branch, *totals, biases[4], modulation
    )
    attended_slope = low(times_transposed(branch_low, weights[3]))
    slopes = layer.attention_back(attended_slope, queries, keys_all, values_all, logs)
    gradient_hidden, mod_slope = layer.start_back(
        slopes, weights, middle_slope, modulation, later
    )
    all_slopes = lax.all_gather(mod_slope, ("dp", "rep"), axis=0, tiled=True)
    all_conditions = lax.all_gather(condition, ("dp", "rep"), axis=0, tiled=True)
    mod_weight, mod_bias = modulation_tail(
        all_slopes, all_conditions, here, shard, modulation_bias.shape[0]
    )
    columns = lax.all_gather(times_transposed(all_slopes, modulation_weight), "dp")
    inner_sums = jnp.concatenate(inner_sums, 1).reshape(dp, 4, shard)
    inner_sums = inner_sums.transpose(1, 0, 2).reshape(4, width)
    others = [column_sums(value) for value in (slopes[0], slopes[2], branch_low, shrink_slope)]
    sums = lax.psum(jnp.concatenate([jnp.stack(others), inner_sums]), ("dp", "rep"))
    att_bias, out_bias, exp_bias, shr_bias = bias_tail(sums, here, shard)
    return (
        layer_out,
        gradient_hidden,
        layer.condition_back(condition_columns(columns, (here * rep + lax.axis_index("rep")) * slots, slots)),
        mod_weight,
        mod_bias,
        summed(low(inner_rows(normed_one, jnp.concatenate(slopes, 1)))),
        att_bias,
        summed(low(inner_rows(attended, branch_low))),
        out_bias,
        summed(jnp.concatenate(expand_terms, 1)),
        exp_bias,
        summed(jnp.concatenate(shrink_terms)),
        shr_bias,
    )


class Ticks:
    def __init__(self):
        self.ops = []

    def at(self, tick, outs, ins, call):
        outs, ins = [(names,) if isinstance(names, str) else names for names in (outs, ins)]
        self.ops.append((tick, len(self.ops), outs, ins, call))

    def run(self, results):
        ops = sorted(self.ops, key=lambda op: op[:2])
        last = {}
        for tick, _, _, ins, _ in ops:
            for name in ins:
                last[name] = tick
        state = {}
        for position, (tick, _, outs, ins, call) in enumerate(ops):
            values = call(*[state[name] for name in ins])
            if len(outs) == 1:
                values = (values,)
            state.update(zip(outs, values))
            ends = position + 1 == len(ops) or ops[position + 1][0] > tick
            if ends:
                names = sorted(name for name in state if last.get(name, -1) > tick)
                kept = [name for name in results if name in state and name not in names]
                final = {name: state[name] for name in kept}
                state = dict(zip(names, lax.optimization_barrier(tuple(state[n] for n in names))))
                state.update(final)
        return [state[name] for name in results]


def ticked_device(
    dp,
    rep,
    hidden_in,
    condition,
    patch_mask,
    image_counts,
    modulation_weight,
    modulation_bias,
    attend_weight,
    attend_bias,
    output_weight,
    output_bias,
    expand_weight,
    expand_bias,
    shrink_weight,
    shrink_bias,
    cotangent,
):
    here = lax.axis_index("dp")
    copy = lax.axis_index("rep")
    depth = dp // 2
    z, x, y, core = here // 2, here % 2, copy // 2, copy % 2
    order = [(2 * core + y) ^ step for step in range(4)]
    layer = Layer(hidden_in, condition, patch_mask, image_counts, cotangent)
    shard, width, slots = modulation_weight.shape[0], layer.width, layer.slots
    ticks = Ticks()
    at = ticks.at

    def up(value):
        return lax.ppermute(value, "dp", [(i, (i + 2) % dp) for i in range(dp)])

    def jump(step, value):
        return lax.ppermute(value, "dp", [(i, (i + 2 * step) % dp) for i in range(dp)])

    def swap_x(value):
        return lax.ppermute(value, "dp", [(i, i ^ 1) for i in range(dp)])

    def swap_y(value):
        return lax.ppermute(value, "rep", [(i, i ^ 2) for i in range(4)])

    def swap_core(value):
        return lax.ppermute(value, "rep", [(i, i ^ 1) for i in range(4)])

    def pair(one, two):
        return jnp.concatenate([one, two])

    def below(step):
        return (z - step) % depth

    def add(one, two):
        return low(one.astype(jnp.float32) + two.astype(jnp.float32))

    def attend_block(index):
        column = jnp.minimum(index, 2) * width
        block = lax.dynamic_slice_in_dim(attend_weight, column, width, 1)
        return jnp.where(index == 3, output_weight, block)[None]

    def shrink_block(index):
        return lax.dynamic_slice_in_dim(shrink_weight, index * shard, shard, 0)[None]

    def pick(stacked, index):
        return lax.dynamic_slice_in_dim(stacked, index, 1, 0)

    at(0, "A0", (), lambda: attend_block(order[0]))
    at(0, "a0", (), lambda: attend_block(order[1]))
    at(0, "Bs", (), lambda: regroup(expand_weight, dp))
    at(0, "P0", "Bs", lambda s: pick(s, order[1]))
    at(0, "C0", (), lambda: shrink_block(order[0]))
    at(0, "c0", (), lambda: shrink_block(order[1]))

    at(0, "AB0", ("A0", "Bs"), lambda p, q: pair(p, pick(q, order[0])))
    for name, ring_ticks, x_ticks in (
        ("AB", (0, 1, 2), (0, 1, 2, 3)),
        ("P", (3, 4, 5), (4, 5, 6, 6)),
        ("C", (3, 6, 7), (6, 7, 7, 8)),
    ):
        for step, tick in enumerate(ring_ticks):
            at(tick, f"{name}{step + 1}", f"{name}{step}", up)
        for step, tick in enumerate(x_ticks):
            at(tick, f"{name}x{step}", f"{name}{step}", swap_x)
    for step, tick in enumerate((1, 2, 3)):
        at(tick, f"ABy{step}", (f"ABx{step}", f"AB{step + 1}"),
           lambda p, q: swap_y(pair_rows(p, 0, q, 0)))
    at(4, "ABy3", "ABx3", lambda p: swap_y(p[:1]))
    for name, tick in (("C1", 5), ("Cx0", 7), ("Cx1", 8), ("C2", 8), ("Cx2", 8), ("C3", 9), ("Cx3", 9)):
        at(tick, f"{name}y", name, swap_y)

    def spot(step, cross):
        return 2 * below(step) + (1 - x if cross else x)

    def unit(blocks):
        parts = [(array, row) for array, row, _, _ in blocks]
        places = [spot(step, cross) for _, _, step, cross in blocks]
        return assemble(parts, places, dp).reshape(dp * shard, width)

    def streamed(zs, xs):
        return unit(
            [(array, row, step, False) for step, (array, row) in enumerate(zs)]
            + [(array, row, step, True) for step, (array, row) in enumerate(xs)]
        )

    def own_unit(row, *parts):
        return streamed([(part, row) for part in parts[:4]], [(part, row) for part in parts[4:]])

    def other_unit(local, *parts):
        return streamed(
            [(local, 0)] + [(part, 1) for part in parts[:3]], [(part, 0) for part in parts]
        )

    def steps(name, ending=""):
        zs = tuple(f"{name}{step}{ending}" for step in range(4))
        return zs, tuple(f"{name}x{step}{ending}" for step in range(4))

    for name, stream, row, tick in (
        ("Aown", "AB", 0, 4), ("Bown", "AB", 1, 5), ("By", "P", 0, 7), ("Cown", "C", 0, 9)
    ):
        zs, xs = steps(stream)
        at(tick, name, zs + xs, partial(own_unit, row))
    at(5, "Ay", ("a0",) + tuple(f"ABy{step}" for step in range(4)), other_unit)
    zs, xs = steps("C", "y")
    at(10, "Cy", ("c0",) + zs[1:] + xs, partial(own_unit, 0))
    at(4, "Ac", "Aown", swap_core)
    at(5, "Acy", "Ay", swap_core)
    at(6, "Bc", "Bown", swap_core)
    at(7, "Bcy", "By", swap_core)
    at(9, "Cc", "Cown", swap_core)
    at(10, "Ccy", "Cy", swap_core)

    def swap_z(distance, value):
        return lax.ppermute(value, "dp", [(i, i ^ (2 * distance)) for i in range(dp)])

    bits = {
        "core": (core, swap_core),
        "y": (y, swap_y),
        "x": (x, swap_x),
        "near": (z % 2, partial(swap_z, 1)),
        "far": (z // 2, partial(swap_z, 2)),
    }

    def grow(tick, name, axes):
        for axis in axes:
            bit, swap = bits[axis]

            def join(mine, other, bit=bit):
                return jnp.where(bit == 0, pair(mine, other), pair(other, mine))

            at(tick, name + "_in", name, swap)
            at(tick, name + "+", (name, name + "_in"), join)
            name += "+"
        return name

    def shrink_terms(tick, name, axes):
        for axis in axes:
            bit, swap = bits[axis]

            def send(terms, bit=bit, swap=swap):
                half = terms.shape[0] // 2
                return swap(lax.dynamic_slice_in_dim(terms, (1 - bit) * half, half, 0))

            def keep(terms, other, bit=bit):
                half = terms.shape[0] // 2
                return lax.dynamic_slice_in_dim(terms, bit * half, half, 0) + other

            at(tick, name + "_in", name, send)
            at(tick, name + "-", (name, name + "_in"), keep)
            name += "-"
        return name

    at(0, "small", (), lambda: pack(
        condition, modulation_bias, attend_bias, output_bias, expand_bias, shrink_bias))
    small = grow(0, "small", ("x",))
    small = grow(1, small, ("near",))
    small = grow(2, small, ("far",))
    at(3, ("mod_bias", "att_bias", "out_bias", "exp_bias", "shr_bias"), small,
       lambda packed: unpack(packed, shard))

    def first_terms(packed):
        conditions = packed[:, : condition.size].reshape(2, 2, 2, slots, width)
        conditions = conditions.transpose(2, 1, 0, 3, 4).reshape(-1, width)
        return times(act_rows(conditions, here, shard), modulation_weight)

    at(2, "terms", small, first_terms)
    terms = shrink_terms(3, "terms", ("x",))
    terms = shrink_terms(4, terms, ("near",))
    terms = shrink_terms(5, terms, ("far",))
    at(6, "mod", (f"{terms}", "mod_bias"), lambda terms, bias: terms + bias)
    at(6, "n1", "mod", layer.start)
    at(6, "gm", "mod", layer.shrink_slope)

    def natural(*units):
        return reorder(units, order, 8)

    at(6, "W", ("Aown", "Ay", "Ac", "Acy"), natural)
    at(6, ("q", "k", "v", "att", "logs"), ("n1", "W", "att_bias"), lambda n1, w, bias: layer.attention(n1, w, bias))
    at(7, ("branch", "middle", "n2"), ("att", "W", "out_bias", "mod"), layer.middle)

    def expand(index, n2, weight, biases):
        return layer.expand(n2, weight, biases, order[index])

    def term(left, right, *received):
        total = inner_rows(left, right)
        for value in received:
            total = total + value.astype(jnp.float32)
        return low(total)

    for index, (name, tick) in enumerate((("own", 7), ("y", 8), ("c", 7), ("cy", 8))):
        at(tick, (f"in_{name}", f"act_{name}"), ("n2", f"B{name}", "exp_bias"), partial(expand, index))
    at(7, "dC_c", ("act_c", "gm"), term)
    at(8, "dC_cy", ("act_cy", "gm"), term)
    at(9, "dC_own", ("act_own", "gm", "dC_rc"), term)
    at(10, "dC_y", ("act_y", "gm", "dC_rcy"), term)

    total = ()
    for index, (name, tick) in enumerate((("own", 9), ("c", 10), ("cy", 11), ("y", 12))):
        ins = (f"in_{name}", f"act_{name}", "gm", f"B{name}", f"C{name}") + total
        total = (f"out{index}", f"back{index}")
        at(tick, (f"gi_{name}", f"sum_{name}") + total, ins, layer.shrink)
    at(10, "dB_c", ("n2", "gi_c"), term)
    at(11, "dB_cy", ("n2", "gi_cy"), term)
    at(12, "dB_own", ("n2", "gi_own", "dB_rc"), term)
    at(13, "dB_y", ("n2", "gi_y", "dB_rcy"), term)

    at(13, ("layer_out", "middle_slope", "branch_low", "later"),
       ("middle", "branch", "out3", "back3", "shr_bias", "mod"), layer.finish)
    at(13, "g_att", ("branch_low", "W"), lambda b, w: low(times_transposed(b, w[3])))
    at(14, ("gq", "gk", "gv"), ("g_att", "q", "k", "v", "logs"), layer.attention_back)
    at(15, ("gradient_hidden", "mod_slope"), ("gq", "gk", "gv", "W", "middle_slope", "mod", "later"),
       lambda a, b, c, w, ms, mod, later: layer.start_back((a, b, c), w, ms, mod, later))

    def attend_term(index, n1, att, gq, gk, gv, branch_low, *received):
        which = order[index]
        right = lax.select_n(which, gq, gk, gv, branch_low)
        return term(jnp.where(which == 3, att, n1), right, *received)

    for index, (name, tick, received) in enumerate(
        (("own", 16, ("dA_rc",)), ("y", 16, ("dA_rcy",)), ("c", 14, ()), ("cy", 14, ()))
    ):
        ins = ("n1", "att", "gq", "gk", "gv", "branch_low") + received
        at(tick, f"dA_{name}", ins, partial(attend_term, index))

    def slab(step, moved, whole, *parts):
        cut = lax.dynamic_slice_in_dim(whole, below(step) * (2 * shard), 2 * shard, 0)
        if parts:
            cut = low(sum(value.astype(jnp.float32) for value in (cut,) + parts))
        return moved(cut)

    def stay(value):
        return value

    def along_ring(name, start, source, added):
        for step in range(1, 5):
            ins = (source,) + tuple(f"{part}{step}" for part in added)
            if step > 1:
                ins += (f"{name}{step - 1}",)
            at(start + step - 1, f"{name}{step}", ins, partial(slab, step, up if step < 4 else stay))
        at(start + 3, f"{name}_in", f"{name}4", lambda total: swap_x(
            lax.dynamic_slice_in_dim(total, (1 - x) * shard, shard, 0)))
        at(start + 4, f"{name}_sum", (f"{name}4", f"{name}_in"), lambda total, other: low(
            lax.dynamic_slice_in_dim(total, x * shard, shard, 0).astype(jnp.float32)
            + other.astype(jnp.float32)))
        return f"{name}_sum"

    def wide(name, start_own, start_other, late):
        one = along_ring(f"{name}_o", start_own, f"{name}_own", ())
        two = along_ring(f"{name}_p", start_other, f"{name}_y", ())
        at(late, f"{name}_yo", two, swap_y)
        at(late, f"{name}_yp", one, swap_y)
        at(late + 1, f"{name}_0", (one, f"{name}_yo"), add)
        at(late + 1, f"{name}_1", (two, f"{name}_yp"), add)
        at(late + 1, f"{name}_2", f"{name}_0", swap_core)
        at(late + 1, f"{name}_3", f"{name}_1", swap_core)
        return late + 2

    def halved(name, y_ticks, start_ring, late):
        for step, tick in enumerate(y_ticks, 1):
            at(tick, f"{name}_s{step}", f"{name}_y", partial(slab, step, swap_y))
        one = along_ring(f"{name}_o", start_ring, f"{name}_own", (f"{name}_s",))
        at(late, f"{name}_0", one, stay)
        at(late, f"{name}_1", one, swap_y)
        at(late + 1, f"{name}_2", one, swap_core)
        at(late + 1, f"{name}_3", f"{name}_1", swap_core)
        return late + 2

    for name, tick_one, tick_two in (("dC", 8, 9), ("dB", 11, 12), ("dA", 15, 15)):
        at(tick_one, f"{name}_rc", f"{name}_c", swap_core)
        at(tick_two, f"{name}_rcy", f"{name}_cy", swap_core)
    end_c = wide("dC", 9, 12, 21)
    end_b = halved("dB", (13, 14, 14, 15), 14, 20)
    end_a = halved("dA", (16, 17, 18, 19), 17, 21)

    def attend_out(*units):
        whole = jnp.zeros((4,) + units[0].shape, units[0].dtype)
        for index, value in zip(order, units):
            whole = lax.dynamic_update_slice(whole, value[None], (index, 0, 0))
        whole = whole.astype(jnp.float32)
        return jnp.concatenate([whole[0], whole[1], whole[2]], 1), whole[3]

    def shrink_out(*units):
        whole = assemble([(unit[None], 0) for unit in units], order, 4)
        return whole.reshape(-1, width).astype(jnp.float32)

    def four(name):
        return tuple(f"{name}_{i}" for i in range(4))

    at(end_c, "shr_weight", four("dC"), shrink_out)
    at(end_b, "exp_weight", four("dB"), lambda *units: spread(units, order, dp))
    at(end_a, ("att_weight", "out_weight"), four("dA"), attend_out)

    def join(tick, name, axis):
        at(tick, name + "_in", name, bits[axis][1])
        at(tick, name + "+", (name, name + "_in"), pair)
        return name + "+"

    mod_size = 6 * width
    def bias_terms(gq, gv, branch_low, gm, *sums):
        unit_sums = jnp.zeros((4, width), jnp.float32)
        for index, value in zip(order, sums):
            unit_sums = lax.dynamic_update_slice(unit_sums, value, (index, 0))
        others = jnp.stack([column_sums(value) for value in (gq, gv, branch_low, gm)])
        return low(pair(others, unit_sums)).reshape(slots, -1)

    at(15, "sums", ("gq", "gv", "branch_low", "gm", "sum_own", "sum_y", "sum_c", "sum_cy"), bias_terms)
    at(16, "sent", ("mod_slope", "sums"), lambda m, sums: jnp.concatenate([m, condition, sums], 1))
    sent = "sent"
    for tick, axis in ((16, "y"), (17, "far"), (18, "near"), (19, "x"), (19, "core")):
        sent = join(tick, sent, axis)

    def modulation_terms(sent):
        slopes = sent[:, :mod_size]
        weight, bias = modulation_tail(
            slopes, sent[:, mod_size : mod_size + width], here, shard, modulation_bias.shape[0]
        )
        row = lax.broadcasted_iota(jnp.int32, (slots, sent.shape[0]), 1)
        picked = low(row % slots == lax.broadcasted_iota(jnp.int32, row.shape, 0))
        sums = times(picked, sent[:, mod_size + width :]).reshape(-1, width)
        return (weight, bias) + bias_tail(sums, here, shard)

    at(20, "columns", sent, lambda sent: times_transposed(sent[:, :mod_size], modulation_weight))
    at(20, ("mod_weight", "mod_bias_out", "att_bias_out", "out_bias_out", "exp_bias_out", "shr_bias_out"),
       sent, modulation_terms)

    def trade(tick, name, axis, swap):
        at(tick, name + "_in", name, lambda held: swap(jnp.split(held, 2, axis)[1]))
        at(tick, name + "+", (name, name + "_in"), lambda held, got: jnp.stack(
            [jnp.split(held, 2, axis)[0], got]))
        return name + "+"

    at(20, "traded", "columns", lambda columns: columns.reshape(
        2, 2, 2, 2, 2, slots, shard)[0, :, :, :, 0])
    traded = trade(20, "traded", 0, swap_x)
    traded = trade(21, traded, 2, partial(swap_z, 1))
    traded = trade(22, traded, 4, partial(swap_z, 2))

    def condition_slope(held):
        for axis, bit in enumerate((z // 2, z % 2, x)):
            held = jnp.where(bit == 1, jnp.flip(held, axis), held)
        held = held.reshape(dp, slots, shard).transpose(1, 0, 2)
        return layer.condition_back(held.reshape(slots, width))

    at(23, "gradient_condition", traded, condition_slope)
    return tuple(
        ticks.run(
            [
                "layer_out",
                "gradient_hidden",
                "gradient_condition",
                "mod_weight",
                "mod_bias_out",
                "att_weight",
                "att_bias_out",
                "out_weight",
                "out_bias_out",
                "exp_weight",
                "exp_bias_out",
                "shr_weight",
                "shr_bias_out",
            ]
        )
    )


def solution(mesh):
    dp, rep = mesh.shape["dp"], mesh.shape["rep"]
    device = ticked_device if (dp, rep) == (8, 4) else plain_device
    return jax.shard_map(
        partial(device, dp, rep),
        mesh=mesh,
        in_specs=(
            P(("dp", "rep"), None, None),
            P(("dp", "rep"), None),
            P(("dp", "rep"), None),
            P(("dp", "rep")),
            P("dp", None),
            P("dp"),
            P("dp", None),
            P(None, "dp"),
            P("dp", None),
            P("dp"),
            P("dp", None),
            P("dp"),
            P("dp", None),
            P("dp"),
            P(("dp", "rep"), None, None),
        ),
        out_specs=(
            P(("dp", "rep"), None, None),
            P(("dp", "rep"), None, None),
            P(("dp", "rep"), None),
            P("dp", None),
            P("dp"),
            P("dp", None),
            P(None, "dp"),
            P("dp", None),
            P("dp"),
            P("dp", None),
            P("dp"),
            P("dp", None),
            P("dp"),
        ),
        check_vma=False,
    )
```

```python
import math
from functools import partial

import jax
import jax.numpy as jnp
from jax import lax
from jax.experimental import pallas as pl
from jax.experimental.pallas import tpu as pltpu
from jax.sharding import PartitionSpec as P

HEADS = 16


epsilon = 1e-06
masked_score = -1e30


def layer_norm(values):
    centered = values - jnp.mean(values, -1, keepdims=True)
    variance = jnp.mean(centered * centered, -1, keepdims=True)
    return centered * lax.rsqrt(variance + epsilon)


def modulate(values, shift_part, scale_part):
    return layer_norm(values) * (1.0 + scale_part) + shift_part


def gelu(values):
    return jax.nn.gelu(values, approximate=True)


def low(values):
    return values.astype(jnp.bfloat16)


def inner_rows(left_side, right_side):
    return lax.dot_general(
        left_side, right_side, (((0,), (0,)), ((), ())), preferred_element_type=jnp.float32
    )


def times(left_side, right_side):
    return jnp.dot(left_side, right_side, preferred_element_type=jnp.float32)


def times_transposed(left_side, right_side):
    return lax.dot_general(
        left_side, right_side, (((1,), (1,)), ((), ())), preferred_element_type=jnp.float32
    )


def column_sums(values):
    return jnp.sum(values, 0, dtype=jnp.float32)


def head_window(head, head_dim, model_width):
    first = head * head_dim
    last = first + head_dim
    start = first // 128 * 128
    stop = min(-(-last // 128) * 128, model_width)
    lane = lax.broadcasted_iota(jnp.int32, (1, stop - start), 1) + start
    return slice(start, stop), (lane >= first) & (lane < last)


def only(inside, values):
    return jnp.where(inside, values, jnp.zeros_like(values))


def head_order(heads):
    half = heads // 2
    return [head + shift for head in range(half) for shift in (0, half)]


def head_scores(query, key_window, valid, score_scale):
    scores = times_transposed(query, key_window) * score_scale
    return jnp.where(valid, scores, masked_score)


def attend_kernel(heads, query_ref, key_ref, value_ref, mask_ref, out_ref, log_ref, total_ref):
    patch_count, model_width = query_ref.shape
    head_dim = model_width // heads
    valid = mask_ref[0] > 0
    total_ref[...] = jnp.zeros_like(total_ref)
    for head in head_order(heads):
        cut, inside = head_window(head, head_dim, model_width)
        query = only(inside, query_ref[:, cut])
        scores = head_scores(query, key_ref[:, cut], valid, head_dim ** (-0.5))
        peak = jnp.max(scores, -1, keepdims=True)
        exponent = jnp.exp(scores - peak)
        row_total = jnp.sum(exponent, -1, keepdims=True)
        log_ref[:, head : head + 1] = peak + jnp.log(row_total)
        probs = low(exponent * (1.0 / row_total))
        total_ref[:, cut] += times(probs, only(inside, value_ref[:, cut]))
    out_ref[...] = low(total_ref[...])


def attend(queries, keys_all, values_all, patch_mask):
    slot_count, patch_count = patch_mask.shape
    model_width = queries.shape[1]
    block = pl.BlockSpec((patch_count, model_width), lambda slot: (slot, 0))
    return pl.pallas_call(
        partial(attend_kernel, HEADS),
        grid=(slot_count,),
        out_shape=[
            jax.ShapeDtypeStruct(queries.shape, jnp.bfloat16),
            jax.ShapeDtypeStruct((queries.shape[0], HEADS), jnp.float32),
        ],
        in_specs=[block] * 3 + [pl.BlockSpec((1, 1, patch_count), lambda slot: (slot, 0, 0))],
        out_specs=[block, pl.BlockSpec((patch_count, HEADS), lambda slot: (slot, 0))],
        scratch_shapes=[pltpu.VMEM((patch_count, model_width), jnp.float32)],
        compiler_params=pltpu.CompilerParams(vmem_limit_bytes=32 << 20),
    )(queries, keys_all, values_all, patch_mask[:, None, :])


def attend_back_kernel(
    heads,
    query_ref,
    key_ref,
    value_ref,
    slope_ref,
    mask_ref,
    log_ref,
    query_out,
    key_out,
    value_out,
    sums_out,
    query_total,
    key_total,
    value_total,
):
    patch_count, model_width = query_ref.shape
    head_dim = model_width // heads
    score_scale = head_dim ** (-0.5)
    valid = mask_ref[0] > 0
    for total in (query_total, key_total, value_total):
        total[...] = jnp.zeros_like(total)
    for head in head_order(heads):
        cut, inside = head_window(head, head_dim, model_width)
        query = only(inside, query_ref[:, cut])
        key = only(inside, key_ref[:, cut])
        slope = only(inside, slope_ref[:, cut])
        probs = jnp.exp(head_scores(query, key, valid, score_scale) - log_ref[:, head : head + 1])
        prob_slope = times_transposed(slope, value_ref[:, cut])
        row = jnp.sum(probs * prob_slope, -1, keepdims=True)
        score_slope = low(probs * (prob_slope - row))
        query_total[:, cut] += times(score_slope, key)
        key_total[:, cut] += inner_rows(score_slope, query)
        value_total[:, cut] += inner_rows(low(probs), slope)
    query_slope = low(query_total[...] * score_scale)
    query_out[...] = query_slope
    sums_out[0, 0:1] = jnp.sum(query_slope.astype(jnp.float32), 0, keepdims=True)
    key_out[...] = low(key_total[...] * score_scale)
    value_slope = low(value_total[...])
    value_out[...] = value_slope
    sums_out[0, 1:2] = jnp.sum(value_slope.astype(jnp.float32), 0, keepdims=True)


def attend_back(queries, keys_all, values_all, slopes, patch_mask, logs):
    slot_count, patch_count = patch_mask.shape
    model_width = queries.shape[1]
    block = pl.BlockSpec((patch_count, model_width), lambda slot: (slot, 0))
    return pl.pallas_call(
        partial(attend_back_kernel, HEADS),
        grid=(slot_count,),
        out_shape=[jax.ShapeDtypeStruct(queries.shape, jnp.bfloat16)] * 3
        + [jax.ShapeDtypeStruct((slot_count, 2, model_width), jnp.float32)],
        in_specs=[block] * 4
        + [
            pl.BlockSpec((1, 1, patch_count), lambda slot: (slot, 0, 0)),
            pl.BlockSpec((patch_count, HEADS), lambda slot: (slot, 0)),
        ],
        out_specs=[block] * 3 + [pl.BlockSpec((1, 2, model_width), lambda slot: (slot, 0, 0))],
        scratch_shapes=[pltpu.VMEM((patch_count, model_width), jnp.float32)] * 3,
        compiler_params=pltpu.CompilerParams(vmem_limit_bytes=32 << 20),
    )(queries, keys_all, values_all, slopes, patch_mask[:, None, :], logs)


def norm_parts(values):
    centered = values - jnp.mean(values, -1, keepdims=True)
    inverse = lax.rsqrt(jnp.mean(centered * centered, -1, keepdims=True) + epsilon)
    return centered * inverse, inverse


def norm_back(normed, inverse, slope):
    mean = jnp.mean(slope, -1, keepdims=True)
    return (slope - mean - normed * jnp.mean(slope * normed, -1, keepdims=True)) * inverse


def patch_sums(values):
    return jnp.sum(values, 0, keepdims=True)


def fetch(sources, held_ref, sems, places=None):
    copies = []
    for index, source in enumerate(sources):
        place = index if places is None else places[index]
        copies.append(pltpu.make_async_copy(source, held_ref.at[place], sems.at[index]))
    for copy in copies:
        copy.start()
    return copies


def project_kernel(
    order_ref, normed_ref, bias_ref, *refs
):
    units, outs, last_ref, held, sems = refs[:4], refs[4:7], refs[7], refs[8], refs[9]
    for copy in fetch(units, held, sems, order_ref):
        copy.wait()
    copy = pltpu.make_async_copy(held.at[3], last_ref, sems.at[4])
    copy.start()
    for index, row in ((0, 0), (1, None), (2, 1)):
        value = times(normed_ref[...], held[index])
        if row is not None:
            value = value + bias_ref[row : row + 1, :]
        outs[index][...] = low(value)
    copy.wait()


def project(normed, units, order, bias):
    rows, width = normed.shape
    vmem = pl.BlockSpec(memory_space=pltpu.VMEM)
    anywhere = pl.BlockSpec(memory_space=pl.ANY)
    return pl.pallas_call(
        project_kernel,
        in_specs=[pl.BlockSpec(memory_space=pltpu.SMEM), vmem, vmem] + [anywhere] * 4,
        out_specs=[vmem] * 3 + [anywhere],
        out_shape=[jax.ShapeDtypeStruct((rows, width), jnp.bfloat16)] * 3
        + [jax.ShapeDtypeStruct((width, width), jnp.bfloat16)],
        scratch_shapes=[
            pltpu.VMEM((4, width, width), jnp.bfloat16),
            pltpu.SemaphoreType.DMA((5,)),
        ],
        compiler_params=pltpu.CompilerParams(vmem_limit_bytes=40 << 20),
    )(jnp.stack(order).astype(jnp.int32), normed, bias, *units)


def middle_kernel(attended_ref, weight_ref, bias_ref, hidden_ref, mod_ref, branch_ref, middle_ref, normed_ref):
    gate_one, shift_two, scale_two = [mod_ref[0, i : i + 1] for i in (2, 3, 4)]
    branch = times(attended_ref[...], weight_ref[...]) + bias_ref[...]
    branch_ref[...] = branch
    middle = hidden_ref[...].astype(jnp.float32) + gate_one * branch
    middle_ref[...] = middle
    normed_ref[...] = low(norm_parts(middle)[0] * (1.0 + scale_two) + shift_two)


def finish_kernel(
    live_ref,
    middle_ref,
    branch_ref,
    out_ref,
    back_ref,
    cotangent_ref,
    bias_ref,
    mod_ref,
    layer_ref,
    middle_slope_ref,
    branch_low_ref,
    slopes_ref,
):
    gate_one, shift_two, scale_two, gate_two = [mod_ref[0, i : i + 1] for i in (2, 3, 4, 5)]
    live = live_ref[pl.program_id(0)]
    middle = middle_ref[...]
    mlp_out = out_ref[...] + bias_ref[...]
    layer_ref[...] = low(live * (middle + gate_two * mlp_out))
    slope = cotangent_ref[...].astype(jnp.float32) * live
    slopes_ref[0, 3:4] = patch_sums(slope * mlp_out)
    normed, inverse = norm_parts(middle)
    back = back_ref[...]
    slopes_ref[0, 1:2] = patch_sums(back)
    slopes_ref[0, 2:3] = patch_sums(back * normed)
    middle_slope = slope + norm_back(normed, inverse, back * (1.0 + scale_two))
    middle_slope_ref[...] = middle_slope
    slopes_ref[0, 0:1] = patch_sums(middle_slope * branch_ref[...])
    branch_low = low(middle_slope * gate_one)
    branch_low_ref[...] = branch_low
    slopes_ref[0, 4:5] = patch_sums(branch_low.astype(jnp.float32))
    slopes_ref[0, 5:6] = patch_sums(low(slope * gate_two).astype(jnp.float32))


def start_back_kernel(
    order_ref,
    query_ref,
    key_ref,
    value_ref,
    middle_slope_ref,
    hidden_ref,
    mod_ref,
    *refs,
):
    units, out_ref, slopes_ref, held, sems = refs[:4], refs[4], refs[5], refs[6], refs[7]

    @pl.when(pl.program_id(0) == 0)
    def _():
        for copy in fetch(units, held, sems, order_ref):
            copy.wait()

    scale_one = mod_ref[0, 1:2]
    back = times_transposed(query_ref[...], held[0])
    back += times_transposed(key_ref[...], held[1])
    back += times_transposed(value_ref[...], held[2])
    normed, inverse = norm_parts(hidden_ref[...].astype(jnp.float32))
    slopes_ref[0, 0:1] = patch_sums(back)
    slopes_ref[0, 1:2] = patch_sums(back * normed)
    out_ref[...] = middle_slope_ref[...] + norm_back(normed, inverse, back * (1.0 + scale_one))


def assemble_kernel(place_ref, *refs):
    blocks, whole_ref = refs[:-1], refs[-1]
    for index, block in enumerate(blocks):
        whole_ref[place_ref[index]] = block[0]


def assemble(blocks, places, count):
    shape = (count,) + blocks[0][0].shape[1:]

    def row_spec(row):
        return pl.BlockSpec((1,) + shape[1:], lambda step: (row, 0, 0))

    return pl.pallas_call(
        assemble_kernel,
        grid=(1,),
        in_specs=[pl.BlockSpec(memory_space=pltpu.SMEM)] + [row_spec(row) for _, row in blocks],
        out_specs=pl.BlockSpec(shape, lambda step: (0, 0, 0)),
        out_shape=jax.ShapeDtypeStruct(shape, blocks[0][0].dtype),
        compiler_params=pltpu.CompilerParams(vmem_limit_bytes=32 << 20),
        cost_estimate=pl.CostEstimate(
            flops=0, bytes_accessed=4 * count * shape[1] * shape[2], transcendentals=0
        ),
    )(jnp.stack(places).astype(jnp.int32), *[array for array, _ in blocks])


def rows_of(parts):
    if len(parts) == 1:
        return parts[0]
    row = lax.broadcasted_iota(jnp.int32, (2, 1, 1), 0)
    return jnp.where(row == 0, parts[0], parts[1])


def take(places, wholes, parts=()):
    count = len(places)
    total = 0.0
    for whole in wholes:
        cut = [lax.dynamic_slice_in_dim(whole, place, 1, 0) for place in places]
        total = total + rows_of(cut).astype(jnp.float32)
    for part, row in parts:
        total = total + part[row : row + count].astype(jnp.float32)
    return low(total)


def pair_rows(one, one_row, two, two_row):
    return rows_of([one[one_row : one_row + 1], two[two_row : two_row + 1]])


def reorder_kernel(place_ref, *refs):
    units, whole_ref = refs[:-1], refs[-1]
    for index, unit in enumerate(units):
        whole_ref[place_ref[index]] = unit[...]


def reorder(units, order, parts):
    rows, width = units[0].shape
    block = rows // parts
    return pl.pallas_call(
        reorder_kernel,
        grid=(parts,),
        in_specs=[pl.BlockSpec(memory_space=pltpu.SMEM)]
        + [pl.BlockSpec((block, width), lambda step: (step, 0))] * 4,
        out_specs=pl.BlockSpec((4, block, width), lambda step: (0, step, 0)),
        out_shape=jax.ShapeDtypeStruct((4, rows, width), units[0].dtype),
        compiler_params=pltpu.CompilerParams(vmem_limit_bytes=32 << 20),
        cost_estimate=pl.CostEstimate(
            flops=0, bytes_accessed=16 * rows * width, transcendentals=0
        ),
    )(jnp.stack(order).astype(jnp.int32), *units)


def regroup_kernel(parts, in_ref, out_ref):
    width = in_ref.shape[1] // (4 * parts)
    for unit in range(4):
        out_ref[unit] = jnp.concatenate(
            [
                in_ref[:, (4 * part + unit) * width : (4 * part + unit + 1) * width]
                for part in range(parts)
            ],
            axis=1,
        )


def regroup(columns, parts):
    rows, width = columns.shape
    return pl.pallas_call(
        partial(regroup_kernel, parts),
        out_shape=jax.ShapeDtypeStruct((4, rows, width // 4), columns.dtype),
        compiler_params=pltpu.CompilerParams(vmem_limit_bytes=32 << 20),
    )(columns)


def attend_out_kernel(order_ref, *refs):
    units, attend_ref, output_ref, held = refs[:4], refs[4], refs[5], refs[6]
    for index in range(4):
        held[order_ref[index]] = units[index][...]
    width = output_ref.shape[1]
    for unit in range(3):
        attend_ref[:, unit * width : (unit + 1) * width] = held[unit].astype(jnp.float32)
    output_ref[...] = held[3].astype(jnp.float32)


def attend_out(units, order):
    rows, width = units[0].shape
    vmem = pl.BlockSpec(memory_space=pltpu.VMEM)
    return pl.pallas_call(
        attend_out_kernel,
        in_specs=[pl.BlockSpec(memory_space=pltpu.SMEM)] + [vmem] * 4,
        out_specs=[vmem] * 2,
        out_shape=[
            jax.ShapeDtypeStruct((rows, 3 * width), jnp.float32),
            jax.ShapeDtypeStruct((rows, width), jnp.float32),
        ],
        scratch_shapes=[pltpu.VMEM((4, rows, width), units[0].dtype)],
        compiler_params=pltpu.CompilerParams(vmem_limit_bytes=32 << 20),
    )(jnp.stack(order).astype(jnp.int32), *units)


def spread_kernel(parts, order_ref, *refs):
    units, out_ref, held = refs[:4], refs[4], refs[5]
    for index in range(4):
        held[order_ref[index]] = units[index][...]
    width = units[0].shape[1] // parts
    out_ref[...] = jnp.concatenate(
        [
            held[unit, :, part * width : (part + 1) * width].astype(jnp.float32)
            for part in range(parts)
            for unit in range(4)
        ],
        axis=1,
    )


def spread(units, order, parts):
    rows, width = units[0].shape
    vmem = pl.BlockSpec(memory_space=pltpu.VMEM)
    return pl.pallas_call(
        partial(spread_kernel, parts),
        in_specs=[pl.BlockSpec(memory_space=pltpu.SMEM)] + [vmem] * 4,
        out_specs=vmem,
        out_shape=jax.ShapeDtypeStruct((rows, 4 * width), jnp.float32),
        scratch_shapes=[pltpu.VMEM((4, rows, width), units[0].dtype)],
        compiler_params=pltpu.CompilerParams(vmem_limit_bytes=32 << 20),
    )(jnp.stack(order).astype(jnp.int32), *units)


class Layer:
    def __init__(self, hidden_in, condition, patch_mask, image_counts, cotangent):
        self.slots, self.patches, self.width = hidden_in.shape
        self.rows = self.slots * self.patches
        self.patch_mask = patch_mask
        self.condition = condition
        self.live = (jnp.arange(self.slots) < image_counts[0]).astype(jnp.float32)
        self.hidden_in = hidden_in
        self.hidden = hidden_in.reshape(self.rows, self.width)
        self.cotangent = cotangent
        self.whole = (self.rows, self.width)

    def flat(self, values):
        return values.reshape(self.rows, self.width)

    def pieces(self, modulation):
        cut = modulation.reshape(self.slots, 6, 1, self.width)
        return [cut[:, i] for i in range(6)]

    def start(self, modulation):
        shift_one, scale_one = self.pieces(modulation)[:2]
        normed = modulate(self.hidden_in.astype(jnp.float32), shift_one, scale_one)
        return self.flat(low(normed))

    def shrink_slope(self, modulation):
        slope = self.cotangent.astype(jnp.float32) * self.live[:, None, None]
        return self.flat(low(slope * self.pieces(modulation)[5]))

    def attention(self, normed_one, units, order, attend_bias):
        queries, keys_all, values_all, output_full = project(
            normed_one, units, order, attend_bias
        )
        attended, logs = attend(queries, keys_all, values_all, self.patch_mask)
        return queries, keys_all, values_all, output_full, attended, logs

    def per_image(self, kernel, outs, ins, scratch=()):
        rows = pl.BlockSpec((self.patches, self.width), lambda slot: (slot, 0))

        def spec(kind, shape):
            if kind == "rows":
                return rows
            if kind == "scalar":
                return pl.BlockSpec(memory_space=pltpu.SMEM)
            if kind == "any":
                return pl.BlockSpec(memory_space=pl.ANY)
            if kind == "all":
                return pl.BlockSpec(shape, lambda slot: (0,) * len(shape))
            return pl.BlockSpec((1,) + shape[1:], lambda slot: (slot, 0, 0))

        shapes = [
            self.whole if kind == "rows" else (self.slots, kind, self.width) for kind, _ in outs
        ]
        return pl.pallas_call(
            kernel,
            grid=(self.slots,),
            in_specs=[spec(kind, array.shape) for kind, array in ins],
            out_specs=[spec(kind, shape) for (kind, _), shape in zip(outs, shapes)],
            out_shape=[jax.ShapeDtypeStruct(shape, kind[1]) for kind, shape in zip(outs, shapes)],
            scratch_shapes=list(scratch),
            compiler_params=pltpu.CompilerParams(vmem_limit_bytes=56 << 20),
        )(*[array for _, array in ins])

    def six(self, modulation):
        return "mod", modulation.reshape(self.slots, 6, self.width)

    def middle(self, attended, output_full, output_bias, modulation):
        return self.per_image(
            middle_kernel,
            [("rows", jnp.float32), ("rows", jnp.float32), ("rows", jnp.bfloat16)],
            [
                ("rows", attended),
                ("all", output_full),
                ("all", output_bias),
                ("rows", self.hidden),
                self.six(modulation),
            ],
        )

    def expand(self, normed_two, unit, biases, index):
        bias = lax.dynamic_index_in_dim(biases, index, 0, keepdims=False)
        inner = times(normed_two, unit) + bias
        return inner, low(gelu(inner))

    def shrink(self, inner, active, shrink_slope, expand_unit, unit, *totals):
        active_slope = times_transposed(shrink_slope, unit)
        inner_slope = low(jax.vjp(gelu, inner)[1](active_slope)[0])
        out = times(active, unit)
        back = times_transposed(inner_slope, expand_unit)
        if totals:
            out, back = out + totals[0], back + totals[1]
        return inner_slope, column_sums(inner_slope)[None], out, back

    def finish(self, middle, branch, out, back, shrink_bias, modulation):
        layer_out, *others = self.per_image(
            finish_kernel,
            [
                ("rows", jnp.bfloat16),
                ("rows", jnp.float32),
                ("rows", jnp.bfloat16),
                (6, jnp.float32),
            ],
            [
                ("scalar", self.live),
                ("rows", middle),
                ("rows", branch),
                ("rows", out),
                ("rows", back),
                ("rows", self.flat(self.cotangent)),
                ("all", shrink_bias),
                self.six(modulation),
            ],
        )
        return layer_out.reshape(self.hidden_in.shape), *others

    def attention_back(self, slopes, queries, keys_all, values_all, logs):
        return attend_back(queries, keys_all, values_all, slopes, self.patch_mask, logs)

    def start_back(self, slopes, units, order, middle_slope, modulation):
        gradient, first_slopes = self.per_image(
            start_back_kernel,
            [("rows", jnp.float32), (2, jnp.float32)],
            [("scalar", jnp.stack(order).astype(jnp.int32))]
            + [("rows", slope) for slope in slopes]
            + [("rows", middle_slope), ("rows", self.hidden), self.six(modulation)]
            + [("any", unit) for unit in units],
            [
                pltpu.VMEM((4, self.width, self.width), jnp.bfloat16),
                pltpu.SemaphoreType.DMA((4,)),
            ],
        )
        return gradient.reshape(self.hidden_in.shape), first_slopes

    def condition_back(self, slope):
        return jax.vjp(jax.nn.silu, self.condition.astype(jnp.float32))[1](slope)[0]


def act_rows(conditions, here, shard):
    rows = lax.dynamic_slice_in_dim(conditions, here * shard, shard, 1)
    return low(jax.nn.silu(rows.astype(jnp.float32)))


def unpack_kernel(parts, packed_ref, mod_ref, attend_ref, output_ref, expand_ref, shrink_ref):
    shard = output_ref.shape[1] // parts
    start = packed_ref.shape[1] - 14 * shard

    def joined(first, size):
        cut = [
            packed_ref[part : part + 1, start + first : start + first + size].astype(jnp.float32)
            for part in range(parts)
        ]
        return jnp.concatenate(cut, axis=1)

    mod_ref[...] = joined(0, 6 * shard)
    for row in range(2):
        attend_ref[row : row + 1] = joined((6 + row) * shard, shard)
    output_ref[...] = joined(8 * shard, shard)
    for unit in range(4):
        expand_ref[unit : unit + 1] = joined((9 + unit) * shard, shard)
    shrink_ref[...] = joined(13 * shard, shard)


def unpack(packed, shard):
    parts = packed.shape[0]
    width = parts * shard
    return pl.pallas_call(
        partial(unpack_kernel, parts),
        out_shape=[
            jax.ShapeDtypeStruct((rows, columns), jnp.float32)
            for rows, columns in ((1, 6 * width), (2, width), (1, width), (4, width), (1, width))
        ],
    )(packed)


def pack_slopes_kernel(order_ref, first_ref, later_ref, head_ref, condition_ref, *refs):
    units, out_ref, held_ref = refs[:4], refs[4], refs[5]
    for index, unit in enumerate(units):
        held_ref[pl.ds(order_ref[index], 1), :] = unit[...]
    slots, width = condition_ref.shape
    sums = [head_ref[0, i : i + 1] + head_ref[1, i : i + 1] for i in range(2)]
    sums += [later_ref[0, i : i + 1] + later_ref[1, i : i + 1] for i in (4, 5)]
    for slot in range(slots):
        parts = [first_ref[slot, i : i + 1] for i in range(2)]
        parts += [later_ref[slot, i : i + 1] for i in range(4)]
        parts += [condition_ref[slot : slot + 1, :].astype(jnp.float32)]
        parts += sums if slot == 0 else [held_ref[i : i + 1, :] for i in range(4)]
        out_ref[slot : slot + 1, :] = low(jnp.concatenate(parts, axis=1))


def pack_slopes(order, first, later, heads, condition, units):
    slots, width = condition.shape
    vmem = pl.BlockSpec(memory_space=pltpu.VMEM)
    return pl.pallas_call(
        pack_slopes_kernel,
        in_specs=[pl.BlockSpec(memory_space=pltpu.SMEM)] + [vmem] * 8,
        out_specs=vmem,
        out_shape=jax.ShapeDtypeStruct((slots, 11 * width), jnp.bfloat16),
        scratch_shapes=[pltpu.VMEM((4, width), jnp.float32)],
    )(jnp.stack(order).astype(jnp.int32), first, later, heads, condition, *units)


def pack(condition, *biases):
    row = jnp.concatenate([condition.reshape(-1)] + [bias.reshape(-1) for bias in biases])
    return row[None]


def modulation_tail(modulation_slopes, conditions, here, shard, bias_size):
    weight = inner_rows(act_rows(conditions, here, shard), modulation_slopes)
    bias = lax.dynamic_slice_in_dim(modulation_slopes, here * bias_size, bias_size, 1)
    return weight, column_sums(bias)


def bias_tail(sums, here, shard):
    mine = lax.dynamic_slice_in_dim(sums, here * shard, shard, 1)
    return mine[0:2], mine[2], mine[4:8].reshape(-1), mine[3]


def condition_columns(gathered, image, slots):
    mine = lax.dynamic_slice_in_dim(gathered, image, slots, 1)
    return mine.transpose(1, 0, 2).reshape(slots, -1)


def plain_device(
    dp,
    rep,
    hidden_in,
    condition,
    patch_mask,
    image_counts,
    modulation_weight,
    modulation_bias,
    attend_weight,
    attend_bias,
    output_weight,
    output_bias,
    expand_weight,
    expand_bias,
    shrink_weight,
    shrink_bias,
    cotangent,
):
    here = lax.axis_index("dp")
    layer = Layer(hidden_in, condition, patch_mask, image_counts, cotangent)
    shard, width, slots = modulation_weight.shape[0], layer.width, layer.slots

    def whole(block):
        return lax.all_gather(block, "dp", axis=0, tiled=True)

    def summed(term):
        return lax.psum(
            lax.psum_scatter(term, "dp", scatter_dimension=0, tiled=True), "rep"
        ).astype(jnp.float32)

    packed = pack(
        condition, modulation_bias, attend_bias, output_bias, expand_bias, shrink_bias
    )
    packed = lax.all_gather(packed, "dp", axis=0, tiled=True)
    conditions = packed[:, : condition.size].reshape(-1, width)
    biases = unpack(packed, shard)
    expand_biases = biases[3].reshape(4, dp, shard).transpose(1, 0, 2).reshape(4, width)
    terms = times(act_rows(conditions, here, shard), modulation_weight)
    modulation = lax.psum_scatter(terms, "dp", scatter_dimension=0, tiled=True) + biases[0]
    weights = whole(jnp.concatenate([attend_weight, output_weight], 1))
    weights = [weights[:, unit * width : (unit + 1) * width] for unit in range(4)]
    natural = [jnp.int32(unit) for unit in range(4)]
    expand_full, shrink_full = whole(expand_weight), whole(shrink_weight)
    normed_one = layer.start(modulation)
    shrink_slope = layer.shrink_slope(modulation)
    queries, keys_all, values_all, output_full, attended, logs = layer.attention(
        normed_one, weights, natural, biases[1]
    )
    branch, middle, normed_two = layer.middle(attended, output_full, biases[2], modulation)
    totals = ()
    expand_terms, shrink_terms, inner_sums = [], [], []
    for unit in range(4):
        cut = slice(unit * width, (unit + 1) * width)
        inner, active = layer.expand(normed_two, expand_full[:, cut], expand_biases, unit)
        inner_slope, inner_sum, *totals = layer.shrink(
            inner, active, shrink_slope, expand_full[:, cut], shrink_full[cut], *totals
        )
        expand_terms.append(low(inner_rows(normed_two, inner_slope)))
        shrink_terms.append(low(inner_rows(active, shrink_slope)))
        inner_sums.append(inner_sum)
    layer_out, middle_slope, branch_low, later = layer.finish(
        middle, branch, *totals, biases[4], modulation
    )
    attended_slope = low(times_transposed(branch_low, output_full))
    *slopes, head_sums = layer.attention_back(
        attended_slope, queries, keys_all, values_all, logs
    )
    gradient_hidden, first = layer.start_back(
        slopes, weights, natural, middle_slope, modulation
    )
    mod_slope = low(jnp.concatenate([first, later[:, :4]], 1)).reshape(slots, -1)
    all_slopes = lax.all_gather(mod_slope, ("dp", "rep"), axis=0, tiled=True)
    all_conditions = lax.all_gather(condition, ("dp", "rep"), axis=0, tiled=True)
    mod_weight, mod_bias = modulation_tail(
        all_slopes, all_conditions, here, shard, modulation_bias.shape[0]
    )
    columns = lax.all_gather(times_transposed(all_slopes, modulation_weight), "dp")
    inner_sums = jnp.concatenate(inner_sums, 1).reshape(dp, 4, shard)
    inner_sums = inner_sums.transpose(1, 0, 2).reshape(4, width)
    sums = jnp.concatenate([jnp.sum(head_sums, 0), jnp.sum(later[:, 4:], 0), inner_sums])
    sums = lax.psum(sums, ("dp", "rep"))
    att_bias, out_bias, exp_bias, shr_bias = bias_tail(sums, here, shard)
    return (
        layer_out,
        gradient_hidden,
        layer.condition_back(condition_columns(columns, (here * rep + lax.axis_index("rep")) * slots, slots)),
        mod_weight,
        mod_bias,
        summed(low(inner_rows(normed_one, jnp.concatenate(slopes, 1)))),
        att_bias,
        summed(low(inner_rows(attended, branch_low))),
        out_bias,
        summed(jnp.concatenate(expand_terms, 1)),
        exp_bias,
        summed(jnp.concatenate(shrink_terms)),
        shr_bias,
    )


class Ticks:
    def __init__(self):
        self.ops = []

    def at(self, tick, outs, ins, call):
        outs, ins = [(names,) if isinstance(names, str) else names for names in (outs, ins)]
        self.ops.append((tick, len(self.ops), outs, ins, call))

    def run(self, results):
        ops = sorted(self.ops, key=lambda op: op[:2])
        last = {}
        for tick, _, _, ins, _ in ops:
            for name in ins:
                last[name] = tick
        state = {}
        for position, (tick, _, outs, ins, call) in enumerate(ops):
            values = call(*[state[name] for name in ins])
            if len(outs) == 1:
                values = (values,)
            state.update(zip(outs, values))
            ends = position + 1 == len(ops) or ops[position + 1][0] > tick
            if ends:
                names = sorted(
                    name for name in state if last.get(name, -1) > tick or name in results
                )
                state = dict(zip(names, lax.optimization_barrier(tuple(state[n] for n in names))))
        return [state[name] for name in results]


class Names:
    def __getattr__(self, name):
        return name


def ticked_device(
    dp,
    rep,
    hidden_in,
    condition,
    patch_mask,
    image_counts,
    modulation_weight,
    modulation_bias,
    attend_weight,
    attend_bias,
    output_weight,
    output_bias,
    expand_weight,
    expand_bias,
    shrink_weight,
    shrink_bias,
    cotangent,
):
    n = Names()
    here = lax.axis_index(n.dp)
    copy = lax.axis_index(n.rep)
    depth = dp // 2
    z, x, y, core = here // 2, here % 2, copy // 2, copy % 2
    order = [(2 * core + y) ^ step for step in range(4)]
    layer = Layer(hidden_in, condition, patch_mask, image_counts, cotangent)
    shard, width, slots = modulation_weight.shape[0], layer.width, layer.slots
    ticks = Ticks()
    at = ticks.at

    def up(value):
        return lax.ppermute(value, n.dp, [(i, (i + 2) % dp) for i in range(dp)])

    def jump(step, value):
        return lax.ppermute(value, n.dp, [(i, (i + 2 * step) % dp) for i in range(dp)])

    def swap_x(value):
        return lax.ppermute(value, n.dp, [(i, i ^ 1) for i in range(dp)])

    def swap_y(value):
        return lax.ppermute(value, n.rep, [(i, i ^ 2) for i in range(4)])

    def swap_core(value):
        return lax.ppermute(value, n.rep, [(i, i ^ 1) for i in range(4)])

    def pair(one, two):
        return jnp.concatenate([one, two])

    def below(step):
        return (z - step) % depth

    def add(one, two):
        return low(one.astype(jnp.float32) + two.astype(jnp.float32))

    def attend_block(index):
        column = jnp.minimum(index, 2) * width
        block = lax.dynamic_slice_in_dim(attend_weight, column, width, 1)
        return jnp.where(index == 3, output_weight, block)[None]

    def shrink_block(index):
        return lax.dynamic_slice_in_dim(shrink_weight, index * shard, shard, 0)[None]

    def pick(stacked, index):
        return lax.dynamic_slice_in_dim(stacked, index, 1, 0)

    at(0, n.A0, (), lambda: attend_block(order[0]))
    at(0, n.a0, (), lambda: attend_block(order[1]))
    at(0, n.Bs, (), lambda: regroup(expand_weight, dp))
    at(0, n.P0, n.Bs, lambda s: pick(s, order[1]))
    at(0, n.C0, (), lambda: shrink_block(order[0]))
    at(0, n.c0, (), lambda: shrink_block(order[1]))

    at(0, n.AB0, (n.A0, n.Bs), lambda p, q: pair(p, pick(q, order[0])))
    for name, ring_ticks, x_ticks in (
        (n.AB, (0, 1, 2), (0, 1, 2, 3)),
        (n.P, (3, 4, 5), (4, 5)),
        (n.C, (3, 6, 7), (6, 7, 7, 8)),
    ):
        for step, tick in enumerate(ring_ticks):
            at(tick, (str(name) + str(step + 1)), (str(name) + str(step)), up)
        for step, tick in enumerate(x_ticks):
            at(tick, (str(name) + n.x + str(step)), (str(name) + str(step)), swap_x)
    for step in range(3):
        at(step + 1, (n.ABy + str(step)), ((n.ABx + str(step)), (n.AB + str(step + 1))),
           lambda p, q: swap_y(pair_rows(p, 0, q, 0)))
    at(4, n.ABy3, n.ABx3, lambda p: swap_y(p[:1]))
    at(6, n.Px23, (n.P2, n.P3), lambda p, q: swap_x(pair(p, q)))
    at(6, n.C1y, n.C1, swap_y)
    for tick, one, two in ((7, n.Cx0, n.C2), (8, n.Cx1, n.C3), (9, n.Cx2, n.Cx3)):
        at(tick, one + two, (one, two), lambda p, q: swap_y(pair(p, q)))

    def spot(step, cross):
        return 2 * below(step) + (1 - x if cross else x)

    def unit(blocks):
        parts = [(array, row) for array, row, _, _ in blocks]
        places = [spot(step, cross) for _, _, step, cross in blocks]
        return assemble(parts, places, dp).reshape(dp * shard, width)

    def streamed(zs, xs):
        return unit(
            [(array, row, step, False) for step, (array, row) in enumerate(zs)]
            + [(array, row, step, True) for step, (array, row) in enumerate(xs)]
        )

    def own_unit(row, *parts):
        return streamed([(part, row) for part in parts[:4]], [(part, row) for part in parts[4:]])

    def other_unit(local, *parts):
        return streamed(
            [(local, 0)] + [(part, 1) for part in parts[:3]], [(part, 0) for part in parts]
        )

    def other_late(local, one, two, three, four):
        return streamed(
            [(local, 0), (one, 0), (two, 1), (three, 1)], [(two, 0), (three, 0), (four, 0), (four, 1)]
        )

    def pair_unit(*parts):
        return streamed(
            [(part, 0) for part in parts[:4]], [(parts[4], 0), (parts[5], 0), (parts[6], 0), (parts[6], 1)]
        )

    for name, stream, row, tick in (
        (n.Aown, n.AB, 0, 5), (n.Bown, n.AB, 1, 6), (n.Cown, n.C, 0, 9)
    ):
        parts = tuple((str(stream) + str(step)) for step in range(4))
        parts += tuple((str(stream) + n.x + str(step)) for step in range(4))
        at(tick, name, parts, partial(own_unit, row))
    at(5, n.Ay, (n.a0,) + tuple((n.ABy + str(step)) for step in range(4)), other_unit)
    at(7, n.By, (n.P0, n.P1, n.P2, n.P3, n.Px0, n.Px1, n.Px23), pair_unit)
    at(10, n.Cy, (n.c0, n.C1y, n.Cx0C2, n.Cx1C3, n.Cx2Cx3), other_late)
    at(5, n.Ac, n.Aown, swap_core)
    at(5, n.Acy, n.Ay, swap_core)
    at(6, n.Bc, n.Bown, swap_core)
    at(7, n.Bcy, n.By, swap_core)
    at(9, n.Cc, n.Cown, swap_core)
    at(10, n.Ccy, n.Cy, swap_core)

    def swap_z(distance, value):
        return lax.ppermute(value, n.dp, [(i, i ^ (2 * distance)) for i in range(dp)])

    bits = {
        n.core: (core, swap_core),
        n.y: (y, swap_y),
        n.x: (x, swap_x),
        n.near: (z % 2, partial(swap_z, 1)),
        n.far: (z // 2, partial(swap_z, 2)),
    }

    def grow(tick, name, axes):
        for axis in axes:
            bit, swap = bits[axis]

            def join(mine, other, bit=bit):
                return jnp.where(bit == 0, pair(mine, other), pair(other, mine))

            at(tick, name + n._in, name, swap)
            at(tick, name + "+", (name, name + n._in), join)
            name += "+"
        return name

    def shrink_terms(tick, name, axes):
        for axis in axes:
            bit, swap = bits[axis]

            def send(terms, bit=bit, swap=swap):
                half = terms.shape[0] // 2
                return swap(lax.dynamic_slice_in_dim(terms, (1 - bit) * half, half, 0))

            def keep(terms, other, bit=bit):
                half = terms.shape[0] // 2
                return lax.dynamic_slice_in_dim(terms, bit * half, half, 0) + other

            at(tick, name + n._in, name, send)
            at(tick, name + "-", (name, name + n._in), keep)
            name += "-"
        return name

    at(0, n.small, (), lambda: pack(
        condition, modulation_bias, attend_bias, output_bias, expand_bias, shrink_bias))
    small = grow(0, n.small, (n.x,))
    small = grow(1, small, (n.near,))
    small = grow(2, small, (n.far,))
    at(3, (n.mod_bias, n.att_bias, n.out_bias, n.exp_bias, n.shr_bias), small,
       lambda packed: unpack(packed, shard))

    def first_terms(packed):
        conditions = packed[:, : condition.size].reshape(2, 2, 2, slots, width)
        conditions = conditions.transpose(2, 1, 0, 3, 4).reshape(-1, width)
        return times(act_rows(conditions, here, shard), modulation_weight)

    at(2, n.terms, small, first_terms)
    terms = shrink_terms(3, n.terms, (n.x,))
    terms = shrink_terms(4, terms, (n.near,))
    terms = shrink_terms(5, terms, (n.far,))
    at(6, n.mod, (str(terms), n.mod_bias), lambda terms, bias: terms + bias)
    at(6, n.n1, n.mod, layer.start)
    at(6, n.gm, n.mod, layer.shrink_slope)

    units_a = (n.Aown, n.Ay, n.Ac, n.Acy)
    at(6, (n.q, n.k, n.v, n.O, n.att, n.logs), (n.n1, n.att_bias) + units_a,
       lambda n1, bias, *units: layer.attention(n1, units, order, bias))
    at(7, (n.branch, n.middle, n.n2), (n.att, n.O, n.out_bias, n.mod), layer.middle)

    def expand(index, n2, weight, biases):
        return layer.expand(n2, weight, biases, order[index])

    def term(left, right, *received):
        total = inner_rows(left, right)
        for value in received:
            total = total + value.astype(jnp.float32)
        return low(total)

    for index, (name, tick) in enumerate(((n.own, 7), (n.y, 8), (n.c, 7), (n.cy, 8))):
        at(tick, ((n.in_ + str(name)), (n.act_ + str(name))), (n.n2, (n.B + str(name)), n.exp_bias), partial(expand, index))
    at(7, n.dC_c, (n.act_c, n.gm), term)
    at(8, n.dC_cy, (n.act_cy, n.gm), term)
    at(9, n.dC_own, (n.act_own, n.gm, n.dC_rc), term)
    at(10, n.dC_y, (n.act_y, n.gm, n.dC_rcy), term)

    total = ()
    for index, (name, tick) in enumerate(((n.own, 9), (n.c, 10), (n.cy, 11), (n.y, 12))):
        ins = ((n.in_ + str(name)), (n.act_ + str(name)), n.gm, (n.B + str(name)), (n.C + str(name))) + total
        total = ((n.out + str(index)), (n.back + str(index)))
        at(tick, ((n.gi_ + str(name)), (n.sum_ + str(name))) + total, ins, layer.shrink)
    at(10, n.dB_c, (n.n2, n.gi_c), term)
    at(11, n.dB_cy, (n.n2, n.gi_cy), term)
    at(12, n.dB_own, (n.n2, n.gi_own, n.dB_rc), term)
    at(13, n.dB_y, (n.n2, n.gi_y, n.dB_rcy), term)

    at(13, (n.layer_out, n.middle_slope, n.branch_low, n.later),
       (n.middle, n.branch, n.out3, n.back3, n.shr_bias, n.mod), layer.finish)
    at(13, n.g_att, (n.branch_low, n.O), lambda b, w: low(times_transposed(b, w)))
    at(14, (n.gq, n.gk, n.gv, n.head_sums), (n.g_att, n.q, n.k, n.v, n.logs), layer.attention_back)
    def attend_term(index, n1, att, gq, gk, gv, branch_low, *received):
        which = order[index]
        right = lax.select_n(which, gq, gk, gv, branch_low)
        return term(jnp.where(which == 3, att, n1), right, *received)

    for index, (name, tick, received) in enumerate(
        ((n.own, 15, ()), (n.y, 15, ()), (n.c, 14, ()), (n.cy, 14, ()))
    ):
        ins = (n.n1, n.att, n.gq, n.gk, n.gv, n.branch_low) + received
        at(tick, (n.dA_ + str(name)), ins, partial(attend_term, index))

    at(16, (n.gradient_hidden, n.first), (n.gq, n.gk, n.gv, n.middle_slope, n.mod) + units_a,
       lambda a, b, c, ms, mod, *units: layer.start_back((a, b, c), units, order, ms, mod))

    def slab(step, moved, count, *values):
        first = below(step) * (2 * shard)
        cuts = [lax.dynamic_slice_in_dim(value, first, 2 * shard, 0) for value in values[:count]]
        cuts += values[count:]
        if len(cuts) == 1:
            return moved(cuts[0])
        return moved(low(sum(value.astype(jnp.float32) for value in cuts)))

    def stay(value):
        return value

    def along_ring(name, start, source, added, rest=0):
        for step in range(1, 5):
            ins = source + tuple((str(part) + str(step)) for part in added)
            if step > 1:
                ins += ((str(name) + str(step - 1)),)
            at(start + step - 1, (str(name) + str(step)), ins, partial(slab, step, up if step < 4 else stay, len(source)))
        at(start + 3 + rest, (str(name) + n._in), (str(name) + str(4)), lambda total: swap_x(
            lax.dynamic_slice_in_dim(total, (1 - x) * shard, shard, 0)))
        at(start + 4 + rest, (str(name) + n._sum), ((str(name) + str(4)), (str(name) + n._in)), lambda total, other: low(
            lax.dynamic_slice_in_dim(total, x * shard, shard, 0).astype(jnp.float32)
            + other.astype(jnp.float32)))
        return (str(name) + n._sum)

    def wide(name, start_own, start_other, late):
        one = along_ring((str(name) + n._o), start_own, ((str(name) + n._own),), ())
        two = along_ring((str(name) + n._p), start_other, ((str(name) + n._y),), ())
        at(late, (str(name) + n._yo), two, swap_y)
        at(late, (str(name) + n._yp), one, swap_y)
        at(late + 1, (str(name) + n._0), (one, (str(name) + n._yo)), add)
        at(late + 1, (str(name) + n._1), (two, (str(name) + n._yp)), add)
        at(late + 1, (str(name) + n._2), (str(name) + n._0), swap_core)
        at(late + 1, (str(name) + n._3), (str(name) + n._1), swap_core)
        return late + 2

    def halved(name, cut_ticks, y_ticks, start_ring, late, received=(), rest=0):
        for step, tick in enumerate(y_ticks, 1):
            ins = ((str(name) + n._y),) + tuple((str(name) + n._ + str(part) + n.y) for part in received)
            at(cut_ticks[step - 1], (str(name) + n._t + str(step)), ins, partial(slab, step, stay, len(ins)))
            at(tick, (str(name) + n._s + str(step)), (str(name) + n._t + str(step)), swap_y)
        own = ((str(name) + n._own),) + tuple((str(name) + n._ + str(part)) for part in received)
        one = along_ring((str(name) + n._o), start_ring, own, ((str(name) + n._s),), rest)
        at(late, (str(name) + n._0), one, stay)
        at(late, (str(name) + n._1), one, swap_y)
        at(late + 1, (str(name) + n._2), one, swap_core)
        at(late + 1, (str(name) + n._3), (str(name) + n._1), swap_core)
        return late + 2

    for name, tick_one, tick_two in ((n.dC, 8, 9), (n.dB, 11, 12), (n.dA, 15, 15)):
        at(tick_one, (str(name) + n._rc), (str(name) + n._c), swap_core)
        at(tick_two, (str(name) + n._rcy), (str(name) + n._cy), swap_core)
    end_c = wide(n.dC, 9, 12, 20)
    end_b = halved(n.dB, (13, 14, 14, 15), (13, 14, 14, 15), 14, 20, rest=1)
    end_a = halved(n.dA, (16, 17, 18, 19), (16, 17, 18, 19), 17, 21, (n.rc,))

    def shrink_out(*units):
        whole = assemble([(unit[None], 0) for unit in units], order, 4)
        return whole.reshape(-1, width).astype(jnp.float32)

    def four(name):
        return tuple((str(name) + n._ + str(i)) for i in range(4))

    at(end_c, n.shr_weight, four(n.dC), shrink_out)
    at(end_b, n.exp_weight, four(n.dB), lambda *units: spread(units, order, dp))
    at(end_a, (n.att_weight, n.out_weight), four(n.dA), lambda *units: attend_out(units, order))

    def join(tick, name, axis):
        at(tick, name + n._in, name, bits[axis][1])
        at(tick, name + "+", (name, name + n._in), pair)
        return name + "+"

    mod_size = 6 * width
    at(16, n.sent, (n.first, n.later, n.head_sums, n.sum_own, n.sum_y, n.sum_c, n.sum_cy),
       lambda first, later, heads, *units: pack_slopes(
           order, first, later, heads, condition, units))
    sent = n.sent
    both_ways = [(4 * i + j, 4 * (i ^ 4) + (j ^ 2)) for i in range(dp) for j in range(4)]
    at(17, n.sent_far, sent, partial(swap_z, 2))
    at(17, n.sent_y, sent, swap_y)
    at(17, n.sent_both, sent, lambda rows: lax.ppermute(rows, (n.dp, n.rep), both_ways))
    at(17, n.rows, (sent, n.sent_far, n.sent_y, n.sent_both), lambda *rows: jnp.concatenate(rows))
    sent = n.rows
    for tick, axis in ((18, n.near), (19, n.x), (20, n.core)):
        sent = join(tick, sent, axis)

    def modulation_terms(sent):
        slopes = sent[:, :mod_size]
        weight, bias = modulation_tail(
            slopes, sent[:, mod_size : mod_size + width], here, shard, modulation_bias.shape[0]
        )
        row = lax.broadcasted_iota(jnp.int32, (slots, sent.shape[0]), 1)
        picked = low(row % slots == lax.broadcasted_iota(jnp.int32, row.shape, 0))
        sums = times(picked, sent[:, mod_size + width :]).reshape(-1, width)
        return (weight, bias) + bias_tail(sums, here, shard)

    at(20, n.columns, sent, lambda sent: times_transposed(sent[:, :mod_size], modulation_weight))
    at(20, (n.mod_weight, n.mod_bias_out, n.att_bias_out, n.out_bias_out, n.exp_bias_out, n.shr_bias_out),
       sent, modulation_terms)

    at(20, n.traded, n.columns, lambda columns: columns.reshape(
        2, 2, 2, 2, 2, slots, shard)[0, :, :, 0])
    at(20, n.traded_x, n.traded, lambda held: swap_x(held[1]))
    at(21, n.held, (n.traded, n.traded_x), lambda held, got: jnp.stack([held[0], got]))
    for step in (1, 2, 3):
        at(21, (n.held + str(step)), n.held, lambda held, step=step: swap_z(step, held[:, step % 2, step // 2]))

    def condition_slope(held, near, far, both):
        held = jnp.stack([held[:, 0, 0], far, near, both]).reshape(2, 2, 2, slots, shard)
        for axis, bit in enumerate((z % 2, z // 2, x)):
            held = jnp.where(bit == 1, jnp.flip(held, axis), held)
        held = held.transpose(3, 1, 0, 2, 4)
        return layer.condition_back(held.reshape(slots, width))

    at(22, n.gradient_condition, (n.held, n.held1, n.held2, n.held3), condition_slope)
    return tuple(
        ticks.run(
            [
                n.layer_out,
                n.gradient_hidden,
                n.gradient_condition,
                n.mod_weight,
                n.mod_bias_out,
                n.att_weight,
                n.att_bias_out,
                n.out_weight,
                n.out_bias_out,
                n.exp_weight,
                n.exp_bias_out,
                n.shr_weight,
                n.shr_bias_out,
            ]
        )
    )


def solution(mesh):
    dp, rep = mesh.shape["dp"], mesh.shape["rep"]
    device = ticked_device if (dp, rep) == (8, 4) else plain_device
    return jax.shard_map(
        partial(device, dp, rep),
        mesh=mesh,
        in_specs=(
            P(("dp", "rep"), None, None),
            P(("dp", "rep"), None),
            P(("dp", "rep"), None),
            P(("dp", "rep")),
            P("dp", None),
            P("dp"),
            P("dp", None),
            P(None, "dp"),
            P("dp", None),
            P("dp"),
            P("dp", None),
            P("dp"),
            P("dp", None),
            P("dp"),
            P(("dp", "rep"), None, None),
        ),
        out_specs=(
            P(("dp", "rep"), None, None),
            P(("dp", "rep"), None, None),
            P(("dp", "rep"), None),
            P("dp", None),
            P("dp"),
            P("dp", None),
            P(None, "dp"),
            P("dp", None),
            P("dp"),
            P("dp", None),
            P("dp"),
            P("dp", None),
            P("dp"),
        ),
        check_vma=False,
    )
```

```python
import math
from functools import partial

import jax
import jax.numpy as jnp
from jax import lax
from jax.experimental import pallas as pl
from jax.experimental.pallas import tpu as pltpu
from jax.sharding import PartitionSpec as P

HEADS = 16


epsilon = 1e-06
masked_score = -1e30


def gelu(values):
    return jax.nn.gelu(values, approximate=True)


def low(values):
    return values.astype(jnp.bfloat16)


def inner_rows(left_side, right_side):
    return lax.dot_general(
        left_side, right_side, (((0,), (0,)), ((), ())), preferred_element_type=jnp.float32
    )


def times(left_side, right_side):
    return jnp.dot(left_side, right_side, preferred_element_type=jnp.float32)


def times_transposed(left_side, right_side):
    return lax.dot_general(
        left_side, right_side, (((1,), (1,)), ((), ())), preferred_element_type=jnp.float32
    )


def column_sums(values):
    return jnp.sum(values, 0, dtype=jnp.float32)


def head_window(head, head_dim, model_width):
    first = head * head_dim
    last = first + head_dim
    start = first // 128 * 128
    stop = min(-(-last // 128) * 128, model_width)
    lane = lax.broadcasted_iota(jnp.int32, (1, stop - start), 1) + start
    return slice(start, stop), (lane >= first) & (lane < last)


def only(inside, values):
    return jnp.where(inside, values, jnp.zeros_like(values))


def head_order(heads):
    half = heads // 2
    return [head + shift for head in range(half) for shift in (0, half)]


def head_scores(query, key_window, valid, score_scale):
    scores = times_transposed(query, key_window) * score_scale
    return jnp.where(valid, scores, masked_score)


def attend_kernel(heads, query_ref, key_ref, value_ref, mask_ref, out_ref, log_ref, total_ref):
    patch_count, model_width = query_ref.shape
    head_dim = model_width // heads
    valid = mask_ref[0] > 0
    total_ref[...] = jnp.zeros_like(total_ref)
    for head in head_order(heads):
        cut, inside = head_window(head, head_dim, model_width)
        query = only(inside, query_ref[:, cut])
        scores = head_scores(query, key_ref[:, cut], valid, head_dim ** (-0.5))
        peak = jnp.max(scores, -1, keepdims=True)
        exponent = jnp.exp(scores - peak)
        row_total = jnp.sum(exponent, -1, keepdims=True)
        log_ref[:, head : head + 1] = peak + jnp.log(row_total)
        probs = low(exponent * (1.0 / row_total))
        total_ref[:, cut] += times(probs, only(inside, value_ref[:, cut]))
    out_ref[...] = low(total_ref[...])


def attend(queries, keys_all, values_all, patch_mask):
    slot_count, patch_count = patch_mask.shape
    model_width = queries.shape[1]
    block = pl.BlockSpec((patch_count, model_width), lambda slot: (slot, 0))
    return pl.pallas_call(
        partial(attend_kernel, HEADS),
        grid=(slot_count,),
        out_shape=[
            jax.ShapeDtypeStruct(queries.shape, jnp.bfloat16),
            jax.ShapeDtypeStruct((queries.shape[0], HEADS), jnp.float32),
        ],
        in_specs=[block] * 3 + [pl.BlockSpec((1, 1, patch_count), lambda slot: (slot, 0, 0))],
        out_specs=[block, pl.BlockSpec((patch_count, HEADS), lambda slot: (slot, 0))],
        scratch_shapes=[pltpu.VMEM((patch_count, model_width), jnp.float32)],
        compiler_params=pltpu.CompilerParams(vmem_limit_bytes=32 << 20),
    )(queries, keys_all, values_all, patch_mask[:, None, :])


def attend_back_kernel(
    heads,
    query_ref,
    key_ref,
    value_ref,
    slope_ref,
    mask_ref,
    log_ref,
    query_out,
    key_out,
    value_out,
    sums_out,
    query_total,
    key_total,
    value_total,
):
    patch_count, model_width = query_ref.shape
    head_dim = model_width // heads
    score_scale = head_dim ** (-0.5)
    valid = mask_ref[0] > 0
    for total in (query_total, key_total, value_total):
        total[...] = jnp.zeros_like(total)
    for head in head_order(heads):
        cut, inside = head_window(head, head_dim, model_width)
        query = only(inside, query_ref[:, cut])
        key = only(inside, key_ref[:, cut])
        slope = only(inside, slope_ref[:, cut])
        probs = jnp.exp(head_scores(query, key, valid, score_scale) - log_ref[:, head : head + 1])
        prob_slope = times_transposed(slope, value_ref[:, cut])
        row = jnp.sum(probs * prob_slope, -1, keepdims=True)
        score_slope = low(probs * (prob_slope - row))
        query_total[:, cut] += times(score_slope, key)
        key_total[:, cut] += inner_rows(score_slope, query)
        value_total[:, cut] += inner_rows(low(probs), slope)
    query_slope = low(query_total[...] * score_scale)
    query_out[...] = query_slope
    sums_out[0, 0:1] = jnp.sum(query_slope.astype(jnp.float32), 0, keepdims=True)
    key_out[...] = low(key_total[...] * score_scale)
    value_slope = low(value_total[...])
    value_out[...] = value_slope
    sums_out[0, 1:2] = jnp.sum(value_slope.astype(jnp.float32), 0, keepdims=True)


def attend_back(queries, keys_all, values_all, slopes, patch_mask, logs):
    slot_count, patch_count = patch_mask.shape
    model_width = queries.shape[1]
    block = pl.BlockSpec((patch_count, model_width), lambda slot: (slot, 0))
    return pl.pallas_call(
        partial(attend_back_kernel, HEADS),
        grid=(slot_count,),
        out_shape=[jax.ShapeDtypeStruct(queries.shape, jnp.bfloat16)] * 3
        + [jax.ShapeDtypeStruct((slot_count, 2, model_width), jnp.float32)],
        in_specs=[block] * 4
        + [
            pl.BlockSpec((1, 1, patch_count), lambda slot: (slot, 0, 0)),
            pl.BlockSpec((patch_count, HEADS), lambda slot: (slot, 0)),
        ],
        out_specs=[block] * 3 + [pl.BlockSpec((1, 2, model_width), lambda slot: (slot, 0, 0))],
        scratch_shapes=[pltpu.VMEM((patch_count, model_width), jnp.float32)] * 3,
        compiler_params=pltpu.CompilerParams(vmem_limit_bytes=32 << 20),
    )(queries, keys_all, values_all, slopes, patch_mask[:, None, :], logs)


def norm_parts(values):
    centered = values - jnp.mean(values, -1, keepdims=True)
    inverse = lax.rsqrt(jnp.mean(centered * centered, -1, keepdims=True) + epsilon)
    return centered * inverse, inverse


def norm_back(normed, inverse, slope):
    mean = jnp.mean(slope, -1, keepdims=True)
    return (slope - mean - normed * jnp.mean(slope * normed, -1, keepdims=True)) * inverse


def patch_sums(values):
    return jnp.sum(values, 0, keepdims=True)


def fetch(sources, held_ref, sems, places=None):
    copies = []
    for index, source in enumerate(sources):
        place = index if places is None else places[index]
        copies.append(pltpu.make_async_copy(source, held_ref.at[place], sems.at[index]))
    for copy in copies:
        copy.start()
    return copies


def project_kernel(
    order_ref, normed_ref, bias_ref, *refs
):
    units, outs, last_ref, held, sems = refs[:4], refs[4:7], refs[7], refs[8], refs[9]
    for copy in fetch(units, held, sems, order_ref):
        copy.wait()
    copy = pltpu.make_async_copy(held.at[3], last_ref, sems.at[4])
    copy.start()
    for index, row in ((0, 0), (1, None), (2, 1)):
        value = times(normed_ref[...], held[index])
        if row is not None:
            value = value + bias_ref[row : row + 1, :]
        outs[index][...] = low(value)
    copy.wait()


def project(normed, units, order, bias):
    rows, width = normed.shape
    vmem = pl.BlockSpec(memory_space=pltpu.VMEM)
    anywhere = pl.BlockSpec(memory_space=pl.ANY)
    return pl.pallas_call(
        project_kernel,
        in_specs=[pl.BlockSpec(memory_space=pltpu.SMEM), vmem, vmem] + [anywhere] * 4,
        out_specs=[vmem] * 3 + [anywhere],
        out_shape=[jax.ShapeDtypeStruct((rows, width), jnp.bfloat16)] * 3
        + [jax.ShapeDtypeStruct((width, width), jnp.bfloat16)],
        scratch_shapes=[
            pltpu.VMEM((4, width, width), jnp.bfloat16),
            pltpu.SemaphoreType.DMA((5,)),
        ],
        compiler_params=pltpu.CompilerParams(vmem_limit_bytes=40 << 20),
    )(jnp.stack(order).astype(jnp.int32), normed, bias, *units)


def start_kernel(
    live_ref, terms_ref, bias_ref, hidden_ref, cotangent_ref, normed_ref, slope_ref, mod_ref
):
    slot = pl.program_id(0)
    width = hidden_ref.shape[1]
    modulation = terms_ref[pl.ds(slot, 1), :] + bias_ref[...]
    cuts = [modulation[:, i * width : (i + 1) * width] for i in range(6)]
    for i in range(6):
        mod_ref[0, i : i + 1] = cuts[i]
    normed = norm_parts(hidden_ref[...].astype(jnp.float32))[0]
    normed_ref[...] = low(normed * (1.0 + cuts[1]) + cuts[0])
    slope_ref[...] = low(cotangent_ref[...].astype(jnp.float32) * live_ref[slot] * cuts[5])


def middle_kernel(attended_ref, weight_ref, bias_ref, hidden_ref, mod_ref, branch_ref, normed_ref):
    gate_one, shift_two, scale_two = [mod_ref[0, i : i + 1] for i in (2, 3, 4)]
    branch = times(attended_ref[...], weight_ref[...]) + bias_ref[...]
    branch_ref[...] = branch
    middle = hidden_ref[...].astype(jnp.float32) + gate_one * branch
    normed_ref[...] = low(norm_parts(middle)[0] * (1.0 + scale_two) + shift_two)


def finish_kernel(
    live_ref,
    hidden_ref,
    branch_ref,
    out_ref,
    back_ref,
    cotangent_ref,
    bias_ref,
    mod_ref,
    layer_ref,
    middle_slope_ref,
    branch_low_ref,
    slopes_ref,
):
    gate_one, shift_two, scale_two, gate_two = [mod_ref[0, i : i + 1] for i in (2, 3, 4, 5)]
    live = live_ref[pl.program_id(0)]
    branch = branch_ref[...]
    middle = hidden_ref[...].astype(jnp.float32) + gate_one * branch
    mlp_out = out_ref[...] + bias_ref[...]
    layer_ref[...] = low(live * (middle + gate_two * mlp_out))
    slope = cotangent_ref[...].astype(jnp.float32) * live
    slopes_ref[0, 3:4] = patch_sums(slope * mlp_out)
    normed, inverse = norm_parts(middle)
    back = back_ref[...]
    slopes_ref[0, 1:2] = patch_sums(back)
    slopes_ref[0, 2:3] = patch_sums(back * normed)
    middle_slope = slope + norm_back(normed, inverse, back * (1.0 + scale_two))
    middle_slope_ref[...] = middle_slope
    slopes_ref[0, 0:1] = patch_sums(middle_slope * branch)
    branch_low = low(middle_slope * gate_one)
    branch_low_ref[...] = branch_low
    slopes_ref[0, 4:5] = patch_sums(branch_low.astype(jnp.float32))
    slopes_ref[0, 5:6] = patch_sums(low(slope * gate_two).astype(jnp.float32))


def start_back_kernel(
    order_ref,
    query_ref,
    key_ref,
    value_ref,
    middle_slope_ref,
    hidden_ref,
    mod_ref,
    *refs,
):
    units, out_ref, slopes_ref, held, sems = refs[:4], refs[4], refs[5], refs[6], refs[7]

    @pl.when(pl.program_id(0) == 0)
    def _():
        for copy in fetch(units, held, sems, order_ref):
            copy.wait()

    scale_one = mod_ref[0, 1:2]
    back = times_transposed(query_ref[...], held[0])
    back += times_transposed(key_ref[...], held[1])
    back += times_transposed(value_ref[...], held[2])
    normed, inverse = norm_parts(hidden_ref[...].astype(jnp.float32))
    slopes_ref[0, 0:1] = patch_sums(back)
    slopes_ref[0, 1:2] = patch_sums(back * normed)
    out_ref[...] = middle_slope_ref[...] + norm_back(normed, inverse, back * (1.0 + scale_one))


def assemble_kernel(place_ref, *refs):
    blocks, whole_ref = refs[:-1], refs[-1]
    for index, block in enumerate(blocks):
        whole_ref[place_ref[index]] = block[0]


def assemble(blocks, places, count):
    shape = (count,) + blocks[0][0].shape[1:]

    def row_spec(row):
        return pl.BlockSpec((1,) + shape[1:], lambda step: (row, 0, 0))

    return pl.pallas_call(
        assemble_kernel,
        grid=(1,),
        in_specs=[pl.BlockSpec(memory_space=pltpu.SMEM)] + [row_spec(row) for _, row in blocks],
        out_specs=pl.BlockSpec(shape, lambda step: (0, 0, 0)),
        out_shape=jax.ShapeDtypeStruct(shape, blocks[0][0].dtype),
        compiler_params=pltpu.CompilerParams(vmem_limit_bytes=32 << 20),
        cost_estimate=pl.CostEstimate(
            flops=0, bytes_accessed=4 * count * shape[1] * shape[2], transcendentals=0
        ),
    )(jnp.stack(places).astype(jnp.int32), *[array for array, _ in blocks])


def rows_of(parts):
    if len(parts) == 1:
        return parts[0]
    row = lax.broadcasted_iota(jnp.int32, (2, 1, 1), 0)
    return jnp.where(row == 0, parts[0], parts[1])


def take(places, wholes, parts=()):
    count = len(places)
    total = 0.0
    for whole in wholes:
        cut = [lax.dynamic_slice_in_dim(whole, place, 1, 0) for place in places]
        total = total + rows_of(cut).astype(jnp.float32)
    for part, row in parts:
        total = total + part[row : row + count].astype(jnp.float32)
    return low(total)


def pair_rows(one, one_row, two, two_row):
    return rows_of([one[one_row : one_row + 1], two[two_row : two_row + 1]])


def reorder_kernel(place_ref, *refs):
    units, whole_ref = refs[:-1], refs[-1]
    for index, unit in enumerate(units):
        whole_ref[place_ref[index]] = unit[...]


def reorder(units, order, parts):
    rows, width = units[0].shape
    block = rows // parts
    return pl.pallas_call(
        reorder_kernel,
        grid=(parts,),
        in_specs=[pl.BlockSpec(memory_space=pltpu.SMEM)]
        + [pl.BlockSpec((block, width), lambda step: (step, 0))] * 4,
        out_specs=pl.BlockSpec((4, block, width), lambda step: (0, step, 0)),
        out_shape=jax.ShapeDtypeStruct((4, rows, width), units[0].dtype),
        compiler_params=pltpu.CompilerParams(vmem_limit_bytes=32 << 20),
        cost_estimate=pl.CostEstimate(
            flops=0, bytes_accessed=16 * rows * width, transcendentals=0
        ),
    )(jnp.stack(order).astype(jnp.int32), *units)


def regroup_kernel(parts, in_ref, out_ref):
    width = in_ref.shape[1] // (4 * parts)
    for unit in range(4):
        out_ref[unit] = jnp.concatenate(
            [
                in_ref[:, (4 * part + unit) * width : (4 * part + unit + 1) * width]
                for part in range(parts)
            ],
            axis=1,
        )


def regroup(columns, parts):
    rows, width = columns.shape
    return pl.pallas_call(
        partial(regroup_kernel, parts),
        out_shape=jax.ShapeDtypeStruct((4, rows, width // 4), columns.dtype),
        compiler_params=pltpu.CompilerParams(vmem_limit_bytes=32 << 20),
    )(columns)


def attend_out_kernel(order_ref, *refs):
    units, attend_ref, output_ref, held = refs[:4], refs[4], refs[5], refs[6]
    for index in range(4):
        held[order_ref[index]] = units[index][...]
    width = output_ref.shape[1]
    for unit in range(3):
        attend_ref[:, unit * width : (unit + 1) * width] = held[unit].astype(jnp.float32)
    output_ref[...] = held[3].astype(jnp.float32)


def attend_out(units, order):
    rows, width = units[0].shape
    vmem = pl.BlockSpec(memory_space=pltpu.VMEM)
    return pl.pallas_call(
        attend_out_kernel,
        in_specs=[pl.BlockSpec(memory_space=pltpu.SMEM)] + [vmem] * 4,
        out_specs=[vmem] * 2,
        out_shape=[
            jax.ShapeDtypeStruct((rows, 3 * width), jnp.float32),
            jax.ShapeDtypeStruct((rows, width), jnp.float32),
        ],
        scratch_shapes=[pltpu.VMEM((4, rows, width), units[0].dtype)],
        compiler_params=pltpu.CompilerParams(vmem_limit_bytes=32 << 20),
    )(jnp.stack(order).astype(jnp.int32), *units)


def shrink_out_kernel(order_ref, *refs):
    for index in range(4):
        refs[4][order_ref[index]] = refs[index][...].astype(jnp.float32)


def shrink_out(units, order):
    rows, width = units[0].shape
    vmem = pl.BlockSpec(memory_space=pltpu.VMEM)
    return pl.pallas_call(
        shrink_out_kernel,
        in_specs=[pl.BlockSpec(memory_space=pltpu.SMEM)] + [vmem] * 4,
        out_specs=vmem,
        out_shape=jax.ShapeDtypeStruct((4, rows, width), jnp.float32),
    )(jnp.stack(order).astype(jnp.int32), *units).reshape(4 * rows, width)


def spread_kernel(parts, order_ref, *refs):
    units, out_ref, held = refs[:4], refs[4], refs[5]
    for index in range(4):
        held[order_ref[index]] = units[index][...]
    width = units[0].shape[1] // parts
    out_ref[...] = jnp.concatenate(
        [
            held[unit, :, part * width : (part + 1) * width].astype(jnp.float32)
            for part in range(parts)
            for unit in range(4)
        ],
        axis=1,
    )


def spread(units, order, parts):
    rows, width = units[0].shape
    vmem = pl.BlockSpec(memory_space=pltpu.VMEM)
    return pl.pallas_call(
        partial(spread_kernel, parts),
        in_specs=[pl.BlockSpec(memory_space=pltpu.SMEM)] + [vmem] * 4,
        out_specs=vmem,
        out_shape=jax.ShapeDtypeStruct((rows, 4 * width), jnp.float32),
        scratch_shapes=[pltpu.VMEM((4, rows, width), units[0].dtype)],
        compiler_params=pltpu.CompilerParams(vmem_limit_bytes=32 << 20),
    )(jnp.stack(order).astype(jnp.int32), *units)


class Layer:
    def __init__(self, hidden_in, condition, patch_mask, image_counts, cotangent):
        self.slots, self.patches, self.width = hidden_in.shape
        self.rows = self.slots * self.patches
        self.patch_mask = patch_mask
        self.condition = condition
        self.live = (jnp.arange(self.slots) < image_counts[0]).astype(jnp.float32)
        self.hidden_in = hidden_in
        self.hidden = hidden_in.reshape(self.rows, self.width)
        self.cotangent = cotangent
        self.whole = (self.rows, self.width)

    def flat(self, values):
        return values.reshape(self.rows, self.width)

    def start(self, terms, bias):
        return self.per_image(
            start_kernel,
            [("rows", jnp.bfloat16), ("rows", jnp.bfloat16), (6, jnp.float32)],
            [
                ("scalar", self.live),
                ("all", terms),
                ("all", bias),
                ("rows", self.hidden),
                ("rows", self.flat(self.cotangent)),
            ],
        )

    def attention(self, normed_one, units, order, attend_bias):
        queries, keys_all, values_all, output_full = project(
            normed_one, units, order, attend_bias
        )
        attended, logs = attend(queries, keys_all, values_all, self.patch_mask)
        return queries, keys_all, values_all, output_full, attended, logs

    def per_image(self, kernel, outs, ins, scratch=()):
        rows = pl.BlockSpec((self.patches, self.width), lambda slot: (slot, 0))

        def spec(kind, shape):
            if kind == "rows":
                return rows
            if kind == "scalar":
                return pl.BlockSpec(memory_space=pltpu.SMEM)
            if kind == "any":
                return pl.BlockSpec(memory_space=pl.ANY)
            if kind == "all":
                return pl.BlockSpec(shape, lambda slot: (0,) * len(shape))
            return pl.BlockSpec((1,) + shape[1:], lambda slot: (slot, 0, 0))

        shapes = [
            self.whole if kind == "rows" else (self.slots, kind, self.width) for kind, _ in outs
        ]
        return pl.pallas_call(
            kernel,
            grid=(self.slots,),
            in_specs=[spec(kind, array.shape) for kind, array in ins],
            out_specs=[spec(kind, shape) for (kind, _), shape in zip(outs, shapes)],
            out_shape=[jax.ShapeDtypeStruct(shape, kind[1]) for kind, shape in zip(outs, shapes)],
            scratch_shapes=list(scratch),
            compiler_params=pltpu.CompilerParams(vmem_limit_bytes=56 << 20),
        )(*[array for _, array in ins])

    def middle(self, attended, output_full, output_bias, modulation):
        return self.per_image(
            middle_kernel,
            [("rows", jnp.float32), ("rows", jnp.bfloat16)],
            [
                ("rows", attended),
                ("all", output_full),
                ("all", output_bias),
                ("rows", self.hidden),
                ("mod", modulation),
            ],
        )

    def expand(self, normed_two, unit, biases, index):
        bias = lax.dynamic_index_in_dim(biases, index, 0, keepdims=False)
        inner = times(normed_two, unit) + bias
        return inner, low(gelu(inner))

    def shrink(self, inner, active, shrink_slope, expand_unit, unit, *totals):
        active_slope = times_transposed(shrink_slope, unit)
        inner_slope = low(jax.vjp(gelu, inner)[1](active_slope)[0])
        out = times(active, unit)
        back = times_transposed(inner_slope, expand_unit)
        if totals:
            out, back = out + totals[0], back + totals[1]
        ones = jnp.ones((8, self.rows), jnp.bfloat16)
        return inner_slope, times(ones, inner_slope), out, back

    def finish(self, branch, out, back, shrink_bias, modulation):
        layer_out, *others = self.per_image(
            finish_kernel,
            [
                ("rows", jnp.bfloat16),
                ("rows", jnp.float32),
                ("rows", jnp.bfloat16),
                (6, jnp.float32),
            ],
            [
                ("scalar", self.live),
                ("rows", self.hidden),
                ("rows", branch),
                ("rows", out),
                ("rows", back),
                ("rows", self.flat(self.cotangent)),
                ("all", shrink_bias),
                ("mod", modulation),
            ],
        )
        return layer_out.reshape(self.hidden_in.shape), *others

    def attention_back(self, slopes, queries, keys_all, values_all, logs):
        return attend_back(queries, keys_all, values_all, slopes, self.patch_mask, logs)

    def start_back(self, slopes, units, order, middle_slope, modulation):
        gradient, first_slopes = self.per_image(
            start_back_kernel,
            [("rows", jnp.float32), (2, jnp.float32)],
            [("scalar", jnp.stack(order).astype(jnp.int32))]
            + [("rows", slope) for slope in slopes]
            + [("rows", middle_slope), ("rows", self.hidden), ("mod", modulation)]
            + [("any", unit) for unit in units],
            [
                pltpu.VMEM((4, self.width, self.width), jnp.bfloat16),
                pltpu.SemaphoreType.DMA((4,)),
            ],
        )
        return gradient.reshape(self.hidden_in.shape), first_slopes

    def condition_back(self, slope):
        return jax.vjp(jax.nn.silu, self.condition.astype(jnp.float32))[1](slope)[0]


def act_rows(conditions, here, shard):
    rows = lax.dynamic_slice_in_dim(conditions, here * shard, shard, 1)
    return low(jax.nn.silu(rows.astype(jnp.float32)))


def unpack_kernel(parts, packed_ref, mod_ref, attend_ref, output_ref, expand_ref, shrink_ref):
    shard = output_ref.shape[1] // parts
    start = packed_ref.shape[1] - 14 * shard

    def joined(first, size):
        cut = [
            packed_ref[part : part + 1, start + first : start + first + size].astype(jnp.float32)
            for part in range(parts)
        ]
        return jnp.concatenate(cut, axis=1)

    mod_ref[...] = joined(0, 6 * shard)
    for row in range(2):
        attend_ref[row : row + 1] = joined((6 + row) * shard, shard)
    output_ref[...] = joined(8 * shard, shard)
    for unit in range(4):
        expand_ref[unit : unit + 1] = joined((9 + unit) * shard, shard)
    shrink_ref[...] = joined(13 * shard, shard)


def unpack(packed, shard):
    parts = packed.shape[0]
    width = parts * shard
    return pl.pallas_call(
        partial(unpack_kernel, parts),
        out_shape=[
            jax.ShapeDtypeStruct((rows, columns), jnp.float32)
            for rows, columns in ((1, 6 * width), (2, width), (1, width), (4, width), (1, width))
        ],
    )(packed)


def pack_slopes_kernel(order_ref, first_ref, later_ref, head_ref, condition_ref, *refs):
    units, out_ref, held_ref = refs[:4], refs[4], refs[5]
    for index, unit in enumerate(units):
        held_ref[pl.ds(order_ref[index], 1), :] = unit[0:1, :]
    slots, width = condition_ref.shape
    sums = [head_ref[0, i : i + 1] + head_ref[1, i : i + 1] for i in range(2)]
    sums += [later_ref[0, i : i + 1] + later_ref[1, i : i + 1] for i in (4, 5)]
    for slot in range(slots):
        parts = [first_ref[slot, i : i + 1] for i in range(2)]
        parts += [later_ref[slot, i : i + 1] for i in range(4)]
        parts += [condition_ref[slot : slot + 1, :].astype(jnp.float32)]
        parts += sums if slot == 0 else [held_ref[i : i + 1, :] for i in range(4)]
        out_ref[slot : slot + 1, :] = low(jnp.concatenate(parts, axis=1))


def pack_slopes(order, first, later, heads, condition, units):
    slots, width = condition.shape
    vmem = pl.BlockSpec(memory_space=pltpu.VMEM)
    return pl.pallas_call(
        pack_slopes_kernel,
        in_specs=[pl.BlockSpec(memory_space=pltpu.SMEM)] + [vmem] * 8,
        out_specs=vmem,
        out_shape=jax.ShapeDtypeStruct((slots, 11 * width), jnp.bfloat16),
        scratch_shapes=[pltpu.VMEM((4, width), jnp.float32)],
    )(jnp.stack(order).astype(jnp.int32), first, later, heads, condition, *units)


def pack(condition, *biases):
    row = jnp.concatenate([condition.reshape(-1)] + [bias.reshape(-1) for bias in biases])
    return row[None]


def modulation_tail(modulation_slopes, conditions, here, shard, bias_size):
    weight = inner_rows(act_rows(conditions, here, shard), modulation_slopes)
    bias = lax.dynamic_slice_in_dim(modulation_slopes, here * bias_size, bias_size, 1)
    return weight, column_sums(bias)


def bias_tail(sums, here, shard):
    mine = lax.dynamic_slice_in_dim(sums, here * shard, shard, 1)
    return mine[0:2], mine[2], mine[4:8].reshape(-1), mine[3]


def condition_columns(gathered, image, slots):
    mine = lax.dynamic_slice_in_dim(gathered, image, slots, 1)
    return mine.transpose(1, 0, 2).reshape(slots, -1)


def plain_device(
    dp,
    rep,
    hidden_in,
    condition,
    patch_mask,
    image_counts,
    modulation_weight,
    modulation_bias,
    attend_weight,
    attend_bias,
    output_weight,
    output_bias,
    expand_weight,
    expand_bias,
    shrink_weight,
    shrink_bias,
    cotangent,
):
    here = lax.axis_index("dp")
    layer = Layer(hidden_in, condition, patch_mask, image_counts, cotangent)
    shard, width, slots = modulation_weight.shape[0], layer.width, layer.slots

    def whole(block):
        return lax.all_gather(block, "dp", axis=0, tiled=True)

    def summed(term):
        return lax.psum(
            lax.psum_scatter(term, "dp", scatter_dimension=0, tiled=True), "rep"
        ).astype(jnp.float32)

    packed = pack(
        condition, modulation_bias, attend_bias, output_bias, expand_bias, shrink_bias
    )
    packed = lax.all_gather(packed, "dp", axis=0, tiled=True)
    conditions = packed[:, : condition.size].reshape(-1, width)
    biases = unpack(packed, shard)
    expand_biases = biases[3].reshape(4, dp, shard).transpose(1, 0, 2).reshape(4, width)
    terms = times(act_rows(conditions, here, shard), modulation_weight)
    terms = lax.psum_scatter(terms, "dp", scatter_dimension=0, tiled=True)
    normed_one, shrink_slope, modulation = layer.start(terms, biases[0])
    weights = whole(jnp.concatenate([attend_weight, output_weight], 1))
    weights = [weights[:, unit * width : (unit + 1) * width] for unit in range(4)]
    natural = [jnp.int32(unit) for unit in range(4)]
    expand_full, shrink_full = whole(expand_weight), whole(shrink_weight)
    queries, keys_all, values_all, output_full, attended, logs = layer.attention(
        normed_one, weights, natural, biases[1]
    )
    branch, normed_two = layer.middle(attended, output_full, biases[2], modulation)
    totals = ()
    expand_terms, shrink_terms, inner_sums = [], [], []
    for unit in range(4):
        cut = slice(unit * width, (unit + 1) * width)
        inner, active = layer.expand(normed_two, expand_full[:, cut], expand_biases, unit)
        inner_slope, inner_sum, *totals = layer.shrink(
            inner, active, shrink_slope, expand_full[:, cut], shrink_full[cut], *totals
        )
        expand_terms.append(low(inner_rows(normed_two, inner_slope)))
        shrink_terms.append(low(inner_rows(active, shrink_slope)))
        inner_sums.append(inner_sum[:1])
    layer_out, middle_slope, branch_low, later = layer.finish(
        branch, *totals, biases[4], modulation
    )
    attended_slope = low(times_transposed(branch_low, output_full))
    *slopes, head_sums = layer.attention_back(
        attended_slope, queries, keys_all, values_all, logs
    )
    gradient_hidden, first = layer.start_back(
        slopes, weights, natural, middle_slope, modulation
    )
    mod_slope = low(jnp.concatenate([first, later[:, :4]], 1)).reshape(slots, -1)
    all_slopes = lax.all_gather(mod_slope, ("dp", "rep"), axis=0, tiled=True)
    all_conditions = lax.all_gather(condition, ("dp", "rep"), axis=0, tiled=True)
    mod_weight, mod_bias = modulation_tail(
        all_slopes, all_conditions, here, shard, modulation_bias.shape[0]
    )
    columns = lax.all_gather(times_transposed(all_slopes, modulation_weight), "dp")
    inner_sums = jnp.concatenate(inner_sums, 1).reshape(dp, 4, shard)
    inner_sums = inner_sums.transpose(1, 0, 2).reshape(4, width)
    sums = jnp.concatenate([jnp.sum(head_sums, 0), jnp.sum(later[:, 4:], 0), inner_sums])
    sums = lax.psum(sums, ("dp", "rep"))
    att_bias, out_bias, exp_bias, shr_bias = bias_tail(sums, here, shard)
    return (
        layer_out,
        gradient_hidden,
        layer.condition_back(condition_columns(columns, (here * rep + lax.axis_index("rep")) * slots, slots)),
        mod_weight,
        mod_bias,
        summed(low(inner_rows(normed_one, jnp.concatenate(slopes, 1)))),
        att_bias,
        summed(low(inner_rows(attended, branch_low))),
        out_bias,
        summed(jnp.concatenate(expand_terms, 1)),
        exp_bias,
        summed(jnp.concatenate(shrink_terms)),
        shr_bias,
    )


class Ticks:
    def __init__(self):
        self.ops = []

    def at(self, tick, outs, ins, call):
        outs, ins = [(names,) if isinstance(names, str) else names for names in (outs, ins)]
        self.ops.append((tick, len(self.ops), outs, ins, call))

    def run(self, results):
        ops = sorted(self.ops, key=lambda op: op[:2])
        last = {}
        for tick, _, _, ins, _ in ops:
            for name in ins:
                last[name] = tick
        state = {}
        for position, (tick, _, outs, ins, call) in enumerate(ops):
            values = call(*[state[name] for name in ins])
            if len(outs) == 1:
                values = (values,)
            state.update(zip(outs, values))
            ends = position + 1 == len(ops) or ops[position + 1][0] > tick
            if ends:
                names = sorted(
                    name for name in state if last.get(name, -1) > tick or name in results
                )
                state = dict(zip(names, lax.optimization_barrier(tuple(state[n] for n in names))))
        return [state[name] for name in results]


class Names:
    def __getattr__(self, name):
        return name


def ticked_device(
    dp,
    rep,
    hidden_in,
    condition,
    patch_mask,
    image_counts,
    modulation_weight,
    modulation_bias,
    attend_weight,
    attend_bias,
    output_weight,
    output_bias,
    expand_weight,
    expand_bias,
    shrink_weight,
    shrink_bias,
    cotangent,
):
    n = Names()
    here = lax.axis_index(n.dp)
    copy = lax.axis_index(n.rep)
    depth = dp // 2
    z, x, y, core = here // 2, here % 2, copy // 2, copy % 2
    order = [(2 * core + y) ^ step for step in range(4)]
    layer = Layer(hidden_in, condition, patch_mask, image_counts, cotangent)
    shard, width, slots = modulation_weight.shape[0], layer.width, layer.slots
    ticks = Ticks()
    at = ticks.at

    def up(value):
        return lax.ppermute(value, n.dp, [(i, (i + 2) % dp) for i in range(dp)])

    def jump(step, value):
        return lax.ppermute(value, n.dp, [(i, (i + 2 * step) % dp) for i in range(dp)])

    def swap_x(value):
        return lax.ppermute(value, n.dp, [(i, i ^ 1) for i in range(dp)])

    def swap_y(value):
        return lax.ppermute(value, n.rep, [(i, i ^ 2) for i in range(4)])

    def swap_core(value):
        return lax.ppermute(value, n.rep, [(i, i ^ 1) for i in range(4)])

    def pair(one, two):
        return jnp.concatenate([one, two])

    def below(step):
        return (z - step) % depth

    def add(one, two):
        return low(one.astype(jnp.float32) + two.astype(jnp.float32))

    def attend_block(index):
        column = jnp.minimum(index, 2) * width
        block = lax.dynamic_slice_in_dim(attend_weight, column, width, 1)
        return jnp.where(index == 3, output_weight, block)[None]

    def shrink_block(index):
        return lax.dynamic_slice_in_dim(shrink_weight, index * shard, shard, 0)[None]

    def pick(stacked, index):
        return lax.dynamic_slice_in_dim(stacked, index, 1, 0)

    at(0, n.A0, (), lambda: attend_block(order[0]))
    at(0, n.a0, (), lambda: attend_block(order[1]))
    at(0, n.Bs, (), lambda: regroup(expand_weight, dp))
    at(0, n.P0, n.Bs, lambda s: pick(s, order[1]))
    at(0, n.C0, (), lambda: shrink_block(order[0]))
    at(0, n.c0, (), lambda: shrink_block(order[1]))

    at(0, n.AB0, (n.A0, n.Bs), lambda p, q: pair(p, pick(q, order[0])))
    for name, ring_ticks, x_ticks in (
        (n.AB, (0, 1, 2), (0, 1, 2, 3)),
        (n.P, (3, 4, 5), (4, 5)),
        (n.C, (3, 6, 7), (6, 7, 7, 8)),
    ):
        for step, tick in enumerate(ring_ticks):
            at(tick, (str(name) + str(step + 1)), (str(name) + str(step)), up)
        for step, tick in enumerate(x_ticks):
            at(tick, (str(name) + n.x + str(step)), (str(name) + str(step)), swap_x)
    for step in range(3):
        at(step + 1, (n.ABy + str(step)), ((n.ABx + str(step)), (n.AB + str(step + 1))),
           lambda p, q: swap_y(pair_rows(p, 0, q, 0)))
    at(4, n.ABy3, n.ABx3, lambda p: swap_y(p[:1]))
    at(6, n.Px23, (n.P2, n.P3), lambda p, q: swap_x(pair(p, q)))
    at(6, n.C1y, n.C1, swap_y)
    for tick, one, two in ((7, n.Cx0, n.C2), (8, n.Cx1, n.C3), (9, n.Cx2, n.Cx3)):
        at(tick, one + two, (one, two), lambda p, q: swap_y(pair(p, q)))

    def spot(step, cross):
        return 2 * below(step) + (1 - x if cross else x)

    def unit(blocks):
        parts = [(array, row) for array, row, _, _ in blocks]
        places = [spot(step, cross) for _, _, step, cross in blocks]
        return assemble(parts, places, dp).reshape(dp * shard, width)

    def streamed(zs, xs):
        return unit(
            [(array, row, step, False) for step, (array, row) in enumerate(zs)]
            + [(array, row, step, True) for step, (array, row) in enumerate(xs)]
        )

    def own_unit(row, *parts):
        return streamed([(part, row) for part in parts[:4]], [(part, row) for part in parts[4:]])

    def other_unit(local, *parts):
        return streamed(
            [(local, 0)] + [(part, 1) for part in parts[:3]], [(part, 0) for part in parts]
        )

    def other_late(local, one, two, three, four):
        return streamed(
            [(local, 0), (one, 0), (two, 1), (three, 1)], [(two, 0), (three, 0), (four, 0), (four, 1)]
        )

    def pair_unit(*parts):
        return streamed(
            [(part, 0) for part in parts[:4]], [(parts[4], 0), (parts[5], 0), (parts[6], 0), (parts[6], 1)]
        )

    for name, stream, row, tick in (
        (n.Aown, n.AB, 0, 4), (n.Bown, n.AB, 1, 5), (n.Cown, n.C, 0, 9)
    ):
        parts = tuple((str(stream) + str(step)) for step in range(4))
        parts += tuple((str(stream) + n.x + str(step)) for step in range(4))
        at(tick, name, parts, partial(own_unit, row))
    at(5, n.Ay, (n.a0,) + tuple((n.ABy + str(step)) for step in range(4)), other_unit)
    at(7, n.By, (n.P0, n.P1, n.P2, n.P3, n.Px0, n.Px1, n.Px23), pair_unit)
    at(10, n.Cy, (n.c0, n.C1y, n.Cx0C2, n.Cx1C3, n.Cx2Cx3), other_late)
    at(5, n.Ac, n.Aown, swap_core)
    at(5, n.Acy, n.Ay, swap_core)
    at(6, n.Bc, n.Bown, swap_core)
    at(7, n.Bcy, n.By, swap_core)
    at(9, n.Cc, n.Cown, swap_core)
    at(10, n.Ccy, n.Cy, swap_core)

    def swap_z(distance, value):
        return lax.ppermute(value, n.dp, [(i, i ^ (2 * distance)) for i in range(dp)])

    bits = {
        n.core: (core, swap_core),
        n.y: (y, swap_y),
        n.x: (x, swap_x),
        n.near: (z % 2, partial(swap_z, 1)),
        n.far: (z // 2, partial(swap_z, 2)),
    }

    def grow(tick, name, axes):
        for axis in axes:
            bit, swap = bits[axis]

            def join(mine, other, bit=bit):
                return jnp.where(bit == 0, pair(mine, other), pair(other, mine))

            at(tick, name + n._in, name, swap)
            at(tick, name + "+", (name, name + n._in), join)
            name += "+"
        return name

    def shrink_terms(tick, name, axes):
        for axis in axes:
            bit, swap = bits[axis]

            def send(terms, bit=bit, swap=swap):
                half = terms.shape[0] // 2
                return swap(lax.dynamic_slice_in_dim(terms, (1 - bit) * half, half, 0))

            def keep(terms, other, bit=bit):
                half = terms.shape[0] // 2
                return lax.dynamic_slice_in_dim(terms, bit * half, half, 0) + other

            at(tick, name + n._in, name, send)
            at(tick, name + "-", (name, name + n._in), keep)
            name += "-"
        return name

    at(0, n.small, (), lambda: pack(
        condition, modulation_bias, attend_bias, output_bias, expand_bias, shrink_bias))
    small = grow(0, n.small, (n.x,))
    small = grow(1, small, (n.near,))
    small = grow(2, small, (n.far,))
    at(3, (n.mod_bias, n.att_bias, n.out_bias, n.exp_bias, n.shr_bias), small,
       lambda packed: unpack(packed, shard))

    def first_terms(packed):
        conditions = packed[:, : condition.size].reshape(2, 2, 2, slots, width)
        conditions = conditions.transpose(2, 1, 0, 3, 4).reshape(-1, width)
        return times(act_rows(conditions, here, shard), modulation_weight)

    at(2, n.terms, small, first_terms)
    terms = shrink_terms(3, n.terms, (n.x,))
    terms = shrink_terms(4, terms, (n.near,))
    terms = shrink_terms(5, terms, (n.far,))
    at(6, (n.n1, n.gm, n.mod), (terms, n.mod_bias), layer.start)

    units_a = (n.Aown, n.Ay, n.Ac, n.Acy)
    at(6, (n.q, n.k, n.v, n.O, n.att, n.logs), (n.n1, n.att_bias) + units_a,
       lambda n1, bias, *units: layer.attention(n1, units, order, bias))
    at(7, (n.branch, n.n2), (n.att, n.O, n.out_bias, n.mod), layer.middle)

    def expand(index, n2, weight, biases):
        return layer.expand(n2, weight, biases, order[index])

    def term(left, right, *received):
        total = inner_rows(left, right)
        for value in received:
            total = total + value.astype(jnp.float32)
        return low(total)

    for index, (name, tick) in enumerate(((n.own, 7), (n.y, 8), (n.c, 7), (n.cy, 8))):
        at(tick, ((n.in_ + str(name)), (n.act_ + str(name))), (n.n2, (n.B + str(name)), n.exp_bias), partial(expand, index))
    at(7, n.dC_c, (n.act_c, n.gm), term)
    at(8, n.dC_cy, (n.act_cy, n.gm), term)
    at(9, n.dC_own, (n.act_own, n.gm, n.dC_rc), term)
    at(10, n.dC_y, (n.act_y, n.gm, n.dC_rcy), term)

    total = ()
    for index, (name, tick) in enumerate(((n.own, 9), (n.c, 10), (n.cy, 11), (n.y, 12))):
        ins = ((n.in_ + str(name)), (n.act_ + str(name)), n.gm, (n.B + str(name)), (n.C + str(name))) + total
        total = ((n.out + str(index)), (n.back + str(index)))
        at(tick, ((n.gi_ + str(name)), (n.sum_ + str(name))) + total, ins, layer.shrink)
    at(10, n.dB_c, (n.n2, n.gi_c), term)
    at(11, n.dB_cy, (n.n2, n.gi_cy), term)
    at(12, n.dB_own, (n.n2, n.gi_own, n.dB_rc), term)
    at(13, n.dB_y, (n.n2, n.gi_y, n.dB_rcy), term)

    at(13, (n.layer_out, n.middle_slope, n.branch_low, n.later),
       (n.branch, n.out3, n.back3, n.shr_bias, n.mod), layer.finish)
    at(13, n.g_att, (n.branch_low, n.O), lambda b, w: low(times_transposed(b, w)))
    at(14, (n.gq, n.gk, n.gv, n.head_sums), (n.g_att, n.q, n.k, n.v, n.logs), layer.attention_back)
    def attend_term(index, n1, att, gq, gk, gv, branch_low, *received):
        which = order[index]
        right = lax.select_n(which, gq, gk, gv, branch_low)
        return term(jnp.where(which == 3, att, n1), right, *received)

    for index, (name, tick, received) in enumerate(
        ((n.own, 15, ()), (n.y, 15, ()), (n.c, 14, ()), (n.cy, 14, ()))
    ):
        ins = (n.n1, n.att, n.gq, n.gk, n.gv, n.branch_low) + received
        at(tick, (n.dA_ + str(name)), ins, partial(attend_term, index))

    at(16, (n.gradient_hidden, n.first), (n.gq, n.gk, n.gv, n.middle_slope, n.mod) + units_a,
       lambda a, b, c, ms, mod, *units: layer.start_back((a, b, c), units, order, ms, mod))

    def slab(step, moved, count, *values):
        first = below(step) * (2 * shard)
        cuts = [lax.dynamic_slice_in_dim(value, first, 2 * shard, 0) for value in values[:count]]
        cuts += values[count:]
        if len(cuts) == 1:
            return moved(cuts[0])
        return moved(low(sum(value.astype(jnp.float32) for value in cuts)))

    def stay(value):
        return value

    def along_ring(name, start, source, added, rest=0):
        for step in range(1, 5):
            ins = source + tuple((str(part) + str(step)) for part in added)
            if step > 1:
                ins += ((str(name) + str(step - 1)),)
            at(start + step - 1, (str(name) + str(step)), ins, partial(slab, step, up if step < 4 else stay, len(source)))
        at(start + 3 + rest, (str(name) + n._in), (str(name) + str(4)), lambda total: swap_x(
            lax.dynamic_slice_in_dim(total, (1 - x) * shard, shard, 0)))
        at(start + 4 + rest, (str(name) + n._sum), ((str(name) + str(4)), (str(name) + n._in)), lambda total, other: low(
            lax.dynamic_slice_in_dim(total, x * shard, shard, 0).astype(jnp.float32)
            + other.astype(jnp.float32)))
        return (str(name) + n._sum)

    def wide(name, start_own, start_other, late):
        one = along_ring((str(name) + n._o), start_own, ((str(name) + n._own),), ())
        two = along_ring((str(name) + n._p), start_other, ((str(name) + n._y),), ())
        at(late, (str(name) + n._yo), two, swap_y)
        at(late, (str(name) + n._yp), one, swap_y)
        at(late + 1, (str(name) + n._0), (one, (str(name) + n._yo)), add)
        at(late + 1, (str(name) + n._1), (two, (str(name) + n._yp)), add)
        at(late + 1, (str(name) + n._2), (str(name) + n._0), swap_core)
        at(late + 1, (str(name) + n._3), (str(name) + n._1), swap_core)
        return late + 2

    def halved(name, cut_ticks, y_ticks, start_ring, late, received=(), rest=0):
        for step, tick in enumerate(y_ticks, 1):
            ins = ((str(name) + n._y),) + tuple((str(name) + n._ + str(part) + n.y) for part in received)
            at(cut_ticks[step - 1], (str(name) + n._t + str(step)), ins, partial(slab, step, stay, len(ins)))
            at(tick, (str(name) + n._s + str(step)), (str(name) + n._t + str(step)), swap_y)
        own = ((str(name) + n._own),) + tuple((str(name) + n._ + str(part)) for part in received)
        one = along_ring((str(name) + n._o), start_ring, own, ((str(name) + n._s),), rest)
        at(late, (str(name) + n._0), one, stay)
        at(late, (str(name) + n._1), one, swap_y)
        at(late + 1, (str(name) + n._2), one, swap_core)
        at(late + 1, (str(name) + n._3), (str(name) + n._1), swap_core)
        return late + 2

    for name, tick_one, tick_two in ((n.dC, 8, 9), (n.dB, 11, 12), (n.dA, 15, 15)):
        at(tick_one, (str(name) + n._rc), (str(name) + n._c), swap_core)
        at(tick_two, (str(name) + n._rcy), (str(name) + n._cy), swap_core)
    end_c = wide(n.dC, 9, 12, 20)
    end_b = halved(n.dB, (13, 14, 14, 15), (13, 14, 14, 15), 14, 19, rest=1)
    end_a = halved(n.dA, (16, 17, 18, 19), (16, 17, 18, 19), 17, 21, (n.rc,))

    def four(name):
        return tuple((str(name) + n._ + str(i)) for i in range(4))

    at(end_c, n.shr_weight, four(n.dC), lambda *units: shrink_out(units, order))
    at(end_b, n.exp_weight, four(n.dB), lambda *units: spread(units, order, dp))
    at(end_a, (n.att_weight, n.out_weight), four(n.dA), lambda *units: attend_out(units, order))

    def join(tick, name, axis):
        at(tick, name + n._in, name, bits[axis][1])
        at(tick, name + "+", (name, name + n._in), pair)
        return name + "+"

    mod_size = 6 * width
    at(16, n.sent, (n.first, n.later, n.head_sums, n.sum_own, n.sum_y, n.sum_c, n.sum_cy),
       lambda first, later, heads, *units: pack_slopes(
           order, first, later, heads, condition, units))
    sent = n.sent
    both_ways = [(4 * i + j, 4 * (i ^ 4) + (j ^ 2)) for i in range(dp) for j in range(4)]
    at(17, n.sent_far, sent, partial(swap_z, 2))
    at(17, n.sent_y, sent, swap_y)
    at(17, n.sent_both, sent, lambda rows: lax.ppermute(rows, (n.dp, n.rep), both_ways))
    at(17, n.rows, (sent, n.sent_far, n.sent_y, n.sent_both), lambda *rows: jnp.concatenate(rows))
    sent = n.rows
    for tick, axis in ((18, n.near), (19, n.x), (20, n.core)):
        sent = join(tick, sent, axis)

    def modulation_terms(sent):
        slopes = sent[:, :mod_size]
        weight, bias = modulation_tail(
            slopes, sent[:, mod_size : mod_size + width], here, shard, modulation_bias.shape[0]
        )
        row = lax.broadcasted_iota(jnp.int32, (slots, sent.shape[0]), 1)
        picked = low(row % slots == lax.broadcasted_iota(jnp.int32, row.shape, 0))
        sums = times(picked, sent[:, mod_size + width :]).reshape(-1, width)
        return (weight, bias) + bias_tail(sums, here, shard)

    at(20, n.columns, sent, lambda sent: times_transposed(sent[:, :mod_size], modulation_weight))
    at(20, (n.mod_weight, n.mod_bias_out, n.att_bias_out, n.out_bias_out, n.exp_bias_out, n.shr_bias_out),
       sent, modulation_terms)

    at(20, n.traded, n.columns, lambda columns: columns.reshape(
        2, 2, 2, 2, 2, slots, shard)[0, :, :, 0])
    at(20, n.traded_x, n.traded, lambda held: swap_x(held[1]))
    at(21, n.held, (n.traded, n.traded_x), lambda held, got: jnp.stack([held[0], got]))
    for step in (1, 2, 3):
        at(21, (n.held + str(step)), n.held, lambda held, step=step: swap_z(step, held[:, step % 2, step // 2]))

    def condition_slope(held, near, far, both):
        held = jnp.stack([held[:, 0, 0], far, near, both]).reshape(2, 2, 2, slots, shard)
        for axis, bit in enumerate((z % 2, z // 2, x)):
            held = jnp.where(bit == 1, jnp.flip(held, axis), held)
        held = held.transpose(3, 1, 0, 2, 4)
        return layer.condition_back(held.reshape(slots, width))

    at(22, n.gradient_condition, (n.held, n.held1, n.held2, n.held3), condition_slope)
    return tuple(
        ticks.run(
            [
                n.layer_out,
                n.gradient_hidden,
                n.gradient_condition,
                n.mod_weight,
                n.mod_bias_out,
                n.att_weight,
                n.att_bias_out,
                n.out_weight,
                n.out_bias_out,
                n.exp_weight,
                n.exp_bias_out,
                n.shr_weight,
                n.shr_bias_out,
            ]
        )
    )


def solution(mesh):
    dp, rep = mesh.shape["dp"], mesh.shape["rep"]
    device = ticked_device if (dp, rep) == (8, 4) else plain_device
    return jax.shard_map(
        partial(device, dp, rep),
        mesh=mesh,
        in_specs=(
            P(("dp", "rep"), None, None),
            P(("dp", "rep"), None),
            P(("dp", "rep"), None),
            P(("dp", "rep")),
            P("dp", None),
            P("dp"),
            P("dp", None),
            P(None, "dp"),
            P("dp", None),
            P("dp"),
            P("dp", None),
            P("dp"),
            P("dp", None),
            P("dp"),
            P(("dp", "rep"), None, None),
        ),
        out_specs=(
            P(("dp", "rep"), None, None),
            P(("dp", "rep"), None, None),
            P(("dp", "rep"), None),
            P("dp", None),
            P("dp"),
            P("dp", None),
            P(None, "dp"),
            P("dp", None),
            P("dp"),
            P("dp", None),
            P("dp"),
            P("dp", None),
            P("dp"),
        ),
        check_vma=False,
    )
```

```python
import math
from functools import partial

import jax
import jax.numpy as jnp
from jax import lax
from jax.experimental import pallas as pl
from jax.experimental.pallas import tpu as pltpu
from jax.sharding import PartitionSpec as P

HEADS = 16


epsilon = 1e-06
masked_score = -1e30


def gelu(values):
    return jax.nn.gelu(values, approximate=True)


def low(values):
    return values.astype(jnp.bfloat16)


def inner_rows(left_side, right_side):
    return lax.dot_general(
        left_side, right_side, (((0,), (0,)), ((), ())), preferred_element_type=jnp.float32
    )


def times(left_side, right_side):
    return jnp.dot(left_side, right_side, preferred_element_type=jnp.float32)


def times_transposed(left_side, right_side):
    return lax.dot_general(
        left_side, right_side, (((1,), (1,)), ((), ())), preferred_element_type=jnp.float32
    )


def column_sums(values):
    return jnp.sum(values, 0, dtype=jnp.float32)


def head_window(head, head_dim, model_width):
    first = head * head_dim
    last = first + head_dim
    start = first // 128 * 128
    stop = min(-(-last // 128) * 128, model_width)
    lane = lax.broadcasted_iota(jnp.int32, (1, stop - start), 1) + start
    return slice(start, stop), (lane >= first) & (lane < last)


def only(inside, values):
    return jnp.where(inside, values, jnp.zeros_like(values))


def head_order(heads):
    half = heads // 2
    return [head + shift for head in range(half) for shift in (0, half)]


def head_scores(query, key_window, valid, score_scale):
    scores = times_transposed(query, key_window) * score_scale
    return jnp.where(valid, scores, masked_score)


def attend_kernel(heads, query_ref, key_ref, value_ref, mask_ref, out_ref, log_ref, total_ref):
    patch_count, model_width = query_ref.shape
    head_dim = model_width // heads
    valid = mask_ref[0] > 0
    total_ref[...] = jnp.zeros_like(total_ref)
    for head in head_order(heads):
        cut, inside = head_window(head, head_dim, model_width)
        query = only(inside, query_ref[:, cut])
        scores = head_scores(query, key_ref[:, cut], valid, head_dim ** (-0.5))
        peak = jnp.max(scores, -1, keepdims=True)
        exponent = jnp.exp(scores - peak)
        row_total = jnp.sum(exponent, -1, keepdims=True)
        log_ref[:, head : head + 1] = peak + jnp.log(row_total)
        probs = low(exponent * (1.0 / row_total))
        total_ref[:, cut] += times(probs, only(inside, value_ref[:, cut]))
    out_ref[...] = low(total_ref[...])


def attend(queries, keys_all, values_all, patch_mask):
    slot_count, patch_count = patch_mask.shape
    model_width = queries.shape[1]
    block = pl.BlockSpec((patch_count, model_width), lambda slot: (slot, 0))
    return pl.pallas_call(
        partial(attend_kernel, HEADS),
        grid=(slot_count,),
        out_shape=[
            jax.ShapeDtypeStruct(queries.shape, jnp.bfloat16),
            jax.ShapeDtypeStruct((queries.shape[0], HEADS), jnp.float32),
        ],
        in_specs=[block] * 3 + [pl.BlockSpec((1, 1, patch_count), lambda slot: (slot, 0, 0))],
        out_specs=[block, pl.BlockSpec((patch_count, HEADS), lambda slot: (slot, 0))],
        scratch_shapes=[pltpu.VMEM((patch_count, model_width), jnp.float32)],
        compiler_params=pltpu.CompilerParams(vmem_limit_bytes=32 << 20),
    )(queries, keys_all, values_all, patch_mask[:, None, :])


def attend_back_kernel(
    heads,
    query_ref,
    key_ref,
    value_ref,
    slope_ref,
    mask_ref,
    log_ref,
    query_out,
    key_out,
    value_out,
    sums_out,
    query_total,
    key_total,
    value_total,
):
    patch_count, model_width = query_ref.shape
    head_dim = model_width // heads
    score_scale = head_dim ** (-0.5)
    valid = mask_ref[0] > 0
    for total in (query_total, key_total, value_total):
        total[...] = jnp.zeros_like(total)
    for head in head_order(heads):
        cut, inside = head_window(head, head_dim, model_width)
        query = only(inside, query_ref[:, cut])
        key = only(inside, key_ref[:, cut])
        slope = only(inside, slope_ref[:, cut])
        probs = jnp.exp(head_scores(query, key, valid, score_scale) - log_ref[:, head : head + 1])
        prob_slope = times_transposed(slope, value_ref[:, cut])
        row = jnp.sum(probs * prob_slope, -1, keepdims=True)
        score_slope = low(probs * (prob_slope - row))
        query_total[:, cut] += times(score_slope, key)
        key_total[:, cut] += inner_rows(score_slope, query)
        value_total[:, cut] += inner_rows(low(probs), slope)
    query_slope = low(query_total[...] * score_scale)
    query_out[...] = query_slope
    sums_out[0, 0:1] = jnp.sum(query_slope.astype(jnp.float32), 0, keepdims=True)
    key_out[...] = low(key_total[...] * score_scale)
    value_slope = low(value_total[...])
    value_out[...] = value_slope
    sums_out[0, 1:2] = jnp.sum(value_slope.astype(jnp.float32), 0, keepdims=True)


def attend_back(queries, keys_all, values_all, slopes, patch_mask, logs):
    slot_count, patch_count = patch_mask.shape
    model_width = queries.shape[1]
    block = pl.BlockSpec((patch_count, model_width), lambda slot: (slot, 0))
    return pl.pallas_call(
        partial(attend_back_kernel, HEADS),
        grid=(slot_count,),
        out_shape=[jax.ShapeDtypeStruct(queries.shape, jnp.bfloat16)] * 3
        + [jax.ShapeDtypeStruct((slot_count, 2, model_width), jnp.float32)],
        in_specs=[block] * 4
        + [
            pl.BlockSpec((1, 1, patch_count), lambda slot: (slot, 0, 0)),
            pl.BlockSpec((patch_count, HEADS), lambda slot: (slot, 0)),
        ],
        out_specs=[block] * 3 + [pl.BlockSpec((1, 2, model_width), lambda slot: (slot, 0, 0))],
        scratch_shapes=[pltpu.VMEM((patch_count, model_width), jnp.float32)] * 3,
        compiler_params=pltpu.CompilerParams(vmem_limit_bytes=32 << 20),
    )(queries, keys_all, values_all, slopes, patch_mask[:, None, :], logs)


def norm_parts(values):
    centered = values - jnp.mean(values, -1, keepdims=True)
    inverse = lax.rsqrt(jnp.mean(centered * centered, -1, keepdims=True) + epsilon)
    return centered * inverse, inverse


def norm_back(normed, inverse, slope):
    mean = jnp.mean(slope, -1, keepdims=True)
    return (slope - mean - normed * jnp.mean(slope * normed, -1, keepdims=True)) * inverse


def patch_sums(values):
    return jnp.sum(values, 0, keepdims=True)


def fetch(sources, held_ref, sems, places=None):
    copies = []
    for index, source in enumerate(sources):
        place = index if places is None else places[index]
        copies.append(pltpu.make_async_copy(source, held_ref.at[place], sems.at[index]))
    for copy in copies:
        copy.start()
    return copies


def begin_kernel(
    order_ref, live_ref, terms_ref, bias_ref, hidden_ref, cotangent_ref, attend_bias_ref, *refs
):
    units = refs[:4]
    normed_ref, slope_ref, mod_ref, query_ref, key_ref, value_ref = refs[4:10]
    last_ref, held, sems = refs[10:]
    copies = fetch(units, held, sems, order_ref)
    slots, _, width = mod_ref.shape
    patches = hidden_ref.shape[0] // slots
    for slot in range(slots):
        rows = slice(slot * patches, (slot + 1) * patches)
        modulation = terms_ref[slot : slot + 1, :] + bias_ref[...]
        cuts = [modulation[:, i * width : (i + 1) * width] for i in range(6)]
        for i in range(6):
            mod_ref[slot, i : i + 1] = cuts[i]
        normed = norm_parts(hidden_ref[rows, :].astype(jnp.float32))[0]
        normed_ref[rows, :] = low(normed * (1.0 + cuts[1]) + cuts[0])
        slope = cotangent_ref[rows, :].astype(jnp.float32) * live_ref[slot]
        slope_ref[rows, :] = low(slope * cuts[5])
    for copy in copies:
        copy.wait()
    copy = pltpu.make_async_copy(held.at[3], last_ref, sems.at[4])
    copy.start()
    query_ref[...] = low(times(normed_ref[...], held[0]) + attend_bias_ref[0:1, :])
    key_ref[...] = low(times(normed_ref[...], held[1]))
    value_ref[...] = low(times(normed_ref[...], held[2]) + attend_bias_ref[1:2, :])
    copy.wait()


def begin(order, live, terms, bias, hidden, cotangent, attend_bias, units):
    rows, width = hidden.shape
    vmem = pl.BlockSpec(memory_space=pltpu.VMEM)
    smem = pl.BlockSpec(memory_space=pltpu.SMEM)
    anywhere = pl.BlockSpec(memory_space=pl.ANY)
    whole = jax.ShapeDtypeStruct((rows, width), jnp.bfloat16)
    return pl.pallas_call(
        begin_kernel,
        in_specs=[smem, smem] + [vmem] * 5 + [anywhere] * 4,
        out_specs=[vmem] * 6 + [anywhere],
        out_shape=[whole, whole, jax.ShapeDtypeStruct((live.shape[0], 6, width), jnp.float32)]
        + [whole] * 3
        + [jax.ShapeDtypeStruct((width, width), jnp.bfloat16)],
        scratch_shapes=[
            pltpu.VMEM((4, width, width), jnp.bfloat16),
            pltpu.SemaphoreType.DMA((5,)),
        ],
        compiler_params=pltpu.CompilerParams(vmem_limit_bytes=40 << 20),
    )(jnp.stack(order).astype(jnp.int32), live, terms, bias, hidden, cotangent, attend_bias, *units)


def middle_kernel(attended_ref, weight_ref, bias_ref, hidden_ref, mod_ref, branch_ref, normed_ref):
    gate_one, shift_two, scale_two = [mod_ref[0, i : i + 1] for i in (2, 3, 4)]
    branch = times(attended_ref[...], weight_ref[...]) + bias_ref[...]
    branch_ref[...] = branch
    middle = hidden_ref[...].astype(jnp.float32) + gate_one * branch
    normed_ref[...] = low(norm_parts(middle)[0] * (1.0 + scale_two) + shift_two)


def finish_kernel(
    live_ref,
    hidden_ref,
    branch_ref,
    out_ref,
    back_ref,
    cotangent_ref,
    bias_ref,
    mod_ref,
    layer_ref,
    middle_slope_ref,
    branch_low_ref,
    slopes_ref,
):
    gate_one, shift_two, scale_two, gate_two = [mod_ref[0, i : i + 1] for i in (2, 3, 4, 5)]
    live = live_ref[pl.program_id(0)]
    branch = branch_ref[...]
    middle = hidden_ref[...].astype(jnp.float32) + gate_one * branch
    mlp_out = out_ref[...] + bias_ref[...]
    layer_ref[...] = low(live * (middle + gate_two * mlp_out))
    slope = cotangent_ref[...].astype(jnp.float32) * live
    slopes_ref[0, 3:4] = patch_sums(slope * mlp_out)
    normed, inverse = norm_parts(middle)
    back = back_ref[...]
    slopes_ref[0, 1:2] = patch_sums(back)
    slopes_ref[0, 2:3] = patch_sums(back * normed)
    middle_slope = slope + norm_back(normed, inverse, back * (1.0 + scale_two))
    middle_slope_ref[...] = middle_slope
    slopes_ref[0, 0:1] = patch_sums(middle_slope * branch)
    branch_low = low(middle_slope * gate_one)
    branch_low_ref[...] = branch_low
    slopes_ref[0, 4:5] = patch_sums(branch_low.astype(jnp.float32))
    slopes_ref[0, 5:6] = patch_sums(low(slope * gate_two).astype(jnp.float32))


def start_back_kernel(
    order_ref,
    query_ref,
    key_ref,
    value_ref,
    middle_slope_ref,
    hidden_ref,
    mod_ref,
    *refs,
):
    units, out_ref, slopes_ref, held, sems = refs[:4], *refs[4:]
    for copy in fetch(units, held, sems, order_ref):
        copy.wait()
    out_ref[...] = times_transposed(query_ref[...], held[0])
    out_ref[...] += times_transposed(key_ref[...], held[1])
    out_ref[...] += times_transposed(value_ref[...], held[2])
    slots = mod_ref.shape[0]
    patches = hidden_ref.shape[0] // slots
    for slot in range(slots):
        rows = slice(slot * patches, (slot + 1) * patches)
        normed, inverse = norm_parts(hidden_ref[rows, :].astype(jnp.float32))
        back = out_ref[rows, :]
        slopes_ref[slot, 0:1] = patch_sums(back)
        slopes_ref[slot, 1:2] = patch_sums(back * normed)
        scale_one = mod_ref[slot, 1:2]
        out_ref[rows, :] = middle_slope_ref[rows, :] + norm_back(
            normed, inverse, back * (1.0 + scale_one)
        )


def assemble_kernel(place_ref, *refs):
    blocks, whole_ref = refs[:-1], refs[-1]
    for index, block in enumerate(blocks):
        whole_ref[place_ref[index]] = block[0]


def assemble(blocks, places, count):
    shape = (count,) + blocks[0][0].shape[1:]

    def row_spec(row):
        return pl.BlockSpec((1,) + shape[1:], lambda step: (row, 0, 0))

    return pl.pallas_call(
        assemble_kernel,
        grid=(1,),
        in_specs=[pl.BlockSpec(memory_space=pltpu.SMEM)] + [row_spec(row) for _, row in blocks],
        out_specs=pl.BlockSpec(shape, lambda step: (0, 0, 0)),
        out_shape=jax.ShapeDtypeStruct(shape, blocks[0][0].dtype),
        compiler_params=pltpu.CompilerParams(vmem_limit_bytes=32 << 20),
        cost_estimate=pl.CostEstimate(
            flops=0, bytes_accessed=4 * count * shape[1] * shape[2], transcendentals=0
        ),
    )(jnp.stack(places).astype(jnp.int32), *[array for array, _ in blocks])


def rows_of(parts):
    if len(parts) == 1:
        return parts[0]
    row = lax.broadcasted_iota(jnp.int32, (2, 1, 1), 0)
    return jnp.where(row == 0, parts[0], parts[1])


def take(places, wholes, parts=()):
    count = len(places)
    total = 0.0
    for whole in wholes:
        cut = [lax.dynamic_slice_in_dim(whole, place, 1, 0) for place in places]
        total = total + rows_of(cut).astype(jnp.float32)
    for part, row in parts:
        total = total + part[row : row + count].astype(jnp.float32)
    return low(total)


def pair_rows(one, one_row, two, two_row):
    return rows_of([one[one_row : one_row + 1], two[two_row : two_row + 1]])


def reorder_kernel(place_ref, *refs):
    units, whole_ref = refs[:-1], refs[-1]
    for index, unit in enumerate(units):
        whole_ref[place_ref[index]] = unit[...]


def reorder(units, order, parts):
    rows, width = units[0].shape
    block = rows // parts
    return pl.pallas_call(
        reorder_kernel,
        grid=(parts,),
        in_specs=[pl.BlockSpec(memory_space=pltpu.SMEM)]
        + [pl.BlockSpec((block, width), lambda step: (step, 0))] * 4,
        out_specs=pl.BlockSpec((4, block, width), lambda step: (0, step, 0)),
        out_shape=jax.ShapeDtypeStruct((4, rows, width), units[0].dtype),
        compiler_params=pltpu.CompilerParams(vmem_limit_bytes=32 << 20),
        cost_estimate=pl.CostEstimate(
            flops=0, bytes_accessed=16 * rows * width, transcendentals=0
        ),
    )(jnp.stack(order).astype(jnp.int32), *units)


def regroup_kernel(parts, in_ref, out_ref):
    width = in_ref.shape[1] // (4 * parts)
    for unit in range(4):
        out_ref[unit] = jnp.concatenate(
            [
                in_ref[:, (4 * part + unit) * width : (4 * part + unit + 1) * width]
                for part in range(parts)
            ],
            axis=1,
        )


def regroup(columns, parts):
    rows, width = columns.shape
    return pl.pallas_call(
        partial(regroup_kernel, parts),
        out_shape=jax.ShapeDtypeStruct((4, rows, width // 4), columns.dtype),
        compiler_params=pltpu.CompilerParams(vmem_limit_bytes=32 << 20),
    )(columns)


def attend_out_kernel(order_ref, *refs):
    units, attend_ref, output_ref, held = refs[:4], refs[4], refs[5], refs[6]
    for index in range(4):
        held[order_ref[index]] = units[index][...]
    width = output_ref.shape[1]
    for unit in range(3):
        attend_ref[:, unit * width : (unit + 1) * width] = held[unit].astype(jnp.float32)
    output_ref[...] = held[3].astype(jnp.float32)


def attend_out(units, order):
    rows, width = units[0].shape
    vmem = pl.BlockSpec(memory_space=pltpu.VMEM)
    return pl.pallas_call(
        attend_out_kernel,
        in_specs=[pl.BlockSpec(memory_space=pltpu.SMEM)] + [vmem] * 4,
        out_specs=[vmem] * 2,
        out_shape=[
            jax.ShapeDtypeStruct((rows, 3 * width), jnp.float32),
            jax.ShapeDtypeStruct((rows, width), jnp.float32),
        ],
        scratch_shapes=[pltpu.VMEM((4, rows, width), units[0].dtype)],
        compiler_params=pltpu.CompilerParams(vmem_limit_bytes=32 << 20),
    )(jnp.stack(order).astype(jnp.int32), *units)


def shrink_out_kernel(order_ref, *refs):
    for index in range(4):
        refs[4][order_ref[index]] = refs[index][...].astype(jnp.float32)


def shrink_out(units, order):
    rows, width = units[0].shape
    vmem = pl.BlockSpec(memory_space=pltpu.VMEM)
    return pl.pallas_call(
        shrink_out_kernel,
        in_specs=[pl.BlockSpec(memory_space=pltpu.SMEM)] + [vmem] * 4,
        out_specs=vmem,
        out_shape=jax.ShapeDtypeStruct((4, rows, width), jnp.float32),
    )(jnp.stack(order).astype(jnp.int32), *units).reshape(4 * rows, width)


def spread_kernel(parts, order_ref, *refs):
    units, out_ref, held = refs[:4], refs[4], refs[5]
    for index in range(4):
        held[order_ref[index]] = units[index][...]
    width = units[0].shape[1] // parts
    out_ref[...] = jnp.concatenate(
        [
            held[unit, :, part * width : (part + 1) * width].astype(jnp.float32)
            for part in range(parts)
            for unit in range(4)
        ],
        axis=1,
    )


def spread(units, order, parts):
    rows, width = units[0].shape
    vmem = pl.BlockSpec(memory_space=pltpu.VMEM)
    return pl.pallas_call(
        partial(spread_kernel, parts),
        in_specs=[pl.BlockSpec(memory_space=pltpu.SMEM)] + [vmem] * 4,
        out_specs=vmem,
        out_shape=jax.ShapeDtypeStruct((rows, 4 * width), jnp.float32),
        scratch_shapes=[pltpu.VMEM((4, rows, width), units[0].dtype)],
        compiler_params=pltpu.CompilerParams(vmem_limit_bytes=32 << 20),
    )(jnp.stack(order).astype(jnp.int32), *units)


class Layer:
    def __init__(self, hidden_in, condition, patch_mask, image_counts, cotangent):
        self.slots, self.patches, self.width = hidden_in.shape
        self.rows = self.slots * self.patches
        self.patch_mask = patch_mask
        self.condition = condition
        self.live = (jnp.arange(self.slots) < image_counts[0]).astype(jnp.float32)
        self.hidden_in = hidden_in
        self.hidden = hidden_in.reshape(self.rows, self.width)
        self.cotangent = cotangent
        self.whole = (self.rows, self.width)

    def flat(self, values):
        return values.reshape(self.rows, self.width)

    def begin(self, order, terms, bias, attend_bias, *units):
        cotangent = self.flat(self.cotangent)
        return begin(order, self.live, terms, bias, self.hidden, cotangent, attend_bias, units)

    def attention(self, queries, keys_all, values_all):
        return attend(queries, keys_all, values_all, self.patch_mask)

    def per_image(self, kernel, outs, ins, scratch=()):
        rows = pl.BlockSpec((self.patches, self.width), lambda slot: (slot, 0))

        def spec(kind, shape):
            if kind == "rows":
                return rows
            if kind == "scalar":
                return pl.BlockSpec(memory_space=pltpu.SMEM)
            if kind == "any":
                return pl.BlockSpec(memory_space=pl.ANY)
            if kind == "all":
                return pl.BlockSpec(shape, lambda slot: (0,) * len(shape))
            return pl.BlockSpec((1,) + shape[1:], lambda slot: (slot, 0, 0))

        shapes = [
            self.whole if kind == "rows" else (self.slots, kind, self.width) for kind, _ in outs
        ]
        return pl.pallas_call(
            kernel,
            grid=(self.slots,),
            in_specs=[spec(kind, array.shape) for kind, array in ins],
            out_specs=[spec(kind, shape) for (kind, _), shape in zip(outs, shapes)],
            out_shape=[jax.ShapeDtypeStruct(shape, kind[1]) for kind, shape in zip(outs, shapes)],
            scratch_shapes=list(scratch),
            compiler_params=pltpu.CompilerParams(vmem_limit_bytes=56 << 20),
        )(*[array for _, array in ins])

    def middle(self, attended, output_full, output_bias, modulation):
        return self.per_image(
            middle_kernel,
            [("rows", jnp.float32), ("rows", jnp.bfloat16)],
            [
                ("rows", attended),
                ("all", output_full),
                ("all", output_bias),
                ("rows", self.hidden),
                ("mod", modulation),
            ],
        )

    def expand(self, normed_two, unit, biases, index):
        bias = lax.dynamic_index_in_dim(biases, index, 0, keepdims=False)
        inner = times(normed_two, unit) + bias
        return inner, low(gelu(inner))

    def shrink(self, inner, active, shrink_slope, expand_unit, unit, *totals):
        active_slope = times_transposed(shrink_slope, unit)
        inner_slope = low(jax.vjp(gelu, inner)[1](active_slope)[0])
        out = times(active, unit)
        back = times_transposed(inner_slope, expand_unit)
        if totals:
            out, back = out + totals[0], back + totals[1]
        ones = jnp.ones((8, self.rows), jnp.bfloat16)
        return inner_slope, times(ones, inner_slope), out, back

    def finish(self, branch, out, back, shrink_bias, modulation):
        layer_out, *others = self.per_image(
            finish_kernel,
            [
                ("rows", jnp.bfloat16),
                ("rows", jnp.float32),
                ("rows", jnp.bfloat16),
                (6, jnp.float32),
            ],
            [
                ("scalar", self.live),
                ("rows", self.hidden),
                ("rows", branch),
                ("rows", out),
                ("rows", back),
                ("rows", self.flat(self.cotangent)),
                ("all", shrink_bias),
                ("mod", modulation),
            ],
        )
        return layer_out.reshape(self.hidden_in.shape), *others

    def attention_back(self, slopes, queries, keys_all, values_all, logs):
        return attend_back(queries, keys_all, values_all, slopes, self.patch_mask, logs)

    def start_back(self, slopes, units, order, middle_slope, modulation):
        vmem = pl.BlockSpec(memory_space=pltpu.VMEM)
        gradient, first_slopes = pl.pallas_call(
            start_back_kernel,
            in_specs=[pl.BlockSpec(memory_space=pltpu.SMEM)]
            + [vmem] * 6
            + [pl.BlockSpec(memory_space=pl.ANY)] * 4,
            out_specs=[vmem] * 2,
            out_shape=[
                jax.ShapeDtypeStruct(self.whole, jnp.float32),
                jax.ShapeDtypeStruct((self.slots, 2, self.width), jnp.float32),
            ],
            scratch_shapes=[
                pltpu.VMEM((4, self.width, self.width), jnp.bfloat16),
                pltpu.SemaphoreType.DMA((4,)),
            ],
            compiler_params=pltpu.CompilerParams(vmem_limit_bytes=48 << 20),
        )(jnp.stack(order).astype(jnp.int32), *slopes, middle_slope, self.hidden, modulation, *units)
        return gradient.reshape(self.hidden_in.shape), first_slopes

    def condition_back(self, slope):
        return jax.vjp(jax.nn.silu, self.condition.astype(jnp.float32))[1](slope)[0]


def act_rows(conditions, here, shard):
    rows = lax.dynamic_slice_in_dim(conditions, here * shard, shard, 1)
    return low(jax.nn.silu(rows.astype(jnp.float32)))


def unpack_kernel(parts, packed_ref, mod_ref, attend_ref, output_ref, expand_ref, shrink_ref):
    shard = output_ref.shape[1] // parts
    start = packed_ref.shape[1] - 14 * shard

    def joined(first, size):
        cut = [
            packed_ref[part : part + 1, start + first : start + first + size].astype(jnp.float32)
            for part in range(parts)
        ]
        return jnp.concatenate(cut, axis=1)

    mod_ref[...] = joined(0, 6 * shard)
    for row in range(2):
        attend_ref[row : row + 1] = joined((6 + row) * shard, shard)
    output_ref[...] = joined(8 * shard, shard)
    for unit in range(4):
        expand_ref[unit : unit + 1] = joined((9 + unit) * shard, shard)
    shrink_ref[...] = joined(13 * shard, shard)


def unpack(packed, shard):
    parts = packed.shape[0]
    width = parts * shard
    return pl.pallas_call(
        partial(unpack_kernel, parts),
        out_shape=[
            jax.ShapeDtypeStruct((rows, columns), jnp.float32)
            for rows, columns in ((1, 6 * width), (2, width), (1, width), (4, width), (1, width))
        ],
    )(packed)


def pack_slopes_kernel(order_ref, first_ref, later_ref, head_ref, condition_ref, *refs):
    units, out_ref, held_ref = refs[:4], refs[4], refs[5]
    for index, unit in enumerate(units):
        held_ref[pl.ds(order_ref[index], 1), :] = unit[0:1, :]
    slots, width = condition_ref.shape
    sums = [head_ref[0, i : i + 1] + head_ref[1, i : i + 1] for i in range(2)]
    sums += [later_ref[0, i : i + 1] + later_ref[1, i : i + 1] for i in (4, 5)]
    for slot in range(slots):
        parts = [first_ref[slot, i : i + 1] for i in range(2)]
        parts += [later_ref[slot, i : i + 1] for i in range(4)]
        parts += [condition_ref[slot : slot + 1, :].astype(jnp.float32)]
        parts += sums if slot == 0 else [held_ref[i : i + 1, :] for i in range(4)]
        out_ref[slot : slot + 1, :] = low(jnp.concatenate(parts, axis=1))


def pack_slopes(order, first, later, heads, condition, units):
    slots, width = condition.shape
    vmem = pl.BlockSpec(memory_space=pltpu.VMEM)
    return pl.pallas_call(
        pack_slopes_kernel,
        in_specs=[pl.BlockSpec(memory_space=pltpu.SMEM)] + [vmem] * 8,
        out_specs=vmem,
        out_shape=jax.ShapeDtypeStruct((slots, 11 * width), jnp.bfloat16),
        scratch_shapes=[pltpu.VMEM((4, width), jnp.float32)],
    )(jnp.stack(order).astype(jnp.int32), first, later, heads, condition, *units)


def pack(condition, *biases):
    row = jnp.concatenate([condition.reshape(-1)] + [bias.reshape(-1) for bias in biases])
    return row[None]


def modulation_tail(modulation_slopes, conditions, here, shard, bias_size):
    weight = inner_rows(act_rows(conditions, here, shard), modulation_slopes)
    bias = lax.dynamic_slice_in_dim(modulation_slopes, here * bias_size, bias_size, 1)
    return weight, column_sums(bias)


def bias_tail(sums, here, shard):
    mine = lax.dynamic_slice_in_dim(sums, here * shard, shard, 1)
    return mine[0:2], mine[2], mine[4:8].reshape(-1), mine[3]


def condition_columns(gathered, image, slots):
    mine = lax.dynamic_slice_in_dim(gathered, image, slots, 1)
    return mine.transpose(1, 0, 2).reshape(slots, -1)


def plain_device(
    dp,
    rep,
    hidden_in,
    condition,
    patch_mask,
    image_counts,
    modulation_weight,
    modulation_bias,
    attend_weight,
    attend_bias,
    output_weight,
    output_bias,
    expand_weight,
    expand_bias,
    shrink_weight,
    shrink_bias,
    cotangent,
):
    here = lax.axis_index("dp")
    layer = Layer(hidden_in, condition, patch_mask, image_counts, cotangent)
    shard, width, slots = modulation_weight.shape[0], layer.width, layer.slots

    def whole(block):
        return lax.all_gather(block, "dp", axis=0, tiled=True)

    def summed(term):
        return lax.psum(
            lax.psum_scatter(term, "dp", scatter_dimension=0, tiled=True), "rep"
        ).astype(jnp.float32)

    packed = pack(
        condition, modulation_bias, attend_bias, output_bias, expand_bias, shrink_bias
    )
    packed = lax.all_gather(packed, "dp", axis=0, tiled=True)
    conditions = packed[:, : condition.size].reshape(-1, width)
    biases = unpack(packed, shard)
    expand_biases = biases[3].reshape(4, dp, shard).transpose(1, 0, 2).reshape(4, width)
    terms = times(act_rows(conditions, here, shard), modulation_weight)
    terms = lax.psum_scatter(terms, "dp", scatter_dimension=0, tiled=True)
    weights = whole(jnp.concatenate([attend_weight, output_weight], 1))
    weights = [weights[:, unit * width : (unit + 1) * width] for unit in range(4)]
    natural = [jnp.int32(unit) for unit in range(4)]
    expand_full, shrink_full = whole(expand_weight), whole(shrink_weight)
    begun = layer.begin(natural, terms, biases[0], biases[1], *weights)
    normed_one, shrink_slope, modulation, queries, keys_all, values_all, output_full = begun
    attended, logs = layer.attention(queries, keys_all, values_all)
    branch, normed_two = layer.middle(attended, output_full, biases[2], modulation)
    totals = ()
    expand_terms, shrink_terms, inner_sums = [], [], []
    for unit in range(4):
        cut = slice(unit * width, (unit + 1) * width)
        inner, active = layer.expand(normed_two, expand_full[:, cut], expand_biases, unit)
        inner_slope, inner_sum, *totals = layer.shrink(
            inner, active, shrink_slope, expand_full[:, cut], shrink_full[cut], *totals
        )
        expand_terms.append(low(inner_rows(normed_two, inner_slope)))
        shrink_terms.append(low(inner_rows(active, shrink_slope)))
        inner_sums.append(inner_sum[:1])
    layer_out, middle_slope, branch_low, later = layer.finish(
        branch, *totals, biases[4], modulation
    )
    attended_slope = low(times_transposed(branch_low, output_full))
    *slopes, head_sums = layer.attention_back(
        attended_slope, queries, keys_all, values_all, logs
    )
    gradient_hidden, first = layer.start_back(
        slopes, weights, natural, middle_slope, modulation
    )
    mod_slope = low(jnp.concatenate([first, later[:, :4]], 1)).reshape(slots, -1)
    all_slopes = lax.all_gather(mod_slope, ("dp", "rep"), axis=0, tiled=True)
    all_conditions = lax.all_gather(condition, ("dp", "rep"), axis=0, tiled=True)
    mod_weight, mod_bias = modulation_tail(
        all_slopes, all_conditions, here, shard, modulation_bias.shape[0]
    )
    columns = lax.all_gather(times_transposed(all_slopes, modulation_weight), "dp")
    inner_sums = jnp.concatenate(inner_sums, 1).reshape(dp, 4, shard)
    inner_sums = inner_sums.transpose(1, 0, 2).reshape(4, width)
    sums = jnp.concatenate([jnp.sum(head_sums, 0), jnp.sum(later[:, 4:], 0), inner_sums])
    sums = lax.psum(sums, ("dp", "rep"))
    att_bias, out_bias, exp_bias, shr_bias = bias_tail(sums, here, shard)
    return (
        layer_out,
        gradient_hidden,
        layer.condition_back(condition_columns(columns, (here * rep + lax.axis_index("rep")) * slots, slots)),
        mod_weight,
        mod_bias,
        summed(low(inner_rows(normed_one, jnp.concatenate(slopes, 1)))),
        att_bias,
        summed(low(inner_rows(attended, branch_low))),
        out_bias,
        summed(jnp.concatenate(expand_terms, 1)),
        exp_bias,
        summed(jnp.concatenate(shrink_terms)),
        shr_bias,
    )


class Ticks:
    def __init__(self):
        self.ops = []

    def at(self, tick, outs, ins, call):
        outs, ins = [(names,) if isinstance(names, str) else names for names in (outs, ins)]
        self.ops.append((tick, len(self.ops), outs, ins, call))

    def run(self, results):
        ops = sorted(self.ops, key=lambda op: op[:2])
        last = {}
        for tick, _, _, ins, _ in ops:
            for name in ins:
                last[name] = tick
        state = {}
        for position, (tick, _, outs, ins, call) in enumerate(ops):
            values = call(*[state[name] for name in ins])
            if len(outs) == 1:
                values = (values,)
            state.update(zip(outs, values))
            ends = position + 1 == len(ops) or ops[position + 1][0] > tick
            if ends:
                names = sorted(
                    name for name in state if last.get(name, -1) > tick or name in results
                )
                state = dict(zip(names, lax.optimization_barrier(tuple(state[n] for n in names))))
        return [state[name] for name in results]


class Names:
    def __getattr__(self, name):
        return name


def ticked_device(
    dp,
    rep,
    hidden_in,
    condition,
    patch_mask,
    image_counts,
    modulation_weight,
    modulation_bias,
    attend_weight,
    attend_bias,
    output_weight,
    output_bias,
    expand_weight,
    expand_bias,
    shrink_weight,
    shrink_bias,
    cotangent,
):
    n = Names()
    here = lax.axis_index(n.dp)
    copy = lax.axis_index(n.rep)
    depth = dp // 2
    z, x, y, core = here // 2, here % 2, copy // 2, copy % 2
    order = [(2 * core + y) ^ step for step in range(4)]
    layer = Layer(hidden_in, condition, patch_mask, image_counts, cotangent)
    shard, width, slots = modulation_weight.shape[0], layer.width, layer.slots
    ticks = Ticks()
    at = ticks.at

    def up(value):
        return lax.ppermute(value, n.dp, [(i, (i + 2) % dp) for i in range(dp)])

    def jump(step, value):
        return lax.ppermute(value, n.dp, [(i, (i + 2 * step) % dp) for i in range(dp)])

    def swap_x(value):
        return lax.ppermute(value, n.dp, [(i, i ^ 1) for i in range(dp)])

    def swap_y(value):
        return lax.ppermute(value, n.rep, [(i, i ^ 2) for i in range(4)])

    def swap_core(value):
        return lax.ppermute(value, n.rep, [(i, i ^ 1) for i in range(4)])

    def pair(one, two):
        return jnp.concatenate([one, two])

    def below(step):
        return (z - step) % depth

    def add(one, two):
        return low(one.astype(jnp.float32) + two.astype(jnp.float32))

    def attend_block(index):
        column = jnp.minimum(index, 2) * width
        block = lax.dynamic_slice_in_dim(attend_weight, column, width, 1)
        return jnp.where(index == 3, output_weight, block)[None]

    def shrink_block(index):
        return lax.dynamic_slice_in_dim(shrink_weight, index * shard, shard, 0)[None]

    def pick(stacked, index):
        return lax.dynamic_slice_in_dim(stacked, index, 1, 0)

    at(0, n.A0, (), lambda: attend_block(order[0]))
    at(0, n.a0, (), lambda: attend_block(order[1]))
    at(0, n.Bs, (), lambda: regroup(expand_weight, dp))
    at(0, n.P0, n.Bs, lambda s: pick(s, order[1]))
    at(0, n.C0, (), lambda: shrink_block(order[0]))
    at(0, n.c0, (), lambda: shrink_block(order[1]))

    at(0, n.AB0, (n.A0, n.Bs), lambda p, q: pair(p, pick(q, order[0])))
    for name, ring_ticks, x_ticks in (
        (n.AB, (0, 1, 2), (0, 1, 2, 3)),
        (n.P, (3, 4, 5), (4, 5)),
        (n.C, (3, 6, 7), (6, 7, 7, 8)),
    ):
        for step, tick in enumerate(ring_ticks):
            at(tick, (str(name) + str(step + 1)), (str(name) + str(step)), up)
        for step, tick in enumerate(x_ticks):
            at(tick, (str(name) + n.x + str(step)), (str(name) + str(step)), swap_x)
    for step in range(3):
        at(step + 1, (n.ABy + str(step)), ((n.ABx + str(step)), (n.AB + str(step + 1))),
           lambda p, q: swap_y(pair_rows(p, 0, q, 0)))
    at(4, n.ABy3, n.ABx3, lambda p: swap_y(p[:1]))
    at(6, n.Px23, (n.P2, n.P3), lambda p, q: swap_x(pair(p, q)))
    at(6, n.C1y, n.C1, swap_y)
    for tick, one, two in ((7, n.Cx0, n.C2), (8, n.Cx1, n.C3), (9, n.Cx2, n.Cx3)):
        at(tick, one + two, (one, two), lambda p, q: swap_y(pair(p, q)))

    def spot(step, cross):
        return 2 * below(step) + (1 - x if cross else x)

    def unit(blocks):
        parts = [(array, row) for array, row, _, _ in blocks]
        places = [spot(step, cross) for _, _, step, cross in blocks]
        return assemble(parts, places, dp).reshape(dp * shard, width)

    def streamed(zs, xs):
        return unit(
            [(array, row, step, False) for step, (array, row) in enumerate(zs)]
            + [(array, row, step, True) for step, (array, row) in enumerate(xs)]
        )

    def own_unit(row, *parts):
        return streamed([(part, row) for part in parts[:4]], [(part, row) for part in parts[4:]])

    def other_unit(local, *parts):
        return streamed(
            [(local, 0)] + [(part, 1) for part in parts[:3]], [(part, 0) for part in parts]
        )

    def other_late(local, one, two, three, four):
        return streamed(
            [(local, 0), (one, 0), (two, 1), (three, 1)], [(two, 0), (three, 0), (four, 0), (four, 1)]
        )

    def pair_unit(*parts):
        return streamed(
            [(part, 0) for part in parts[:4]], [(parts[4], 0), (parts[5], 0), (parts[6], 0), (parts[6], 1)]
        )

    for name, stream, row, tick in (
        (n.Aown, n.AB, 0, 4), (n.Bown, n.AB, 1, 5)
    ):
        parts = tuple((str(stream) + str(step)) for step in range(4))
        parts += tuple((str(stream) + n.x + str(step)) for step in range(4))
        at(tick, name, parts, partial(own_unit, row))
    at(5, n.Ay, (n.a0,) + tuple((n.ABy + str(step)) for step in range(4)), other_unit)
    at(7, n.By, (n.P0, n.P1, n.P2, n.P3, n.Px0, n.Px1, n.Px23), pair_unit)
    at(10, n.Cy, (n.c0, n.C1y, n.Cx0C2, n.Cx1C3, n.Cx2Cx3), other_late)
    at(5, n.Ac, n.Aown, swap_core)
    at(5, n.Acy, n.Ay, swap_core)
    at(6, n.Bc, n.Bown, swap_core)
    at(7, n.Bcy, n.By, swap_core)
    at(10, n.Ccy, n.Cy, swap_core)

    def swap_z(distance, value):
        return lax.ppermute(value, n.dp, [(i, i ^ (2 * distance)) for i in range(dp)])

    bits = {
        n.core: (core, swap_core),
        n.y: (y, swap_y),
        n.x: (x, swap_x),
        n.near: (z % 2, partial(swap_z, 1)),
        n.far: (z // 2, partial(swap_z, 2)),
    }

    def grow(tick, name, axes):
        for axis in axes:
            bit, swap = bits[axis]

            def join(mine, other, bit=bit):
                return jnp.where(bit == 0, pair(mine, other), pair(other, mine))

            at(tick, name + n._in, name, swap)
            at(tick, name + "+", (name, name + n._in), join)
            name += "+"
        return name

    def shrink_terms(tick, name, axes):
        for axis in axes:
            bit, swap = bits[axis]

            def send(terms, bit=bit, swap=swap):
                half = terms.shape[0] // 2
                return swap(lax.dynamic_slice_in_dim(terms, (1 - bit) * half, half, 0))

            def keep(terms, other, bit=bit):
                half = terms.shape[0] // 2
                return lax.dynamic_slice_in_dim(terms, bit * half, half, 0) + other

            at(tick, name + n._in, name, send)
            at(tick, name + "-", (name, name + n._in), keep)
            name += "-"
        return name

    at(0, n.small, (), lambda: pack(
        condition, modulation_bias, attend_bias, output_bias, expand_bias, shrink_bias))
    small = grow(0, n.small, (n.x,))
    small = grow(1, small, (n.near,))
    small = grow(2, small, (n.far,))
    at(3, (n.mod_bias, n.att_bias, n.out_bias, n.exp_bias, n.shr_bias), small,
       lambda packed: unpack(packed, shard))

    def first_terms(packed):
        conditions = packed[:, : condition.size].reshape(2, 2, 2, slots, width)
        conditions = conditions.transpose(2, 1, 0, 3, 4).reshape(-1, width)
        return times(act_rows(conditions, here, shard), modulation_weight)

    at(2, n.terms, small, first_terms)
    terms = shrink_terms(3, n.terms, (n.x,))
    terms = shrink_terms(4, terms, (n.near,))
    terms = shrink_terms(5, terms, (n.far,))

    units_a = (n.Aown, n.Ay, n.Ac, n.Acy)
    at(6, (n.n1, n.gm, n.mod, n.q, n.k, n.v, n.O), (terms, n.mod_bias, n.att_bias) + units_a,
       partial(layer.begin, order))
    at(6, (n.att, n.logs), (n.q, n.k, n.v), layer.attention)
    at(7, (n.branch, n.n2), (n.att, n.O, n.out_bias, n.mod), layer.middle)

    def expand(index, n2, weight, biases):
        return layer.expand(n2, weight, biases, order[index])

    def term(left, right, *received):
        total = inner_rows(left, right)
        for value in received:
            total = total + value.astype(jnp.float32)
        return low(total)

    for index, (name, tick) in enumerate(((n.own, 8), (n.y, 8), (n.c, 7), (n.cy, 8))):
        at(tick, ((n.in_ + str(name)), (n.act_ + str(name))), (n.n2, (n.B + str(name)), n.exp_bias), partial(expand, index))
    at(7, n.dC_c, (n.act_c, n.gm), term)
    at(8, n.dC_cy, (n.act_cy, n.gm), term)
    at(9, n.dC_own, (n.act_own, n.gm, n.dC_rc), term)
    at(11, n.dC_y, (n.act_y, n.gm, n.dC_rcy), term)

    at(9, n.Cown, (n.C0, n.C1, n.C2, n.C3, n.Cx0, n.Cx1, n.Cx2, n.Cx3, n.dC_own),
       lambda *parts: own_unit(0, *lax.optimization_barrier(parts)[:8]))
    at(9, n.Cc, n.Cown, swap_core)
    total = ()
    for index, (name, tick) in enumerate(((n.own, 9), (n.c, 10), (n.cy, 11), (n.y, 12))):
        ins = ((n.in_ + str(name)), (n.act_ + str(name)), n.gm, (n.B + str(name)), (n.C + str(name))) + total
        total = ((n.out + str(index)), (n.back + str(index)))
        at(tick, ((n.gi_ + str(name)), (n.sum_ + str(name))) + total, ins, layer.shrink)
    at(10, n.dB_c, (n.n2, n.gi_c), term)
    at(11, n.dB_cy, (n.n2, n.gi_cy), term)
    at(12, n.dB_own, (n.n2, n.gi_own, n.dB_rc), term)
    at(13, n.dB_y, (n.n2, n.gi_y, n.dB_rcy), term)

    at(13, (n.layer_out, n.middle_slope, n.branch_low, n.later),
       (n.branch, n.out3, n.back3, n.shr_bias, n.mod), layer.finish)
    at(13, n.g_att, (n.branch_low, n.O), lambda b, w: low(times_transposed(b, w)))
    at(14, (n.gq, n.gk, n.gv, n.head_sums), (n.g_att, n.q, n.k, n.v, n.logs), layer.attention_back)
    def attend_term(index, n1, att, gq, gk, gv, branch_low, *received):
        which = order[index]
        right = lax.select_n(which, gq, gk, gv, branch_low)
        return term(jnp.where(which == 3, att, n1), right, *received)

    for index, (name, tick, received) in enumerate(
        ((n.own, 15, ()), (n.y, 15, ()), (n.c, 14, ()), (n.cy, 14, ()))
    ):
        ins = (n.n1, n.att, n.gq, n.gk, n.gv, n.branch_low) + received
        at(tick, (n.dA_ + str(name)), ins, partial(attend_term, index))

    at(16, (n.gradient_hidden, n.first), (n.gq, n.gk, n.gv, n.middle_slope, n.mod) + units_a,
       lambda a, b, c, ms, mod, *units: layer.start_back((a, b, c), units, order, ms, mod))


    def slab(step, moved, count, *values):
        first = below(step) * (2 * shard)
        cuts = [lax.dynamic_slice_in_dim(value, first, 2 * shard, 0) for value in values[:count]]
        cuts += values[count:]
        if len(cuts) == 1:
            return moved(cuts[0])
        return moved(low(sum(value.astype(jnp.float32) for value in cuts)))

    def stay(value):
        return value

    def along_ring(name, start, source, added, rest=0):
        for step in range(1, 5):
            ins = source + tuple((str(part) + str(step)) for part in added)
            if step > 1:
                ins += ((str(name) + str(step - 1)),)
            at(start + step - 1, (str(name) + str(step)), ins, partial(slab, step, up if step < 4 else stay, len(source)))
        at(start + 3 + rest, (str(name) + n._in), (str(name) + str(4)), lambda total: swap_x(
            lax.dynamic_slice_in_dim(total, (1 - x) * shard, shard, 0)))
        at(start + 4 + rest, (str(name) + n._sum), ((str(name) + str(4)), (str(name) + n._in)), lambda total, other: low(
            lax.dynamic_slice_in_dim(total, x * shard, shard, 0).astype(jnp.float32)
            + other.astype(jnp.float32)))
        return (str(name) + n._sum)

    def wide(name, start_own, start_other, late):
        one = along_ring((str(name) + n._o), start_own, ((str(name) + n._own),), ())
        two = along_ring((str(name) + n._p), start_other, ((str(name) + n._y),), ())
        at(late, (str(name) + n._yo), two, swap_y)
        at(late, (str(name) + n._yp), one, swap_y)
        at(late + 1, (str(name) + n._0), (one, (str(name) + n._yo)), add)
        at(late + 1, (str(name) + n._1), (two, (str(name) + n._yp)), add)
        at(late + 1, (str(name) + n._2), (str(name) + n._0), swap_core)
        at(late + 1, (str(name) + n._3), (str(name) + n._1), swap_core)
        return late + 2

    def halved(name, cut_ticks, y_ticks, start_ring, late, received=(), rest=0):
        for step, tick in enumerate(y_ticks, 1):
            ins = ((str(name) + n._y),) + tuple((str(name) + n._ + str(part) + n.y) for part in received)
            at(cut_ticks[step - 1], (str(name) + n._t + str(step)), ins, partial(slab, step, stay, len(ins)))
            at(tick, (str(name) + n._s + str(step)), (str(name) + n._t + str(step)), swap_y)
        own = ((str(name) + n._own),) + tuple((str(name) + n._ + str(part)) for part in received)
        one = along_ring((str(name) + n._o), start_ring, own, ((str(name) + n._s),), rest)
        at(late, (str(name) + n._0), one, stay)
        at(late, (str(name) + n._1), one, swap_y)
        at(late + 1, (str(name) + n._2), one, swap_core)
        at(late + 1, (str(name) + n._3), (str(name) + n._1), swap_core)
        return late + 2

    for name, tick_one, tick_two in ((n.dC, 8, 9), (n.dB, 11, 12), (n.dA, 15, 15)):
        at(tick_one, (str(name) + n._rc), (str(name) + n._c), swap_core)
        at(tick_two, (str(name) + n._rcy), (str(name) + n._cy), swap_core)
    end_c = wide(n.dC, 9, 12, 20)
    end_b = halved(n.dB, (13, 14, 14, 15), (13, 14, 14, 15), 14, 19, rest=1)
    end_a = halved(n.dA, (16, 17, 18, 19), (16, 17, 18, 19), 17, 21, (n.rc,))

    def four(name):
        return tuple((str(name) + n._ + str(i)) for i in range(4))

    at(end_c, n.shr_weight, four(n.dC), lambda *units: shrink_out(units, order))
    at(end_b, n.exp_weight, four(n.dB), lambda *units: spread(units, order, dp))
    at(end_a, (n.att_weight, n.out_weight), four(n.dA), lambda *units: attend_out(units, order))

    def join(tick, name, axis):
        at(tick, name + n._in, name, bits[axis][1])
        at(tick, name + "+", (name, name + n._in), pair)
        return name + "+"

    mod_size = 6 * width
    at(16, n.sent, (n.first, n.later, n.head_sums, n.sum_own, n.sum_y, n.sum_c, n.sum_cy),
       lambda first, later, heads, *units: pack_slopes(
           order, first, later, heads, condition, units))
    sent = n.sent
    both_ways = [(4 * i + j, 4 * (i ^ 4) + (j ^ 2)) for i in range(dp) for j in range(4)]
    at(17, n.sent_far, sent, partial(swap_z, 2))
    at(17, n.sent_y, sent, swap_y)
    at(17, n.sent_both, sent, lambda rows: lax.ppermute(rows, (n.dp, n.rep), both_ways))
    at(17, n.rows, (sent, n.sent_far, n.sent_y, n.sent_both), lambda *rows: jnp.concatenate(rows))
    sent = n.rows
    for tick, axis in ((18, n.near), (19, n.x), (20, n.core)):
        sent = join(tick, sent, axis)

    def modulation_terms(sent):
        slopes = sent[:, :mod_size]
        weight, bias = modulation_tail(
            slopes, sent[:, mod_size : mod_size + width], here, shard, modulation_bias.shape[0]
        )
        row = lax.broadcasted_iota(jnp.int32, (slots, sent.shape[0]), 1)
        picked = low(row % slots == lax.broadcasted_iota(jnp.int32, row.shape, 0))
        sums = times(picked, sent[:, mod_size + width :]).reshape(-1, width)
        return (weight, bias) + bias_tail(sums, here, shard)

    at(20, n.columns, sent, lambda sent: times_transposed(sent[:, :mod_size], modulation_weight))
    at(20, (n.mod_weight, n.mod_bias_out, n.att_bias_out, n.out_bias_out, n.exp_bias_out, n.shr_bias_out),
       sent, modulation_terms)

    at(20, n.traded, n.columns, lambda columns: columns.reshape(
        2, 2, 2, 2, 2, slots, shard)[0, :, :, 0])
    at(20, n.traded_x, n.traded, lambda held: swap_x(held[1]))
    at(21, n.held, (n.traded, n.traded_x), lambda held, got: jnp.stack([held[0], got]))
    for step in (1, 2, 3):
        at(21, (n.held + str(step)), n.held, lambda held, step=step: swap_z(step, held[:, step % 2, step // 2]))

    def condition_slope(held, near, far, both):
        held = jnp.stack([held[:, 0, 0], far, near, both]).reshape(2, 2, 2, slots, shard)
        for axis, bit in enumerate((z % 2, z // 2, x)):
            held = jnp.where(bit == 1, jnp.flip(held, axis), held)
        held = held.transpose(3, 1, 0, 2, 4)
        return layer.condition_back(held.reshape(slots, width))

    at(22, n.gradient_condition, (n.held, n.held1, n.held2, n.held3), condition_slope)
    return tuple(
        ticks.run(
            [
                n.layer_out,
                n.gradient_hidden,
                n.gradient_condition,
                n.mod_weight,
                n.mod_bias_out,
                n.att_weight,
                n.att_bias_out,
                n.out_weight,
                n.out_bias_out,
                n.exp_weight,
                n.exp_bias_out,
                n.shr_weight,
                n.shr_bias_out,
            ]
        )
    )


def solution(mesh):
    dp, rep = mesh.shape["dp"], mesh.shape["rep"]
    device = ticked_device if (dp, rep) == (8, 4) else plain_device
    return jax.shard_map(
        partial(device, dp, rep),
        mesh=mesh,
        in_specs=(
            P(("dp", "rep"), None, None),
            P(("dp", "rep"), None),
            P(("dp", "rep"), None),
            P(("dp", "rep")),
            P("dp", None),
            P("dp"),
            P("dp", None),
            P(None, "dp"),
            P("dp", None),
            P("dp"),
            P("dp", None),
            P("dp"),
            P("dp", None),
            P("dp"),
            P(("dp", "rep"), None, None),
        ),
        out_specs=(
            P(("dp", "rep"), None, None),
            P(("dp", "rep"), None, None),
            P(("dp", "rep"), None),
            P("dp", None),
            P("dp"),
            P("dp", None),
            P(None, "dp"),
            P("dp", None),
            P("dp"),
            P("dp", None),
            P("dp"),
            P("dp", None),
            P("dp"),
        ),
        check_vma=False,
    )
```

```python
import math
from functools import partial

import jax
import jax.numpy as jnp
from jax import lax
from jax.experimental import pallas as pl
from jax.experimental.pallas import tpu as pltpu
from jax.sharding import PartitionSpec as P

HEADS = 16


epsilon = 1e-06
masked_score = -1e30


def gelu(values):
    return jax.nn.gelu(values, approximate=True)


def low(values):
    return values.astype(jnp.bfloat16)


def inner_rows(left_side, right_side):
    return lax.dot_general(
        left_side, right_side, (((0,), (0,)), ((), ())), preferred_element_type=jnp.float32
    )


def times(left_side, right_side):
    return jnp.dot(left_side, right_side, preferred_element_type=jnp.float32)


def times_transposed(left_side, right_side):
    return lax.dot_general(
        left_side, right_side, (((1,), (1,)), ((), ())), preferred_element_type=jnp.float32
    )


def column_sums(values):
    return jnp.sum(values, 0, dtype=jnp.float32)


def head_window(head, head_dim, model_width):
    first = head * head_dim
    last = first + head_dim
    start = first // 128 * 128
    stop = min(-(-last // 128) * 128, model_width)
    lane = lax.broadcasted_iota(jnp.int32, (1, stop - start), 1) + start
    return slice(start, stop), (lane >= first) & (lane < last)


def only(inside, values):
    return jnp.where(inside, values, jnp.zeros_like(values))


def head_order(heads):
    half = heads // 2
    return [head + shift for head in range(half) for shift in (0, half)]


def head_scores(query, key_window, valid, score_scale):
    scores = times_transposed(query, key_window) * score_scale
    return jnp.where(valid, scores, masked_score)


def attend_kernel(heads, query_ref, key_ref, value_ref, mask_ref, out_ref, log_ref, total_ref):
    patch_count, model_width = query_ref.shape
    head_dim = model_width // heads
    valid = mask_ref[0] > 0
    total_ref[...] = jnp.zeros_like(total_ref)
    for head in head_order(heads):
        cut, inside = head_window(head, head_dim, model_width)
        query = only(inside, query_ref[:, cut])
        scores = head_scores(query, key_ref[:, cut], valid, head_dim ** (-0.5))
        peak = jnp.max(scores, -1, keepdims=True)
        exponent = jnp.exp(scores - peak)
        row_total = jnp.sum(exponent, -1, keepdims=True)
        log_ref[:, head : head + 1] = peak + jnp.log(row_total)
        probs = low(exponent * (1.0 / row_total))
        total_ref[:, cut] += times(probs, only(inside, value_ref[:, cut]))
    out_ref[...] = low(total_ref[...])


def attend(queries, keys_all, values_all, patch_mask):
    slot_count, patch_count = patch_mask.shape
    model_width = queries.shape[1]
    block = pl.BlockSpec((patch_count, model_width), lambda slot: (slot, 0))
    return pl.pallas_call(
        partial(attend_kernel, HEADS),
        grid=(slot_count,),
        out_shape=[
            jax.ShapeDtypeStruct(queries.shape, jnp.bfloat16),
            jax.ShapeDtypeStruct((queries.shape[0], HEADS), jnp.float32),
        ],
        in_specs=[block] * 3 + [pl.BlockSpec((1, 1, patch_count), lambda slot: (slot, 0, 0))],
        out_specs=[block, pl.BlockSpec((patch_count, HEADS), lambda slot: (slot, 0))],
        scratch_shapes=[pltpu.VMEM((patch_count, model_width), jnp.float32)],
        compiler_params=pltpu.CompilerParams(vmem_limit_bytes=32 << 20),
    )(queries, keys_all, values_all, patch_mask[:, None, :])


def attend_back_kernel(
    heads,
    query_ref,
    key_ref,
    value_ref,
    slope_ref,
    mask_ref,
    log_ref,
    query_out,
    key_out,
    value_out,
    sums_out,
    query_total,
    key_total,
    value_total,
):
    patch_count, model_width = query_ref.shape
    head_dim = model_width // heads
    score_scale = head_dim ** (-0.5)
    valid = mask_ref[0] > 0
    for total in (query_total, key_total, value_total):
        total[...] = jnp.zeros_like(total)
    for head in head_order(heads):
        cut, inside = head_window(head, head_dim, model_width)
        query = only(inside, query_ref[:, cut])
        key = only(inside, key_ref[:, cut])
        slope = only(inside, slope_ref[:, cut])
        probs = jnp.exp(head_scores(query, key, valid, score_scale) - log_ref[:, head : head + 1])
        prob_slope = times_transposed(slope, value_ref[:, cut])
        row = jnp.sum(probs * prob_slope, -1, keepdims=True)
        score_slope = low(probs * (prob_slope - row))
        query_total[:, cut] += times(score_slope, key)
        key_total[:, cut] += inner_rows(score_slope, query)
        value_total[:, cut] += inner_rows(low(probs), slope)
    query_slope = low(query_total[...] * score_scale)
    query_out[...] = query_slope
    sums_out[0, 0:1] = jnp.sum(query_slope.astype(jnp.float32), 0, keepdims=True)
    key_out[...] = low(key_total[...] * score_scale)
    value_slope = low(value_total[...])
    value_out[...] = value_slope
    sums_out[0, 1:2] = jnp.sum(value_slope.astype(jnp.float32), 0, keepdims=True)


def attend_back(queries, keys_all, values_all, slopes, patch_mask, logs):
    slot_count, patch_count = patch_mask.shape
    model_width = queries.shape[1]
    block = pl.BlockSpec((patch_count, model_width), lambda slot: (slot, 0))
    return pl.pallas_call(
        partial(attend_back_kernel, HEADS),
        grid=(slot_count,),
        out_shape=[jax.ShapeDtypeStruct(queries.shape, jnp.bfloat16)] * 3
        + [jax.ShapeDtypeStruct((slot_count, 2, model_width), jnp.float32)],
        in_specs=[block] * 4
        + [
            pl.BlockSpec((1, 1, patch_count), lambda slot: (slot, 0, 0)),
            pl.BlockSpec((patch_count, HEADS), lambda slot: (slot, 0)),
        ],
        out_specs=[block] * 3 + [pl.BlockSpec((1, 2, model_width), lambda slot: (slot, 0, 0))],
        scratch_shapes=[pltpu.VMEM((patch_count, model_width), jnp.float32)] * 3,
        compiler_params=pltpu.CompilerParams(vmem_limit_bytes=32 << 20),
    )(queries, keys_all, values_all, slopes, patch_mask[:, None, :], logs)


def norm_parts(values):
    centered = values - jnp.mean(values, -1, keepdims=True)
    inverse = lax.rsqrt(jnp.mean(centered * centered, -1, keepdims=True) + epsilon)
    return centered * inverse, inverse


def norm_back(normed, inverse, slope):
    mean = jnp.mean(slope, -1, keepdims=True)
    return (slope - mean - normed * jnp.mean(slope * normed, -1, keepdims=True)) * inverse


def patch_sums(values):
    return jnp.sum(values, 0, keepdims=True)


def fetch(sources, held_ref, sems, places=None):
    copies = []
    for index, source in enumerate(sources):
        place = index if places is None else places[index]
        copies.append(pltpu.make_async_copy(source, held_ref.at[place], sems.at[index]))
    for copy in copies:
        copy.start()
    return copies


def begin_kernel(
    order_ref, live_ref, terms_ref, bias_ref, hidden_ref, cotangent_ref, attend_bias_ref, *refs
):
    units = refs[:4]
    normed_ref, slope_ref, mod_ref, query_ref, key_ref, value_ref = refs[4:10]
    last_ref, held, sems = refs[10:]
    copies = fetch(units, held, sems, order_ref)
    slots, _, width = mod_ref.shape
    patches = hidden_ref.shape[0] // slots
    for slot in range(slots):
        rows = slice(slot * patches, (slot + 1) * patches)
        modulation = terms_ref[slot : slot + 1, :] + bias_ref[...]
        cuts = [modulation[:, i * width : (i + 1) * width] for i in range(6)]
        for i in range(6):
            mod_ref[slot, i : i + 1] = cuts[i]
        normed = norm_parts(hidden_ref[rows, :].astype(jnp.float32))[0]
        normed_ref[rows, :] = low(normed * (1.0 + cuts[1]) + cuts[0])
        slope = cotangent_ref[rows, :].astype(jnp.float32) * live_ref[slot]
        slope_ref[rows, :] = low(slope * cuts[5])
    for copy in copies:
        copy.wait()
    copy = pltpu.make_async_copy(held.at[3], last_ref, sems.at[4])
    copy.start()
    query_ref[...] = low(times(normed_ref[...], held[0]) + attend_bias_ref[0:1, :])
    key_ref[...] = low(times(normed_ref[...], held[1]))
    value_ref[...] = low(times(normed_ref[...], held[2]) + attend_bias_ref[1:2, :])
    copy.wait()


def begin(order, live, terms, bias, hidden, cotangent, attend_bias, units):
    rows, width = hidden.shape
    vmem = pl.BlockSpec(memory_space=pltpu.VMEM)
    smem = pl.BlockSpec(memory_space=pltpu.SMEM)
    anywhere = pl.BlockSpec(memory_space=pl.ANY)
    whole = jax.ShapeDtypeStruct((rows, width), jnp.bfloat16)
    return pl.pallas_call(
        begin_kernel,
        in_specs=[smem, smem] + [vmem] * 5 + [anywhere] * 4,
        out_specs=[vmem] * 6 + [anywhere],
        out_shape=[whole, whole, jax.ShapeDtypeStruct((live.shape[0], 6, width), jnp.float32)]
        + [whole] * 3
        + [jax.ShapeDtypeStruct((width, width), jnp.bfloat16)],
        scratch_shapes=[
            pltpu.VMEM((4, width, width), jnp.bfloat16),
            pltpu.SemaphoreType.DMA((5,)),
        ],
        compiler_params=pltpu.CompilerParams(vmem_limit_bytes=40 << 20),
    )(jnp.stack(order).astype(jnp.int32), live, terms, bias, hidden, cotangent, attend_bias, *units)


def middle_kernel(attended_ref, weight_ref, bias_ref, hidden_ref, mod_ref, branch_ref, normed_ref):
    gate_one, shift_two, scale_two = [mod_ref[0, i : i + 1] for i in (2, 3, 4)]
    branch = times(attended_ref[...], weight_ref[...]) + bias_ref[...]
    branch_ref[...] = branch
    middle = hidden_ref[...].astype(jnp.float32) + gate_one * branch
    normed_ref[...] = low(norm_parts(middle)[0] * (1.0 + scale_two) + shift_two)


def finish_kernel(
    live_ref,
    hidden_ref,
    branch_ref,
    out_ref,
    back_ref,
    cotangent_ref,
    bias_ref,
    mod_ref,
    layer_ref,
    middle_slope_ref,
    branch_low_ref,
    slopes_ref,
):
    gate_one, shift_two, scale_two, gate_two = [mod_ref[0, i : i + 1] for i in (2, 3, 4, 5)]
    live = live_ref[pl.program_id(0)]
    branch = branch_ref[...]
    middle = hidden_ref[...].astype(jnp.float32) + gate_one * branch
    mlp_out = out_ref[...] + bias_ref[...]
    layer_ref[...] = low(live * (middle + gate_two * mlp_out))
    slope = cotangent_ref[...].astype(jnp.float32) * live
    slopes_ref[0, 3:4] = patch_sums(slope * mlp_out)
    normed, inverse = norm_parts(middle)
    back = back_ref[...]
    slopes_ref[0, 1:2] = patch_sums(back)
    slopes_ref[0, 2:3] = patch_sums(back * normed)
    middle_slope = slope + norm_back(normed, inverse, back * (1.0 + scale_two))
    middle_slope_ref[...] = middle_slope
    slopes_ref[0, 0:1] = patch_sums(middle_slope * branch)
    branch_low = low(middle_slope * gate_one)
    branch_low_ref[...] = branch_low
    slopes_ref[0, 4:5] = patch_sums(branch_low.astype(jnp.float32))
    slopes_ref[0, 5:6] = patch_sums(low(slope * gate_two).astype(jnp.float32))


def start_back_kernel(
    order_ref,
    query_ref,
    key_ref,
    value_ref,
    middle_slope_ref,
    hidden_ref,
    mod_ref,
    *refs,
):
    units, out_ref, slopes_ref, held, sems = refs[:4], *refs[4:]
    for copy in fetch(units, held, sems, order_ref):
        copy.wait()
    out_ref[...] = times_transposed(query_ref[...], held[0])
    out_ref[...] += times_transposed(key_ref[...], held[1])
    out_ref[...] += times_transposed(value_ref[...], held[2])
    slots = mod_ref.shape[0]
    patches = hidden_ref.shape[0] // slots
    for slot in range(slots):
        rows = slice(slot * patches, (slot + 1) * patches)
        normed, inverse = norm_parts(hidden_ref[rows, :].astype(jnp.float32))
        back = out_ref[rows, :]
        slopes_ref[slot, 0:1] = patch_sums(back)
        slopes_ref[slot, 1:2] = patch_sums(back * normed)
        scale_one = mod_ref[slot, 1:2]
        out_ref[rows, :] = middle_slope_ref[rows, :] + norm_back(
            normed, inverse, back * (1.0 + scale_one)
        )


def assemble_kernel(place_ref, *refs):
    blocks, whole_ref = refs[:-1], refs[-1]
    for index, block in enumerate(blocks):
        whole_ref[place_ref[index]] = block[0]


def assemble(blocks, places, count):
    shape = (count,) + blocks[0][0].shape[1:]

    def row_spec(row):
        return pl.BlockSpec((1,) + shape[1:], lambda step: (row, 0, 0))

    return pl.pallas_call(
        assemble_kernel,
        grid=(1,),
        in_specs=[pl.BlockSpec(memory_space=pltpu.SMEM)] + [row_spec(row) for _, row in blocks],
        out_specs=pl.BlockSpec(shape, lambda step: (0, 0, 0)),
        out_shape=jax.ShapeDtypeStruct(shape, blocks[0][0].dtype),
        compiler_params=pltpu.CompilerParams(vmem_limit_bytes=32 << 20),
        cost_estimate=pl.CostEstimate(
            flops=0, bytes_accessed=4 * count * shape[1] * shape[2], transcendentals=0
        ),
    )(jnp.stack(places).astype(jnp.int32), *[array for array, _ in blocks])


def rows_of(parts):
    if len(parts) == 1:
        return parts[0]
    row = lax.broadcasted_iota(jnp.int32, (2, 1, 1), 0)
    return jnp.where(row == 0, parts[0], parts[1])


def take(places, wholes, parts=()):
    count = len(places)
    total = 0.0
    for whole in wholes:
        cut = [lax.dynamic_slice_in_dim(whole, place, 1, 0) for place in places]
        total = total + rows_of(cut).astype(jnp.float32)
    for part, row in parts:
        total = total + part[row : row + count].astype(jnp.float32)
    return low(total)


def pair_rows(one, one_row, two, two_row):
    return rows_of([one[one_row : one_row + 1], two[two_row : two_row + 1]])


def reorder_kernel(place_ref, *refs):
    units, whole_ref = refs[:-1], refs[-1]
    for index, unit in enumerate(units):
        whole_ref[place_ref[index]] = unit[...]


def reorder(units, order, parts):
    rows, width = units[0].shape
    block = rows // parts
    return pl.pallas_call(
        reorder_kernel,
        grid=(parts,),
        in_specs=[pl.BlockSpec(memory_space=pltpu.SMEM)]
        + [pl.BlockSpec((block, width), lambda step: (step, 0))] * 4,
        out_specs=pl.BlockSpec((4, block, width), lambda step: (0, step, 0)),
        out_shape=jax.ShapeDtypeStruct((4, rows, width), units[0].dtype),
        compiler_params=pltpu.CompilerParams(vmem_limit_bytes=32 << 20),
        cost_estimate=pl.CostEstimate(
            flops=0, bytes_accessed=16 * rows * width, transcendentals=0
        ),
    )(jnp.stack(order).astype(jnp.int32), *units)


def regroup_kernel(parts, in_ref, out_ref):
    width = in_ref.shape[1] // (4 * parts)
    for unit in range(4):
        out_ref[unit] = jnp.concatenate(
            [
                in_ref[:, (4 * part + unit) * width : (4 * part + unit + 1) * width]
                for part in range(parts)
            ],
            axis=1,
        )


def regroup(columns, parts):
    rows, width = columns.shape
    return pl.pallas_call(
        partial(regroup_kernel, parts),
        out_shape=jax.ShapeDtypeStruct((4, rows, width // 4), columns.dtype),
        compiler_params=pltpu.CompilerParams(vmem_limit_bytes=32 << 20),
    )(columns)


def attend_out_kernel(order_ref, *refs):
    units, attend_ref, output_ref, held = refs[:4], refs[4], refs[5], refs[6]
    for index in range(4):
        held[order_ref[index]] = units[index][...]
    width = output_ref.shape[1]
    for unit in range(3):
        attend_ref[:, unit * width : (unit + 1) * width] = held[unit].astype(jnp.float32)
    output_ref[...] = held[3].astype(jnp.float32)


def attend_out(units, order):
    rows, width = units[0].shape
    vmem = pl.BlockSpec(memory_space=pltpu.VMEM)
    return pl.pallas_call(
        attend_out_kernel,
        in_specs=[pl.BlockSpec(memory_space=pltpu.SMEM)] + [vmem] * 4,
        out_specs=[vmem] * 2,
        out_shape=[
            jax.ShapeDtypeStruct((rows, 3 * width), jnp.float32),
            jax.ShapeDtypeStruct((rows, width), jnp.float32),
        ],
        scratch_shapes=[pltpu.VMEM((4, rows, width), units[0].dtype)],
        compiler_params=pltpu.CompilerParams(vmem_limit_bytes=32 << 20),
    )(jnp.stack(order).astype(jnp.int32), *units)


def shrink_out_kernel(order_ref, *refs):
    for index in range(4):
        refs[4][order_ref[index]] = refs[index][...].astype(jnp.float32)


def shrink_out(units, order):
    rows, width = units[0].shape
    vmem = pl.BlockSpec(memory_space=pltpu.VMEM)
    return pl.pallas_call(
        shrink_out_kernel,
        in_specs=[pl.BlockSpec(memory_space=pltpu.SMEM)] + [vmem] * 4,
        out_specs=vmem,
        out_shape=jax.ShapeDtypeStruct((4, rows, width), jnp.float32),
    )(jnp.stack(order).astype(jnp.int32), *units).reshape(4 * rows, width)


def spread_kernel(parts, order_ref, *refs):
    units, out_ref, held = refs[:4], refs[4], refs[5]
    for index in range(4):
        held[order_ref[index]] = units[index][...]
    width = units[0].shape[1] // parts
    out_ref[...] = jnp.concatenate(
        [
            held[unit, :, part * width : (part + 1) * width].astype(jnp.float32)
            for part in range(parts)
            for unit in range(4)
        ],
        axis=1,
    )


def spread(units, order, parts):
    rows, width = units[0].shape
    vmem = pl.BlockSpec(memory_space=pltpu.VMEM)
    return pl.pallas_call(
        partial(spread_kernel, parts),
        in_specs=[pl.BlockSpec(memory_space=pltpu.SMEM)] + [vmem] * 4,
        out_specs=vmem,
        out_shape=jax.ShapeDtypeStruct((rows, 4 * width), jnp.float32),
        scratch_shapes=[pltpu.VMEM((4, rows, width), units[0].dtype)],
        compiler_params=pltpu.CompilerParams(vmem_limit_bytes=32 << 20),
    )(jnp.stack(order).astype(jnp.int32), *units)


class Layer:
    def __init__(self, hidden_in, condition, patch_mask, image_counts, cotangent):
        self.slots, self.patches, self.width = hidden_in.shape
        self.rows = self.slots * self.patches
        self.patch_mask = patch_mask
        self.condition = condition
        self.live = (jnp.arange(self.slots) < image_counts[0]).astype(jnp.float32)
        self.hidden_in = hidden_in
        self.hidden = hidden_in.reshape(self.rows, self.width)
        self.cotangent = cotangent
        self.whole = (self.rows, self.width)

    def flat(self, values):
        return values.reshape(self.rows, self.width)

    def begin(self, order, terms, bias, attend_bias, *units):
        cotangent = self.flat(self.cotangent)
        return begin(order, self.live, terms, bias, self.hidden, cotangent, attend_bias, units)

    def attention(self, queries, keys_all, values_all):
        return attend(queries, keys_all, values_all, self.patch_mask)

    def per_image(self, kernel, outs, ins, scratch=()):
        rows = pl.BlockSpec((self.patches, self.width), lambda slot: (slot, 0))

        def spec(kind, shape):
            if kind == "rows":
                return rows
            if kind == "scalar":
                return pl.BlockSpec(memory_space=pltpu.SMEM)
            if kind == "any":
                return pl.BlockSpec(memory_space=pl.ANY)
            if kind == "all":
                return pl.BlockSpec(shape, lambda slot: (0,) * len(shape))
            return pl.BlockSpec((1,) + shape[1:], lambda slot: (slot, 0, 0))

        shapes = [
            self.whole if kind == "rows" else (self.slots, kind, self.width) for kind, _ in outs
        ]
        return pl.pallas_call(
            kernel,
            grid=(self.slots,),
            in_specs=[spec(kind, array.shape) for kind, array in ins],
            out_specs=[spec(kind, shape) for (kind, _), shape in zip(outs, shapes)],
            out_shape=[jax.ShapeDtypeStruct(shape, kind[1]) for kind, shape in zip(outs, shapes)],
            scratch_shapes=list(scratch),
            compiler_params=pltpu.CompilerParams(vmem_limit_bytes=56 << 20),
        )(*[array for _, array in ins])

    def middle(self, attended, output_full, output_bias, modulation):
        return self.per_image(
            middle_kernel,
            [("rows", jnp.float32), ("rows", jnp.bfloat16)],
            [
                ("rows", attended),
                ("all", output_full),
                ("all", output_bias),
                ("rows", self.hidden),
                ("mod", modulation),
            ],
        )

    def expand(self, normed_two, unit, biases, index):
        bias = lax.dynamic_index_in_dim(biases, index, 0, keepdims=False)
        inner = times(normed_two, unit) + bias
        return inner, low(gelu(inner))

    def shrink(self, inner, active, shrink_slope, expand_unit, unit, *totals):
        active_slope = times_transposed(shrink_slope, unit)
        inner_slope = low(jax.vjp(gelu, inner)[1](active_slope)[0])
        out = times(active, unit)
        back = times_transposed(inner_slope, expand_unit)
        if totals:
            out, back = out + totals[0], back + totals[1]
        ones = jnp.ones((8, self.rows), jnp.bfloat16)
        return inner_slope, times(ones, inner_slope), out, back

    def finish(self, branch, out, back, shrink_bias, modulation):
        layer_out, *others = self.per_image(
            finish_kernel,
            [
                ("rows", jnp.bfloat16),
                ("rows", jnp.float32),
                ("rows", jnp.bfloat16),
                (6, jnp.float32),
            ],
            [
                ("scalar", self.live),
                ("rows", self.hidden),
                ("rows", branch),
                ("rows", out),
                ("rows", back),
                ("rows", self.flat(self.cotangent)),
                ("all", shrink_bias),
                ("mod", modulation),
            ],
        )
        return layer_out.reshape(self.hidden_in.shape), *others

    def attention_back(self, slopes, queries, keys_all, values_all, logs):
        return attend_back(queries, keys_all, values_all, slopes, self.patch_mask, logs)

    def start_back(self, slopes, units, order, middle_slope, modulation):
        vmem = pl.BlockSpec(memory_space=pltpu.VMEM)
        gradient, first_slopes = pl.pallas_call(
            start_back_kernel,
            in_specs=[pl.BlockSpec(memory_space=pltpu.SMEM)]
            + [vmem] * 6
            + [pl.BlockSpec(memory_space=pl.ANY)] * 4,
            out_specs=[vmem] * 2,
            out_shape=[
                jax.ShapeDtypeStruct(self.whole, jnp.float32),
                jax.ShapeDtypeStruct((self.slots, 2, self.width), jnp.float32),
            ],
            scratch_shapes=[
                pltpu.VMEM((4, self.width, self.width), jnp.bfloat16),
                pltpu.SemaphoreType.DMA((4,)),
            ],
            compiler_params=pltpu.CompilerParams(vmem_limit_bytes=48 << 20),
        )(jnp.stack(order).astype(jnp.int32), *slopes, middle_slope, self.hidden, modulation, *units)
        return gradient.reshape(self.hidden_in.shape), first_slopes

    def condition_back(self, slope):
        return jax.vjp(jax.nn.silu, self.condition.astype(jnp.float32))[1](slope)[0]


def act_rows(conditions, here, shard):
    rows = lax.dynamic_slice_in_dim(conditions, here * shard, shard, 1)
    return low(jax.nn.silu(rows.astype(jnp.float32)))


def unpack_kernel(parts, packed_ref, mod_ref, attend_ref, output_ref, expand_ref, shrink_ref):
    shard = output_ref.shape[1] // parts
    start = packed_ref.shape[1] - 14 * shard

    def joined(first, size):
        cut = [
            packed_ref[part : part + 1, start + first : start + first + size].astype(jnp.float32)
            for part in range(parts)
        ]
        return jnp.concatenate(cut, axis=1)

    mod_ref[...] = joined(0, 6 * shard)
    for row in range(2):
        attend_ref[row : row + 1] = joined((6 + row) * shard, shard)
    output_ref[...] = joined(8 * shard, shard)
    for unit in range(4):
        expand_ref[unit : unit + 1] = joined((9 + unit) * shard, shard)
    shrink_ref[...] = joined(13 * shard, shard)


def unpack(packed, shard):
    parts = packed.shape[0]
    width = parts * shard
    return pl.pallas_call(
        partial(unpack_kernel, parts),
        out_shape=[
            jax.ShapeDtypeStruct((rows, columns), jnp.float32)
            for rows, columns in ((1, 6 * width), (2, width), (1, width), (4, width), (1, width))
        ],
    )(packed)


def pack_slopes_kernel(order_ref, first_ref, later_ref, head_ref, condition_ref, *refs):
    units, out_ref, held_ref = refs[:4], refs[4], refs[5]
    for index, unit in enumerate(units):
        held_ref[pl.ds(order_ref[index], 1), :] = unit[0:1, :]
    slots, width = condition_ref.shape
    sums = [head_ref[0, i : i + 1] + head_ref[1, i : i + 1] for i in range(2)]
    sums += [later_ref[0, i : i + 1] + later_ref[1, i : i + 1] for i in (4, 5)]
    for slot in range(slots):
        parts = [first_ref[slot, i : i + 1] for i in range(2)]
        parts += [later_ref[slot, i : i + 1] for i in range(4)]
        parts += [condition_ref[slot : slot + 1, :].astype(jnp.float32)]
        parts += sums if slot == 0 else [held_ref[i : i + 1, :] for i in range(4)]
        out_ref[slot : slot + 1, :] = low(jnp.concatenate(parts, axis=1))


def pack_slopes(order, first, later, heads, condition, units):
    slots, width = condition.shape
    vmem = pl.BlockSpec(memory_space=pltpu.VMEM)
    return pl.pallas_call(
        pack_slopes_kernel,
        in_specs=[pl.BlockSpec(memory_space=pltpu.SMEM)] + [vmem] * 8,
        out_specs=vmem,
        out_shape=jax.ShapeDtypeStruct((slots, 11 * width), jnp.bfloat16),
        scratch_shapes=[pltpu.VMEM((4, width), jnp.float32)],
    )(jnp.stack(order).astype(jnp.int32), first, later, heads, condition, *units)


def pack(condition, *biases):
    row = jnp.concatenate([condition.reshape(-1)] + [bias.reshape(-1) for bias in biases])
    return row[None]


def modulation_tail(modulation_slopes, conditions, here, shard, bias_size):
    weight = inner_rows(act_rows(conditions, here, shard), modulation_slopes)
    bias = lax.dynamic_slice_in_dim(modulation_slopes, here * bias_size, bias_size, 1)
    return weight, column_sums(bias)


def bias_tail(sums, here, shard):
    mine = lax.dynamic_slice_in_dim(sums, here * shard, shard, 1)
    return mine[0:2], mine[2], mine[4:8].reshape(-1), mine[3]


def condition_columns(gathered, image, slots):
    mine = lax.dynamic_slice_in_dim(gathered, image, slots, 1)
    return mine.transpose(1, 0, 2).reshape(slots, -1)


def plain_device(
    dp,
    rep,
    hidden_in,
    condition,
    patch_mask,
    image_counts,
    modulation_weight,
    modulation_bias,
    attend_weight,
    attend_bias,
    output_weight,
    output_bias,
    expand_weight,
    expand_bias,
    shrink_weight,
    shrink_bias,
    cotangent,
):
    here = lax.axis_index("dp")
    layer = Layer(hidden_in, condition, patch_mask, image_counts, cotangent)
    shard, width, slots = modulation_weight.shape[0], layer.width, layer.slots

    def whole(block):
        return lax.all_gather(block, "dp", axis=0, tiled=True)

    def summed(term):
        return lax.psum(
            lax.psum_scatter(term, "dp", scatter_dimension=0, tiled=True), "rep"
        ).astype(jnp.float32)

    packed = pack(
        condition, modulation_bias, attend_bias, output_bias, expand_bias, shrink_bias
    )
    packed = lax.all_gather(packed, "dp", axis=0, tiled=True)
    conditions = packed[:, : condition.size].reshape(-1, width)
    biases = unpack(packed, shard)
    expand_biases = biases[3].reshape(4, dp, shard).transpose(1, 0, 2).reshape(4, width)
    terms = times(act_rows(conditions, here, shard), modulation_weight)
    terms = lax.psum_scatter(terms, "dp", scatter_dimension=0, tiled=True)
    weights = whole(jnp.concatenate([attend_weight, output_weight], 1))
    weights = [weights[:, unit * width : (unit + 1) * width] for unit in range(4)]
    natural = [jnp.int32(unit) for unit in range(4)]
    expand_full, shrink_full = whole(expand_weight), whole(shrink_weight)
    begun = layer.begin(natural, terms, biases[0], biases[1], *weights)
    normed_one, shrink_slope, modulation, queries, keys_all, values_all, output_full = begun
    attended, logs = layer.attention(queries, keys_all, values_all)
    branch, normed_two = layer.middle(attended, output_full, biases[2], modulation)
    totals = ()
    expand_terms, shrink_terms, inner_sums = [], [], []
    for unit in range(4):
        cut = slice(unit * width, (unit + 1) * width)
        inner, active = layer.expand(normed_two, expand_full[:, cut], expand_biases, unit)
        inner_slope, inner_sum, *totals = layer.shrink(
            inner, active, shrink_slope, expand_full[:, cut], shrink_full[cut], *totals
        )
        expand_terms.append(low(inner_rows(normed_two, inner_slope)))
        shrink_terms.append(low(inner_rows(active, shrink_slope)))
        inner_sums.append(inner_sum[:1])
    layer_out, middle_slope, branch_low, later = layer.finish(
        branch, *totals, biases[4], modulation
    )
    attended_slope = low(times_transposed(branch_low, output_full))
    *slopes, head_sums = layer.attention_back(
        attended_slope, queries, keys_all, values_all, logs
    )
    gradient_hidden, first = layer.start_back(
        slopes, weights, natural, middle_slope, modulation
    )
    mod_slope = low(jnp.concatenate([first, later[:, :4]], 1)).reshape(slots, -1)
    all_slopes = lax.all_gather(mod_slope, ("dp", "rep"), axis=0, tiled=True)
    all_conditions = lax.all_gather(condition, ("dp", "rep"), axis=0, tiled=True)
    mod_weight, mod_bias = modulation_tail(
        all_slopes, all_conditions, here, shard, modulation_bias.shape[0]
    )
    columns = lax.all_gather(times_transposed(all_slopes, modulation_weight), "dp")
    inner_sums = jnp.concatenate(inner_sums, 1).reshape(dp, 4, shard)
    inner_sums = inner_sums.transpose(1, 0, 2).reshape(4, width)
    sums = jnp.concatenate([jnp.sum(head_sums, 0), jnp.sum(later[:, 4:], 0), inner_sums])
    sums = lax.psum(sums, ("dp", "rep"))
    att_bias, out_bias, exp_bias, shr_bias = bias_tail(sums, here, shard)
    return (
        layer_out,
        gradient_hidden,
        layer.condition_back(condition_columns(columns, (here * rep + lax.axis_index("rep")) * slots, slots)),
        mod_weight,
        mod_bias,
        summed(low(inner_rows(normed_one, jnp.concatenate(slopes, 1)))),
        att_bias,
        summed(low(inner_rows(attended, branch_low))),
        out_bias,
        summed(jnp.concatenate(expand_terms, 1)),
        exp_bias,
        summed(jnp.concatenate(shrink_terms)),
        shr_bias,
    )


class Ticks:
    def __init__(self):
        self.ops = []

    def at(self, tick, outs, ins, call):
        outs, ins = [(names,) if isinstance(names, str) else names for names in (outs, ins)]
        self.ops.append((tick, len(self.ops), outs, ins, call))

    def run(self, results):
        ops = sorted(self.ops, key=lambda op: op[:2])
        last = {}
        for tick, _, _, ins, _ in ops:
            for name in ins:
                last[name] = tick
        state = {}
        for position, (tick, _, outs, ins, call) in enumerate(ops):
            values = call(*[state[name] for name in ins])
            if len(outs) == 1:
                values = (values,)
            state.update(zip(outs, values))
            ends = position + 1 == len(ops) or ops[position + 1][0] > tick
            if ends:
                names = sorted(
                    name for name in state if last.get(name, -1) > tick or name in results
                )
                state = dict(zip(names, lax.optimization_barrier(tuple(state[n] for n in names))))
        return [state[name] for name in results]


class Names:
    def __getattr__(self, name):
        return name


def ticked_device(
    dp,
    rep,
    hidden_in,
    condition,
    patch_mask,
    image_counts,
    modulation_weight,
    modulation_bias,
    attend_weight,
    attend_bias,
    output_weight,
    output_bias,
    expand_weight,
    expand_bias,
    shrink_weight,
    shrink_bias,
    cotangent,
):
    n = Names()
    here = lax.axis_index(n.dp)
    copy = lax.axis_index(n.rep)
    depth = dp // 2
    z, x, y, core = here // 2, here % 2, copy // 2, copy % 2
    order = [(2 * core + y) ^ step for step in range(4)]
    layer = Layer(hidden_in, condition, patch_mask, image_counts, cotangent)
    shard, width, slots = modulation_weight.shape[0], layer.width, layer.slots
    ticks = Ticks()
    at = ticks.at

    def up(value):
        return lax.ppermute(value, n.dp, [(i, (i + 2) % dp) for i in range(dp)])

    def jump(step, value):
        return lax.ppermute(value, n.dp, [(i, (i + 2 * step) % dp) for i in range(dp)])

    def swap_x(value):
        return lax.ppermute(value, n.dp, [(i, i ^ 1) for i in range(dp)])

    def swap_y(value):
        return lax.ppermute(value, n.rep, [(i, i ^ 2) for i in range(4)])

    def swap_core(value):
        return lax.ppermute(value, n.rep, [(i, i ^ 1) for i in range(4)])

    def pair(one, two):
        return jnp.concatenate([one, two])

    def below(step):
        return (z - step) % depth

    def add(one, two):
        return low(one.astype(jnp.float32) + two.astype(jnp.float32))

    def attend_block(index):
        column = jnp.minimum(index, 2) * width
        block = lax.dynamic_slice_in_dim(attend_weight, column, width, 1)
        return jnp.where(index == 3, output_weight, block)[None]

    def shrink_block(index):
        return lax.dynamic_slice_in_dim(shrink_weight, index * shard, shard, 0)[None]

    def pick(stacked, index):
        return lax.dynamic_slice_in_dim(stacked, index, 1, 0)

    at(0, n.A0, (), lambda: attend_block(order[0]))
    at(0, n.a0, (), lambda: attend_block(order[1]))
    at(0, n.Bs, (), lambda: regroup(expand_weight, dp))
    at(0, n.P0, n.Bs, lambda s: pick(s, order[1]))
    at(0, n.C0, (), lambda: shrink_block(order[0]))
    at(0, n.c0, (), lambda: shrink_block(order[1]))

    at(0, n.AB0, (n.A0, n.Bs), lambda p, q: pair(p, pick(q, order[0])))
    for name, ring_ticks, x_ticks in (
        (n.AB, (0, 1, 2), (0, 1, 2, 3)),
        (n.P, (3, 4, 5), (4, 5)),
        (n.C, (3, 6, 7), (6, 7, 7, 8)),
    ):
        for step, tick in enumerate(ring_ticks):
            at(tick, (str(name) + str(step + 1)), (str(name) + str(step)), up)
        for step, tick in enumerate(x_ticks):
            at(tick, (str(name) + n.x + str(step)), (str(name) + str(step)), swap_x)
    for step in range(3):
        at(step + 1, (n.ABy + str(step)), ((n.ABx + str(step)), (n.AB + str(step + 1))),
           lambda p, q: swap_y(pair_rows(p, 0, q, 0)))
    at(4, n.ABy3, n.ABx3, lambda p: swap_y(p[:1]))
    at(6, n.Px23, (n.P2, n.P3), lambda p, q: swap_x(pair(p, q)))
    at(6, n.C1y, n.C1, swap_y)
    for tick, one, two in ((7, n.Cx0, n.C2), (8, n.Cx1, n.C3), (9, n.Cx2, n.Cx3)):
        at(tick, one + two, (one, two), lambda p, q: swap_y(pair(p, q)))

    def spot(step, cross):
        return 2 * below(step) + (1 - x if cross else x)

    def unit(blocks):
        parts = [(array, row) for array, row, _, _ in blocks]
        places = [spot(step, cross) for _, _, step, cross in blocks]
        return assemble(parts, places, dp).reshape(dp * shard, width)

    def streamed(zs, xs):
        return unit(
            [(array, row, step, False) for step, (array, row) in enumerate(zs)]
            + [(array, row, step, True) for step, (array, row) in enumerate(xs)]
        )

    def own_unit(row, *parts):
        return streamed([(part, row) for part in parts[:4]], [(part, row) for part in parts[4:]])

    def other_unit(local, *parts):
        return streamed(
            [(local, 0)] + [(part, 1) for part in parts[:3]], [(part, 0) for part in parts]
        )

    def other_late(local, one, two, three, four):
        return streamed(
            [(local, 0), (one, 0), (two, 1), (three, 1)], [(two, 0), (three, 0), (four, 0), (four, 1)]
        )

    def pair_unit(*parts):
        return streamed(
            [(part, 0) for part in parts[:4]], [(parts[4], 0), (parts[5], 0), (parts[6], 0), (parts[6], 1)]
        )

    for name, stream, row, tick in (
        (n.Aown, n.AB, 0, 4), (n.Bown, n.AB, 1, 5)
    ):
        parts = tuple((str(stream) + str(step)) for step in range(4))
        parts += tuple((str(stream) + n.x + str(step)) for step in range(4))
        at(tick, name, parts, partial(own_unit, row))
    at(5, n.Ay, (n.a0,) + tuple((n.ABy + str(step)) for step in range(4)), other_unit)
    at(7, n.By, (n.P0, n.P1, n.P2, n.P3, n.Px0, n.Px1, n.Px23), pair_unit)
    at(10, n.Cy, (n.c0, n.C1y, n.Cx0C2, n.Cx1C3, n.Cx2Cx3), other_late)
    at(5, n.Ac, n.Aown, swap_core)
    at(5, n.Acy, n.Ay, swap_core)
    at(6, n.Bc, n.Bown, swap_core)
    at(7, n.Bcy, n.By, swap_core)
    at(10, n.Ccy, n.Cy, swap_core)

    def swap_z(distance, value):
        return lax.ppermute(value, n.dp, [(i, i ^ (2 * distance)) for i in range(dp)])

    bits = {
        n.core: (core, swap_core),
        n.y: (y, swap_y),
        n.x: (x, swap_x),
        n.near: (z % 2, partial(swap_z, 1)),
        n.far: (z // 2, partial(swap_z, 2)),
    }

    def grow(tick, name, axes):
        for axis in axes:
            bit, swap = bits[axis]

            def join(mine, other, bit=bit):
                return jnp.where(bit == 0, pair(mine, other), pair(other, mine))

            at(tick, name + n._in, name, swap)
            at(tick, name + "+", (name, name + n._in), join)
            name += "+"
        return name

    def shrink_terms(tick, name, axes):
        for axis in axes:
            bit, swap = bits[axis]

            def send(terms, bit=bit, swap=swap):
                half = terms.shape[0] // 2
                return swap(lax.dynamic_slice_in_dim(terms, (1 - bit) * half, half, 0))

            def keep(terms, other, bit=bit):
                half = terms.shape[0] // 2
                return lax.dynamic_slice_in_dim(terms, bit * half, half, 0) + other

            at(tick, name + n._in, name, send)
            at(tick, name + "-", (name, name + n._in), keep)
            name += "-"
        return name

    at(0, n.small, (), lambda: pack(
        condition, modulation_bias, attend_bias, output_bias, expand_bias, shrink_bias))
    small = grow(0, n.small, (n.x,))
    small = grow(1, small, (n.near,))
    small = grow(2, small, (n.far,))
    at(3, (n.mod_bias, n.att_bias, n.out_bias, n.exp_bias, n.shr_bias), small,
       lambda packed: unpack(packed, shard))

    def first_terms(packed):
        conditions = packed[:, : condition.size].reshape(2, 2, 2, slots, width)
        conditions = conditions.transpose(2, 1, 0, 3, 4).reshape(-1, width)
        return times(act_rows(conditions, here, shard), modulation_weight)

    at(2, n.terms, small, first_terms)
    terms = shrink_terms(3, n.terms, (n.x,))
    terms = shrink_terms(4, terms, (n.near,))
    terms = shrink_terms(5, terms, (n.far,))

    units_a = (n.Aown, n.Ay, n.Ac, n.Acy)
    at(6, (n.n1, n.gm, n.mod, n.q, n.k, n.v, n.O), (terms, n.mod_bias, n.att_bias) + units_a,
       partial(layer.begin, order))
    at(6, (n.att, n.logs), (n.q, n.k, n.v), layer.attention)
    at(7, (n.branch, n.n2), (n.att, n.O, n.out_bias, n.mod), layer.middle)

    def expand(index, n2, weight, biases):
        return layer.expand(n2, weight, biases, order[index])

    def term(left, right, *received):
        total = inner_rows(left, right)
        for value in received:
            total = total + value.astype(jnp.float32)
        return low(total)

    for index, (name, tick) in enumerate(((n.own, 8), (n.y, 8), (n.c, 7), (n.cy, 8))):
        at(tick, ((n.in_ + str(name)), (n.act_ + str(name))), (n.n2, (n.B + str(name)), n.exp_bias), partial(expand, index))
    at(7, n.dC_c, (n.act_c, n.gm), term)
    at(9, n.dC_cy, (n.act_cy, n.gm), term)
    at(9, n.dC_own, (n.act_own, n.gm, n.dC_rc), term)
    at(11, n.dC_y, (n.act_y, n.gm, n.dC_rcy), term)

    at(9, n.Cown, (n.C0, n.C1, n.C2, n.C3, n.Cx0, n.Cx1, n.Cx2, n.Cx3, n.dC_own),
       lambda *parts: own_unit(0, *lax.optimization_barrier(parts)[:8]))
    at(9, n.Cc, n.Cown, swap_core)
    total = ()
    for index, (name, tick) in enumerate(((n.own, 9), (n.c, 10), (n.cy, 11), (n.y, 12))):
        ins = ((n.in_ + str(name)), (n.act_ + str(name)), n.gm, (n.B + str(name)), (n.C + str(name))) + total
        total = ((n.out + str(index)), (n.back + str(index)))
        at(tick, ((n.gi_ + str(name)), (n.sum_ + str(name))) + total, ins, layer.shrink)
    at(10, n.dB_c, (n.n2, n.gi_c), term)
    at(11, n.dB_cy, (n.n2, n.gi_cy), term)
    at(12, n.dB_own, (n.n2, n.gi_own, n.dB_rc), term)
    at(13, n.dB_y, (n.n2, n.gi_y, n.dB_rcy), term)

    at(13, (n.layer_out, n.middle_slope, n.branch_low, n.later),
       (n.branch, n.out3, n.back3, n.shr_bias, n.mod), layer.finish)
    at(13, n.g_att, (n.branch_low, n.O), lambda b, w: low(times_transposed(b, w)))
    at(14, (n.gq, n.gk, n.gv, n.head_sums), (n.g_att, n.q, n.k, n.v, n.logs), layer.attention_back)
    def attend_term(index, n1, att, gq, gk, gv, branch_low, *received):
        which = order[index]
        right = lax.select_n(which, gq, gk, gv, branch_low)
        return term(jnp.where(which == 3, att, n1), right, *received)

    for index, (name, tick, received) in enumerate(
        ((n.own, 15, ()), (n.y, 15, ()), (n.c, 14, ()), (n.cy, 14, ()))
    ):
        ins = (n.n1, n.att, n.gq, n.gk, n.gv, n.branch_low) + received
        at(tick, (n.dA_ + str(name)), ins, partial(attend_term, index))

    at(16, (n.gradient_hidden, n.first), (n.gq, n.gk, n.gv, n.middle_slope, n.mod) + units_a,
       lambda a, b, c, ms, mod, *units: layer.start_back((a, b, c), units, order, ms, mod))


    def slab(step, moved, count, *values):
        first = below(step) * (2 * shard)
        cuts = [lax.dynamic_slice_in_dim(value, first, 2 * shard, 0) for value in values[:count]]
        cuts += values[count:]
        if len(cuts) == 1:
            return moved(cuts[0])
        return moved(low(sum(value.astype(jnp.float32) for value in cuts)))

    def stay(value):
        return value

    def along_ring(name, start, source, added, rest=0):
        for step in range(1, 5):
            ins = source + tuple((str(part) + str(step)) for part in added)
            if step > 1:
                ins += ((str(name) + str(step - 1)),)
            at(start + step - 1, (str(name) + str(step)), ins, partial(slab, step, up if step < 4 else stay, len(source)))
        at(start + 3 + rest, (str(name) + n._in), (str(name) + str(4)), lambda total: swap_x(
            lax.dynamic_slice_in_dim(total, (1 - x) * shard, shard, 0)))
        at(start + 4 + rest, (str(name) + n._sum), ((str(name) + str(4)), (str(name) + n._in)), lambda total, other: low(
            lax.dynamic_slice_in_dim(total, x * shard, shard, 0).astype(jnp.float32)
            + other.astype(jnp.float32)))
        return (str(name) + n._sum)

    def wide(name, start_own, start_other, late):
        one = along_ring((str(name) + n._o), start_own, ((str(name) + n._own),), ())
        two = along_ring((str(name) + n._p), start_other, ((str(name) + n._y),), ())
        at(late, (str(name) + n._yo), two, swap_y)
        at(late, (str(name) + n._yp), one, swap_y)
        at(late + 1, (str(name) + n._0), (one, (str(name) + n._yo)), add)
        at(late + 1, (str(name) + n._1), (two, (str(name) + n._yp)), add)
        at(late + 1, (str(name) + n._2), (str(name) + n._0), swap_core)
        at(late + 1, (str(name) + n._3), (str(name) + n._1), swap_core)
        return late + 2

    def halved(name, cut_ticks, y_ticks, start_ring, late, received=(), rest=0):
        for step, tick in enumerate(y_ticks, 1):
            ins = ((str(name) + n._y),) + tuple((str(name) + n._ + str(part) + n.y) for part in received)
            at(cut_ticks[step - 1], (str(name) + n._t + str(step)), ins, partial(slab, step, stay, len(ins)))
            at(tick, (str(name) + n._s + str(step)), (str(name) + n._t + str(step)), swap_y)
        own = ((str(name) + n._own),) + tuple((str(name) + n._ + str(part)) for part in received)
        one = along_ring((str(name) + n._o), start_ring, own, ((str(name) + n._s),), rest)
        at(late, (str(name) + n._0), one, stay)
        at(late, (str(name) + n._1), one, swap_y)
        at(late + 1, (str(name) + n._2), one, swap_core)
        at(late + 1, (str(name) + n._3), (str(name) + n._1), swap_core)
        return late + 2

    for name, tick_one, tick_two in ((n.dC, 8, 10), (n.dB, 11, 12), (n.dA, 15, 15)):
        at(tick_one, (str(name) + n._rc), (str(name) + n._c), swap_core)
        at(tick_two, (str(name) + n._rcy), (str(name) + n._cy), swap_core)
    end_c = wide(n.dC, 9, 12, 20)
    end_b = halved(n.dB, (13, 14, 14, 15), (13, 14, 14, 15), 14, 19, rest=1)
    end_a = halved(n.dA, (16, 17, 18, 19), (16, 17, 18, 19), 17, 21, (n.rc,))

    def four(name):
        return tuple((str(name) + n._ + str(i)) for i in range(4))

    at(end_c, n.shr_weight, four(n.dC), lambda *units: shrink_out(units, order))
    at(end_b, n.exp_weight, four(n.dB), lambda *units: spread(units, order, dp))
    at(end_a, (n.att_weight, n.out_weight), four(n.dA), lambda *units: attend_out(units, order))

    def join(tick, name, axis):
        at(tick, name + n._in, name, bits[axis][1])
        at(tick, name + "+", (name, name + n._in), pair)
        return name + "+"

    mod_size = 6 * width
    at(16, n.sent, (n.first, n.later, n.head_sums, n.sum_own, n.sum_y, n.sum_c, n.sum_cy),
       lambda first, later, heads, *units: pack_slopes(
           order, first, later, heads, condition, units))
    sent = n.sent
    both_ways = [(4 * i + j, 4 * (i ^ 4) + (j ^ 2)) for i in range(dp) for j in range(4)]
    at(17, n.sent_far, sent, partial(swap_z, 2))
    at(17, n.sent_y, sent, swap_y)
    at(17, n.sent_both, sent, lambda rows: lax.ppermute(rows, (n.dp, n.rep), both_ways))
    at(17, n.rows, (sent, n.sent_far, n.sent_y, n.sent_both), lambda *rows: jnp.concatenate(rows))
    sent = n.rows
    for tick, axis in ((18, n.near), (19, n.x), (20, n.core)):
        sent = join(tick, sent, axis)

    def modulation_terms(sent):
        slopes = sent[:, :mod_size]
        weight, bias = modulation_tail(
            slopes, sent[:, mod_size : mod_size + width], here, shard, modulation_bias.shape[0]
        )
        row = lax.broadcasted_iota(jnp.int32, (slots, sent.shape[0]), 1)
        picked = low(row % slots == lax.broadcasted_iota(jnp.int32, row.shape, 0))
        sums = times(picked, sent[:, mod_size + width :]).reshape(-1, width)
        return (weight, bias) + bias_tail(sums, here, shard)

    at(20, n.columns, sent, lambda sent: times_transposed(sent[:, :mod_size], modulation_weight))
    at(20, (n.mod_weight, n.mod_bias_out, n.att_bias_out, n.out_bias_out, n.exp_bias_out, n.shr_bias_out),
       sent, modulation_terms)

    at(20, n.traded, n.columns, lambda columns: columns.reshape(
        2, 2, 2, 2, 2, slots, shard)[0, :, :, 0])
    at(20, n.traded_x, n.traded, lambda held: swap_x(held[1]))
    at(21, n.held, (n.traded, n.traded_x), lambda held, got: jnp.stack([held[0], got]))
    for step in (1, 2, 3):
        at(21, (n.held + str(step)), n.held, lambda held, step=step: swap_z(step, held[:, step % 2, step // 2]))

    def condition_slope(held, near, far, both):
        held = jnp.stack([held[:, 0, 0], far, near, both]).reshape(2, 2, 2, slots, shard)
        for axis, bit in enumerate((z % 2, z // 2, x)):
            held = jnp.where(bit == 1, jnp.flip(held, axis), held)
        held = held.transpose(3, 1, 0, 2, 4)
        return layer.condition_back(held.reshape(slots, width))

    at(22, n.gradient_condition, (n.held, n.held1, n.held2, n.held3), condition_slope)
    return tuple(
        ticks.run(
            [
                n.layer_out,
                n.gradient_hidden,
                n.gradient_condition,
                n.mod_weight,
                n.mod_bias_out,
                n.att_weight,
                n.att_bias_out,
                n.out_weight,
                n.out_bias_out,
                n.exp_weight,
                n.exp_bias_out,
                n.shr_weight,
                n.shr_bias_out,
            ]
        )
    )


def solution(mesh):
    dp, rep = mesh.shape["dp"], mesh.shape["rep"]
    device = ticked_device if (dp, rep) == (8, 4) else plain_device
    return jax.shard_map(
        partial(device, dp, rep),
        mesh=mesh,
        in_specs=(
            P(("dp", "rep"), None, None),
            P(("dp", "rep"), None),
            P(("dp", "rep"), None),
            P(("dp", "rep")),
            P("dp", None),
            P("dp"),
            P("dp", None),
            P(None, "dp"),
            P("dp", None),
            P("dp"),
            P("dp", None),
            P("dp"),
            P("dp", None),
            P("dp"),
            P(("dp", "rep"), None, None),
        ),
        out_specs=(
            P(("dp", "rep"), None, None),
            P(("dp", "rep"), None, None),
            P(("dp", "rep"), None),
            P("dp", None),
            P("dp"),
            P("dp", None),
            P(None, "dp"),
            P("dp", None),
            P("dp"),
            P("dp", None),
            P("dp"),
            P("dp", None),
            P("dp"),
        ),
        check_vma=False,
    )
```
